32 devices in a mesh: dp: 8 (over z, y), section: 4 (over x, core).
Axes of the slice: x: 2, y: 2, z: 4, core: 2. Of those that a mesh axis runs over, the one named last changes fastest.
Arguments:
- tokens: bfloat16 [24, 512, 768], P('dp'), may hold values from -6 to 6
- lengths: int32 [24], P('dp'), may hold values from 64 to 512, as said below
- w_main: bfloat16 [4, 768, 3072], P('section'), may hold values from -2 to 2
- w_down_half: bfloat16 [4, 1536, 768], P('section'), may hold values from -0.21875 to 0.21875
- out_bias: float32 [4, 768], P('section'), may hold values from -3 to 3
- ln_gain: float32 [4, 768], P('section'), may hold values from 0.25 to 1.75
- ln_bias: float32 [4, 768], P('section'), may hold values from -3 to 3
- cotangent: bfloat16 [24, 512, 768], P('dp'), may hold values from -6 to 6
Outputs:
- section_out: bfloat16 [4, 24, 512, 768], P('section', 'dp')
- section_in_grad: bfloat16 [4, 24, 512, 768], P('section', 'dp')
- grad_w_main: float32 [4, 768, 3072], P('section')
- grad_w_down: float32 [4, 1536, 768], P('section')
- grad_out_bias: float32 [4, 768], P('section')
- grad_ln_gain: float32 [4, 768], P('section')
- grad_ln_bias: float32 [4, 768], P('section')
The draws below stay inside these ranges and needn't reach their ends.
Inputs may be any that keep to these rules, and one draw needn't show every extreme that they name: `lengths`: one sequence has exactly 512 valid tokens and one exactly 64.
All inputs are finite; a program needn't handle non-finite values.
Results may differ from the reference program's by a relative error of at most 0.015.
Values may be sent and summed in bfloat16 or wider, within the bound.
A program may use at most 192 MiB of HBM per device.

```python
import jax
import jax.numpy as jnp
from jax import lax

D = 768
HEADS = 12
HEAD = 64
FF = 3072
LEN = 512
SEQS = 24
N_SECTION = 4


def draw_lengths(key, part):
    drawn_lengths = jax.random.randint(jax.random.fold_in(key, 1), (SEQS,), LEN // 8, LEN + 1)
    long_place = jax.random.randint(jax.random.fold_in(key, 2), (), 0, SEQS)
    offset = jax.random.randint(jax.random.fold_in(key, 3), (), 1, SEQS)
    short_place = (long_place + offset) % SEQS
    positions = jnp.arange(SEQS)
    drawn_lengths = jnp.where(positions == long_place, LEN, drawn_lengths)
    return jnp.where(positions == short_place, LEN // 8, drawn_lengths).astype(jnp.int32)


def draw_w_main(key, part):
    values = jax.random.normal(jax.random.fold_in(key, 7), (N_SECTION, D, 4 * D), jnp.float32)
    values = jnp.clip(values, -6.0, 6.0) * D ** (-0.5)
    section_ids = jnp.arange(N_SECTION)[:, None, None]
    column = jnp.arange(4 * D)[None, None, :]
    enlarge = jnp.where((section_ids % 2 == 0) & (column >= 3 * D), 8.0, 1.0)
    return jnp.clip(values * enlarge, -2.0, 2.0).astype(jnp.bfloat16)


def block_scale(own_key, shape, pieces, smallest, high):
    level, own = 1.0, jax.random.fold_in(own_key, 6)
    for axis_at, shards_of in pieces:
        draws = jnp.exp(jax.random.uniform(jax.random.fold_in(own, axis_at), (shards_of,), jnp.float32, smallest / len(pieces), high / len(pieces)))
        level = level * jnp.repeat(draws, shape[axis_at] // shards_of).reshape([-1 if axis == axis_at else 1 for axis in range(len(shape))])
    return level


def noise(stream_key, extent, deviation, bound, pieces=(), kind=jnp.bfloat16):
    values = jax.random.normal(stream_key, extent, jnp.float32) * deviation
    if len(pieces) > 0:
        values = block_scale(stream_key, extent, pieces, -0.22, 0.18) * values
    return jnp.clip(values, min=-bound, max=bound).astype(kind)


def setup_inputs(seed: int = 0) -> dict:
    keys = jax.random.split(jax.random.key(seed), 9)
    tokens = noise(keys[0], (SEQS, LEN, D), 1.0, 6.0, ((0, 8),))
    lengths = draw_lengths(jax.random.fold_in(keys[8], 71), 0)
    w_main = draw_w_main(jax.random.fold_in(keys[8], 71), 0)
    w_down_half = noise(keys[3], (N_SECTION, FF // 2, D), D ** -0.5, 0.21875, ((0, 4),))
    out_bias = noise(keys[4], (N_SECTION, D), 0.5, 3.0, ((0, 4),), jnp.float32)
    ln_gain = jnp.clip(1.0 + 0.15 * jax.random.normal(keys[5], (N_SECTION, D), jnp.float32), 0.25, 1.75)
    ln_bias = noise(keys[6], (N_SECTION, D), 0.5, 3.0, ((0, 4),), jnp.float32)
    cotangent = noise(keys[7], (SEQS, LEN, D), 1.0, 6.0, ((0, 8),))
    return {"tokens": tokens, "lengths": lengths, "w_main": w_main, "w_down_half": w_down_half, "out_bias": out_bias, "ln_gain": ln_gain, "ln_bias": ln_bias, "cotangent": cotangent}


NORM_EPS = 1e-06
MASK_FILL = -1000000000.0
HIGHEST = lax.Precision.HIGHEST

@jax.custom_vjp
def low(v):
    return lax.optimization_barrier(v.astype(jnp.bfloat16)).astype(jnp.float32)

@jax.custom_vjp
def low_back(v):
    return v

def low_keep(v):
    return (low(v), None)

def low_pass(kept, grad):
    return (grad,)

def back_keep(v):
    return (v, None)

def back_low(kept, grad):
    return (low(grad),)
low.defvjp(low_keep, low_pass)
low_back.defvjp(back_keep, back_low)

def layer_norm(residual, gain_row, shift_row):
    center = lax.optimization_barrier(jnp.mean(residual, axis=-1, keepdims=True))
    centred = residual - center
    spread = lax.optimization_barrier(jnp.mean(centred * centred, axis=-1, keepdims=True))
    return centred * lax.rsqrt(spread + NORM_EPS) * gain_row + shift_row

def attend(inputs, weights, bias_row, gain_row, shift_row, key_valid):
    seq_len, model_width = inputs.shape
    mixed_qkv = low_back(low(jnp.dot(inputs, weights[:, :3 * model_width], precision=HIGHEST)))
    query_heads = mixed_qkv[:, :model_width].reshape(seq_len, HEADS, HEAD)
    key_heads = mixed_qkv[:, model_width:2 * model_width].reshape(seq_len, HEADS, HEAD)
    value_heads = mixed_qkv[:, 2 * model_width:].reshape(seq_len, HEADS, HEAD)
    scores = jnp.einsum('qhd,khd->hqk', query_heads, key_heads, precision=HIGHEST) * HEAD ** (-0.5)
    scores = low_back(jnp.where(key_valid[None, None, :], scores, MASK_FILL))
    soft_low = low(jax.nn.softmax(scores, axis=-1))
    context = jnp.einsum('hqk,khd->qhd', soft_low, value_heads, precision=HIGHEST).reshape(seq_len, model_width)
    context = low_back(low(context))
    branch = low_back(jnp.dot(context, weights[:, 3 * model_width:], precision=HIGHEST)) + bias_row
    return layer_norm(inputs + branch, gain_row, shift_row)

def feed_block(inputs, weights, down_full, bias_row, gain_row, shift_row):
    pre_act = low_back(jnp.dot(inputs, weights, precision=HIGHEST))
    hidden = low(jax.nn.gelu(pre_act, approximate=False))
    branch = low_back(jnp.dot(hidden, down_full, precision=HIGHEST)) + bias_row
    return layer_norm(inputs + branch, gain_row, shift_row)

def block_chain(main_w, down_half, bias_all, gain_all, shift_all, nudges, inputs, key_valid):
    state = low_back(inputs + nudges[0])
    kept_outs = []
    result = state
    for section_number in range(N_SECTION):
        if section_number % 2 == 0:
            result = attend(state, main_w[section_number], bias_all[section_number], gain_all[section_number], shift_all[section_number], key_valid)
        else:
            down_full = jnp.concatenate([down_half[section_number - 1], down_half[section_number]], axis=0)
            result = feed_block(state, main_w[section_number], down_full, bias_all[section_number], gain_all[section_number], shift_all[section_number])
        result = low(result)
        kept_outs.append(result)
        if section_number + 1 < N_SECTION:
            state = low_back(result + nudges[section_number + 1])
    return (result, jnp.stack(kept_outs))

def reference(tokens, lengths, w_main, w_down_half, out_bias, ln_gain, ln_bias, cotangent):
    main_w = w_main.astype(jnp.float32)
    down_half = w_down_half.astype(jnp.float32)
    bias_all = out_bias.astype(jnp.float32)
    gain_all = ln_gain.astype(jnp.float32)
    shift_all = ln_bias.astype(jnp.float32)
    zero_init = (jnp.zeros_like(main_w), jnp.zeros_like(down_half), jnp.zeros_like(bias_all), jnp.zeros_like(gain_all), jnp.zeros_like(shift_all))

    def one_sequence(accumulated_sums, seq_item):
        inputs, length, seed_grad = seq_item
        key_valid = jnp.arange(LEN, dtype=jnp.int32) < length
        nudges = jnp.zeros((N_SECTION, LEN, D), jnp.float32)

        def forward(arg_main, arg_down, arg_bias, arg_gain, arg_shift, arg_nudges):
            return block_chain(arg_main, arg_down, arg_bias, arg_gain, arg_shift, arg_nudges, inputs.astype(jnp.float32), key_valid)
        final_out, pull_back, kept_outs = jax.vjp(forward, main_w, down_half, bias_all, gain_all, shift_all, nudges, has_aux=True)
        grad_list = pull_back(seed_grad.astype(jnp.float32))
        accumulated_sums = tuple((running_total + summand_value for running_total, summand_value in zip(accumulated_sums, grad_list[:5])))
        return (accumulated_sums, (kept_outs.astype(jnp.bfloat16), grad_list[5].astype(jnp.bfloat16)))
    accumulated_sums, (kept_outs, input_grads) = lax.scan(one_sequence, zero_init, (tokens, lengths, cotangent))
    section_out = jnp.swapaxes(kept_outs, 0, 1)
    section_in_grad = jnp.swapaxes(input_grads, 0, 1)
    return (section_out, section_in_grad, accumulated_sums[0], accumulated_sums[1], accumulated_sums[2], accumulated_sums[3], accumulated_sums[4])
```

```python
from functools import partial

import jax
import jax.numpy as jnp
from jax import lax
from jax.experimental import pallas as pl
from jax.experimental.pallas import tpu as pltpu
from jax.sharding import PartitionSpec as P

HEAD = 64
NORM_EPS = 1e-06
MASK_FILL = -1000000000.0
MESH = pl.DeviceIdType.MESH
BF = jnp.bfloat16
F32 = jnp.float32
MIB = 1024 * 1024
NN = (((1,), (0,)), ((), ()))
NT = (((1,), (1,)), ((), ()))
TN = (((0,), (0,)), ((), ()))
LN_ROWS = 64
W_ORDER = (1, 2, 0, 3)


def mm(a, b, dims=NN):
    return lax.dot_general(a, b, dims, preferred_element_type=F32)


def gelu_pair(x):
    ax = jnp.abs(x)
    t = 1.0 / (1.0 + ax * (0.3275911 * 0.7071067811865476))
    e = jnp.exp(x * x * -0.5)
    poly = ((((0.5 * 1.061405429) * t + (0.5 * -1.453152027)) * t + (0.5 * 1.421413741)) * t + (0.5 * -0.284496736)) * t + (0.5 * 0.254829592)
    tail = poly * t * e
    cdf = jnp.where(x >= 0.0, 1.0 - tail, tail)
    return x * cdf, cdf + x * (e * 0.3989422804014327)


def layer_kernel(
    tok, cot, lens, wm, wd, vec,
    out_ref, ing_ref, g_ref, small_ref,
    W, W2, V, L, R, Q, KV, N, RS, LSE, H2, GIN, GMID, GOUT, RES, DCTX, DKV, DKVR, GR, GS, VR,
    sem_w, sem_tok, sem_cot, send_w, recv_w, send_kv, recv_kv, send_h, recv_h, sem_o, recv_o,
    send_dkv, recv_dkv, send_g, recv_g, sem_i, recv_i, send_gr, recv_gr, sem_go, send_v, recv_v,
):
    nq, seq_len, D = tok.shape
    half = seq_len // 2
    pairs = D // 128
    dp = lax.axis_index("dp")
    s = lax.axis_index("section")
    p = lax.rem(s, 2)
    layer = s // 2
    partner = (dp, s + 1 - 2 * p)
    across = (dp, lax.rem(s + 2, 4))
    first = layer == 0
    last = layer == 1
    own = pl.ds(pl.multiple_of(p * half, half), half)
    other = pl.ds(pl.multiple_of((1 - p) * half, half), half)

    def rows(q):
        return pl.ds(pl.multiple_of(q * half, half), half)

    def copy_w(b):
        return pltpu.make_async_copy(wm.at[:, pl.ds(b * D, D)], W.at[p, b], sem_w.at[b])

    def copy_w2(b):
        return pltpu.make_async_copy(wd.at[pl.ds(b * D, D), :], W2.at[2 * p + b], sem_w.at[4 + b])

    def copy_tok(q):
        return pltpu.make_async_copy(tok.at[q, own], L.at[0, rows(q)], sem_tok.at[q])

    def copy_cot(q):
        return pltpu.make_async_copy(cot.at[q, own], GIN.at[q], sem_cot.at[q])

    @pl.when(first)
    def _():
        for q in range(nq):
            copy_tok(q).start()

    for b in W_ORDER:
        copy_w(b).start()
    for b in range(2):
        copy_w2(b).start()

    @pl.when(last)
    def _():
        for q in range(nq):
            copy_cot(q).start()

    barrier = pltpu.get_barrier_semaphore()
    for peer in (partner, across):
        pl.semaphore_signal(barrier, inc=1, device_id=peer, device_id_type=MESH)
    pl.semaphore_wait(barrier, 2)

    def remote(src, dst, send, recv, dev):
        return pltpu.make_async_remote_copy(
            src_ref=src, dst_ref=dst, send_sem=send, recv_sem=recv, device_id=dev, device_id_type=MESH
        )

    def send_weights(b):
        return remote(wm.at[:, pl.ds(b * D, D)], W.at[p, b], send_w.at[b], recv_w.at[b], partner)

    def send_weights2(b):
        return remote(wd.at[pl.ds(b * D, D), :], W2.at[2 * p + b], send_w.at[4 + b], recv_w.at[4 + b], partner)

    def send_vec():
        return remote(vec, VR, send_v, recv_v, partner)

    send_vec().start()
    for b in W_ORDER:
        send_weights(b).start()
    for b in range(2):
        send_weights2(b).start()

    def need_w(sec, b):
        @pl.when(p == sec)
        def _():
            copy_w(b).wait()

        @pl.when(p != sec)
        def _():
            remote(wm.at[:, pl.ds(b * D, D)], W.at[1 - p, b], send_w.at[b], recv_w.at[b], partner).wait_recv()

    def need_w2():
        for b in range(2):
            copy_w2(b).wait()
            remote(
                wd.at[pl.ds(b * D, D), :], W2.at[2 * (1 - p) + b], send_w.at[4 + b], recv_w.at[4 + b], partner
            ).wait_recv()

    def send_keys(q):
        return remote(KV.at[q, own], KV.at[q, own], send_kv.at[q], recv_kv.at[q], partner)

    def take_keys(q):
        return remote(KV.at[q, other], KV.at[q, other], send_kv.at[q], recv_kv.at[q], partner)

    def hand_on(q):
        return remote(H2.at[q], L.at[0, rows(q)], send_h.at[q], recv_h.at[q], across)

    def hand_back(q):
        return remote(GOUT.at[q], GIN.at[q], send_g.at[q], recv_g.at[q], across)

    def put(src, dst_ref, q, sec, sems, recvs):
        keep = pltpu.make_async_copy(src, dst_ref.at[q, own], sems.at[sec, q])
        give = remote(src, dst_ref.at[q, own], sems.at[sec, q], recvs.at[q], partner)
        return keep, give

    def put_start(src, dst_ref, q, sec, sems, recvs):
        keep, give = put(src, dst_ref, q, sec, sems, recvs)

        @pl.when(p == sec)
        def _():
            keep.start()

        @pl.when(p != sec)
        def _():
            give.start()

    def put_wait(src, dst_ref, q, sec, sems, recvs):
        keep, give = put(src, dst_ref, q, sec, sems, recvs)

        @pl.when(p == sec)
        def _():
            keep.wait()
            remote(src, dst_ref.at[q, other], sems.at[sec, q], recvs.at[q], partner).wait_recv()

        @pl.when(p != sec)
        def _():
            give.wait_send()

    lane = lax.broadcasted_iota(jnp.int32, (1, 128), 1)
    low_lanes = (lane < HEAD).astype(F32)
    high_lanes = 1.0 - low_lanes

    def split_lanes(x):
        wide = x.astype(F32)
        return (wide * low_lanes).astype(BF), (wide * high_lanes).astype(BF)

    key_row = lax.broadcasted_iota(jnp.int32, (seq_len, half), 0)

    def norm_forward(sec, h_ref_at, dst, q):
        bias, gain, shift = V[sec, 0:1, :], V[sec, 1:2, :], V[sec, 2:3, :]

        def body(i, c):
            r = pl.ds(pl.multiple_of(i * LN_ROWS, LN_ROWS), LN_ROWS)
            rq = pl.ds(pl.multiple_of(q * half + i * LN_ROWS, LN_ROWS), LN_ROWS)
            residual = L[h_ref_at, rq, :].astype(F32) + (RES[r, :] + bias)
            center = jnp.mean(residual, axis=-1, keepdims=True)
            centred = residual - center
            spread = jnp.mean(centred * centred, axis=-1, keepdims=True)
            rstd = lax.rsqrt(spread + NORM_EPS)
            normed = centred * rstd
            N[sec, rq, :] = normed.astype(BF)
            RS[sec, rq, :] = jnp.broadcast_to(rstd, (LN_ROWS, 128))
            dst(r, rq, (normed * gain + shift).astype(BF))
            return c

        lax.fori_loop(0, half // LN_ROWS, body, 0)

    def norm_backward(sec, g_ref, at, q):
        gain = V[sec, 1:2, :]

        def body(i, c):
            r = pl.ds(pl.multiple_of(i * LN_ROWS, LN_ROWS), LN_ROWS)
            rq = pl.ds(pl.multiple_of(q * half + i * LN_ROWS, LN_ROWS), LN_ROWS)
            g = g_ref[q, r, :].astype(F32)
            normed = N[sec, rq, :].astype(F32)
            rstd = RS[sec, rq, 0:1]
            gg = g * gain
            first_mean = jnp.mean(gg, axis=-1, keepdims=True)
            second_mean = jnp.mean(gg * normed, axis=-1, keepdims=True)
            dres = rstd * (gg - first_mean - normed * second_mean)
            RES[r, :] = dres
            R[at, rq, :] = dres.astype(BF)
            b, a, t = c
            return (
                b + jnp.sum(dres, axis=0, keepdims=True),
                a + jnp.sum(g * normed, axis=0, keepdims=True),
                t + jnp.sum(g, axis=0, keepdims=True),
            )

        zero = jnp.zeros((1, D), F32)
        b, a, t = lax.fori_loop(0, half // LN_ROWS, body, (zero, zero, zero))
        small_ref[sec, 0:1, :] += b
        small_ref[sec, 1:2, :] += a
        small_ref[sec, 2:3, :] += t

    small_ref[...] = jnp.zeros_like(small_ref)

    def forward(q, carry):
        length = lens[q]

        @pl.when(first)
        def _():
            copy_tok(q).wait()

        @pl.when(last)
        def _():
            hand_on(q).wait_recv()

        @pl.when(q == 0)
        def _():
            need_w(0, 1)

        h = L[0, rows(q), :]
        KV[q, own, 0:D] = mm(h, W[0, 1]).astype(BF)

        @pl.when(q == 0)
        def _():
            need_w(0, 2)

        KV[q, own, D : 2 * D] = mm(h, W[0, 2]).astype(BF)
        send_keys(q).start()

        @pl.when(q == 0)
        def _():
            need_w(0, 0)

        Q[rows(q), :] = (mm(h, W[0, 0]) * HEAD ** (-0.5)).astype(BF)
        take_keys(q).wait_recv()
        valid = key_row < length

        def heads(hp, c):
            cols = pl.ds(pl.multiple_of(hp * 128, 128), 128)
            vcols = pl.ds(pl.multiple_of(D + hp * 128, 128), 128)
            kp = KV[q, :, cols]
            v_t = jnp.transpose(KV[q, :, vcols])
            done = []
            for i, qh in enumerate(split_lanes(Q[rows(q), cols])):
                st = jnp.where(valid, mm(kp, qh, NT), MASK_FILL)
                top = jnp.max(st, axis=0, keepdims=True)
                e = jnp.exp(st - top)
                total = jnp.sum(e, axis=0, keepdims=True)
                LSE[q, 2 * hp + i] = top + jnp.log(total)
                ct = mm(v_t[i * HEAD : (i + 1) * HEAD, :], e.astype(BF))
                done.append(ct * (1.0 / total))
            L[1, rows(q), cols] = jnp.transpose(jnp.concatenate(done, axis=0)).astype(BF)
            return c

        lax.fori_loop(0, pairs, heads, 0)

        @pl.when(q == 0)
        def _():
            need_w(0, 3)
            send_vec().wait_recv()
            mine = vec[...]
            theirs = VR[...]

            @pl.when(p == 0)
            def _():
                V[0] = mine
                V[1] = theirs

            @pl.when(p == 1)
            def _():
                V[0] = theirs
                V[1] = mine

        RES[...] = mm(L[1, rows(q), :], W[0, 3])

        def keep_mid(r, rq, x):
            L[2, rq, :] = x

        norm_forward(0, 0, keep_mid, q)
        put_start(L.at[2, rows(q)], out_ref, q, 0, sem_o, recv_o)

        def up(b, c):
            for j in range(4):
                @pl.when((q == 0) & (b == j))
                def _():
                    need_w(1, j)
            hidden, slope = gelu_pair(mm(L[2, rows(q), :], W[1, b]))
            L[3 + b, rows(q), :] = hidden.astype(BF)
            R[5 + b, rows(q), :] = slope.astype(BF)
            return c

        lax.fori_loop(0, 4, up, 0)

        @pl.when(q == 0)
        def _():
            need_w2()

        for n in range(D // 256):
            c = slice(n * 256, (n + 1) * 256)
            acc = mm(L[3, rows(q), :], W2[0, :, c])
            for b in range(1, 4):
                acc += mm(L[3 + b, rows(q), :], W2[b, :, c])
            RES[:, c] = acc

        def keep_out(r, rq, x):
            H2[q, r, :] = x

        norm_forward(1, 2, keep_out, q)

        @pl.when(first)
        def _():
            hand_on(q).start()

        put_start(H2.at[q], out_ref, q, 1, sem_o, recv_o)
        return carry

    lax.fori_loop(0, nq, forward, 0)

    def send_dkeys(q):
        return remote(DKV.at[1 - p], DKVR.at[q], send_dkv.at[q], recv_dkv.at[q], partner)

    def backward(q, carry):
        length = lens[q]

        @pl.when(last)
        def _():
            copy_cot(q).wait()

        @pl.when(first)
        def _():
            hand_back(q).wait_recv()

        norm_backward(1, GIN, 4, q)

        def down(b, c):
            dh = mm(R[4, rows(q), :], W2[b], NT)
            R[5 + b, rows(q), :] = (dh * R[5 + b, rows(q), :].astype(F32)).astype(BF)
            return c

        lax.fori_loop(0, 4, down, 0)

        for n in range(D // 256):
            c = slice(n * 256, (n + 1) * 256)
            acc = RES[:, c]
            for b in range(4):
                acc += mm(R[5 + b, rows(q), :], W[1, b, c, :], NT)
            GMID[q, :, c] = acc.astype(BF)
        put_start(GMID.at[q], ing_ref, q, 1, sem_i, recv_i)

        norm_backward(0, GMID, 3, q)
        DCTX[...] = mm(R[3, rows(q), :], W[0, 3], NT).astype(BF)

        @pl.when(q > 0)
        def _():
            send_dkeys(q - 1).wait_send()

        valid = key_row < length

        def heads(hp, c):
            cols = pl.ds(pl.multiple_of(hp * 128, 128), 128)
            vcols = pl.ds(pl.multiple_of(D + hp * 128, 128), 128)
            kp = KV[q, :, cols]
            vp = KV[q, :, vcols]
            qp = Q[rows(q), cols]
            dcp = DCTX[:, cols]
            k_t = jnp.transpose(kp)
            dqs, dks, dvs = [], [], []
            for i, (qh, dch) in enumerate(zip(split_lanes(qp), split_lanes(dcp))):
                st = jnp.where(valid, mm(kp, qh, NT), MASK_FILL)
                prob = jnp.exp(st - LSE[q, 2 * hp + i])
                dprob = mm(vp, dch, NT)
                mean = jnp.sum(prob * dprob, axis=0, keepdims=True)
                ds = (prob * (dprob - mean)).astype(BF)
                dvs.append(mm(prob.astype(BF), dcp))
                dks.append(mm(ds, qp))
                dqs.append(mm(k_t[i * HEAD : (i + 1) * HEAD, :], ds))
            dq = jnp.concatenate(dqs, axis=0) * HEAD ** (-0.5)
            R[0, rows(q), cols] = jnp.transpose(dq).astype(BF)
            low = lane < HEAD
            dk = jnp.where(low, dks[0], dks[1]).astype(BF)
            dv = jnp.where(low, dvs[0], dvs[1]).astype(BF)
            DKV[0, :, cols] = dk[:half]
            DKV[1, :, cols] = dk[half:]
            DKV[0, :, vcols] = dv[:half]
            DKV[1, :, vcols] = dv[half:]
            return c

        lax.fori_loop(0, pairs, heads, 0)
        send_dkeys(q).start()
        for n in range(D // 256):
            c = slice(n * 256, (n + 1) * 256)
            RES[:, c] = RES[:, c] + mm(R[0, rows(q), :], W[0, 0, c, :], NT)
        send_dkeys(q).wait_recv()
        R[1, rows(q), :] = (DKV[p, :, 0:D].astype(F32) + DKVR[q, :, 0:D].astype(F32)).astype(BF)
        R[2, rows(q), :] = (DKV[p, :, D : 2 * D].astype(F32) + DKVR[q, :, D : 2 * D].astype(F32)).astype(BF)
        for n in range(D // 256):
            c = slice(n * 256, (n + 1) * 256)
            acc = RES[:, c]
            for b in range(1, 3):
                acc += mm(R[b, rows(q), :], W[0, b, c, :], NT)
            GOUT[q, :, c] = acc.astype(BF)

        @pl.when(last)
        def _():
            hand_back(q).start()

        put_start(GOUT.at[q], ing_ref, q, 0, sem_i, recv_i)
        return carry

    lax.fori_loop(0, nq, backward, 0)

    left = ((0, 0, 0, 1, 3, 4), (2, 2, 2, 2, 5, 6))
    right = ((0, 1, 2, 3, 4, 4), (5, 6, 7, 8, 4, 4))

    def pick(table, sec, j):
        return table[0][j] + sec * (table[1][j] - table[0][j])

    def send_grad(j):
        return remote(GS.at[j % 2], GR.at[j], send_gr.at[j], recv_gr.at[j], partner)

    def store_grad(j):
        return pltpu.make_async_copy(GR.at[j], g_ref.at[j], sem_go.at[j])

    for j in range(6):
        li, ri = pick(left, 1 - p, j), pick(right, 1 - p, j)
        if j >= 2:
            send_grad(j - 2).wait_send()
        for n in range(D // 256):
            c = slice(n * 256, (n + 1) * 256)
            GS[j % 2, :, c] = mm(L[li], R[ri, :, c], TN).astype(BF)
        send_grad(j).start()
    for j in range(6):
        li, ri = pick(left, p, j), pick(right, p, j)
        send_grad(j).wait_recv()
        for n in range(D // 256):
            c = slice(n * 256, (n + 1) * 256)
            GR[j, :, c] = (mm(L[li], R[ri, :, c], TN) + GR[j, :, c].astype(F32)).astype(BF)
        store_grad(j).start()

    for j in range(4, 6):
        send_grad(j).wait_send()
    for j in range(6):
        store_grad(j).wait()
    send_vec().wait_send()
    for b in range(4):
        send_weights(b).wait_send()
    for b in range(2):
        send_weights2(b).wait_send()
    send_dkeys(nq - 1).wait_send()
    for q in range(nq):
        send_keys(q).wait_send()

        @pl.when(first)
        def _():
            hand_on(q).wait_send()

        @pl.when(last)
        def _():
            hand_back(q).wait_send()

        put_wait(L.at[2, rows(q)], out_ref, q, 0, sem_o, recv_o)
        put_wait(H2.at[q], out_ref, q, 1, sem_o, recv_o)
        put_wait(GMID.at[q], ing_ref, q, 1, sem_i, recv_i)
        put_wait(GOUT.at[q], ing_ref, q, 0, sem_i, recv_i)


def run_layers(tokens, cotangent, lengths, weights, w_down, vec):
    nq, seq_len, D = tokens.shape
    half = seq_len // 2
    tall = nq * half
    dma = pltpu.SemaphoreType.DMA
    any_spec = pl.BlockSpec(memory_space=pl.ANY)
    vmem_spec = pl.BlockSpec(memory_space=pltpu.VMEM)
    return pl.pallas_call(
        layer_kernel,
        name="layers",
        out_shape=(
            jax.ShapeDtypeStruct((nq, seq_len, D), BF),
            jax.ShapeDtypeStruct((nq, seq_len, D), BF),
            jax.ShapeDtypeStruct((6, D, D), BF),
            jax.ShapeDtypeStruct((2, 8, D), F32),
        ),
        in_specs=[any_spec, any_spec, pl.BlockSpec(memory_space=pltpu.SMEM), any_spec, any_spec, vmem_spec],
        out_specs=(any_spec, any_spec, any_spec, vmem_spec),
        scratch_shapes=[
            pltpu.VMEM((2, 4, D, D), BF),
            pltpu.VMEM((4, D, D), BF),
            pltpu.VMEM((2, 8, D), F32),
            pltpu.VMEM((7, tall, D), BF),
            pltpu.VMEM((9, tall, D), BF),
            pltpu.VMEM((tall, D), BF),
            pltpu.VMEM((nq, seq_len, 2 * D), BF),
            pltpu.VMEM((2, tall, D), BF),
            pltpu.VMEM((2, tall, 128), F32),
            pltpu.VMEM((nq, D // HEAD, 1, half), F32),
            pltpu.VMEM((nq, half, D), BF),
            pltpu.VMEM((nq, half, D), BF),
            pltpu.VMEM((nq, half, D), BF),
            pltpu.VMEM((nq, half, D), BF),
            pltpu.VMEM((half, D), F32),
            pltpu.VMEM((half, D), BF),
            pltpu.VMEM((2, half, 2 * D), BF),
            pltpu.VMEM((nq, half, 2 * D), BF),
            pltpu.VMEM((6, D, D), BF),
            pltpu.VMEM((2, D, D), BF),
            pltpu.VMEM((8, D), F32),
            dma((6,)), dma((nq,)), dma((nq,)), dma((6,)), dma((6,)),
            dma((nq,)), dma((nq,)), dma((nq,)), dma((nq,)), dma((2, nq)), dma((nq,)),
            dma((nq,)), dma((nq,)), dma((nq,)), dma((nq,)), dma((2, nq)), dma((nq,)),
            dma((6,)), dma((6,)), dma((6,)), dma, dma,
        ],
        compiler_params=pltpu.CompilerParams(
            collective_id=0, has_side_effects=True, vmem_limit_bytes=63 * MIB
        ),
        cost_estimate=pl.CostEstimate(flops=60 * 10**9, bytes_accessed=40 * 10**6, transcendentals=10**7),
    )(tokens, cotangent, lengths, weights, w_down, vec)


CLASS_ROWS = (112, 112, 160)
CLASS_AT = (0, 112, 224)
STEP_ROWS = 384
LAG = 4


def sum_kernel(line, g_ref, small_in, fin_ref, small_out, G, RV, FIN, SR, sem_in, sem_out, s_up, s_down, r_up, r_fin, t_up, t_down, q_up, q_fin):
    blocks, D, _ = g_ref.shape
    steps = blocks * D // STEP_ROWS
    per = D // STEP_ROWS
    dp = lax.axis_index("dp")
    s = lax.axis_index("section")
    y = lax.rem(dp, 2)
    z = dp // 2
    has_dn = z > 0
    has_up = z < line - 1
    side = (dp + 1 - 2 * y, s)
    below = (lax.rem(dp + 2 * line - 2, 2 * line), s)
    above = (lax.rem(dp + 2, 2 * line), s)
    peers = (side, below, above)

    def load(b):
        return pltpu.make_async_copy(g_ref.at[b], G.at[b], sem_in.at[b])

    def store(b):
        return pltpu.make_async_copy(FIN.at[b], fin_ref.at[b], sem_out.at[b])

    for b in range(blocks):
        load(b).start()

    barrier = pltpu.get_barrier_semaphore()
    pl.semaphore_signal(barrier, inc=1, device_id=side, device_id_type=MESH)

    @pl.when(has_dn)
    def _():
        pl.semaphore_signal(barrier, inc=1, device_id=below, device_id_type=MESH)

    @pl.when(has_up)
    def _():
        pl.semaphore_signal(barrier, inc=1, device_id=above, device_id_type=MESH)

    pl.semaphore_wait(barrier, 1 + has_dn.astype(jnp.int32) + has_up.astype(jnp.int32))

    def roles(kind, k):
        if kind < 2:
            rail = y == kind
            return (
                (rail, rail & (z <= k) & has_dn, rail & (z >= k) & has_up),
                (jnp.logical_not(rail), rail & (z > k), rail & (z < k)),
            )
        at = z == k
        return (
            (at & (y == 0), (z <= k) & has_dn, (z >= k) & has_up),
            (at & (y == 1), z > k, z < k),
        )

    def root_of(kind, i):
        if kind < 2:
            return line // 2 - 1 + lax.rem(i, 2)
        return lax.rem(line // 2 - 1 + i, line)

    def rem_copy(src, dst, send, recv, dev):
        return pltpu.make_async_remote_copy(
            src_ref=src, dst_ref=dst, send_sem=send, recv_sem=recv, device_id=dev, device_id_type=MESH
        )

    slot_at_parent = (0, 2, 1)

    def tree(kids, parents, acc, slots, fin, sup, sdown, rup, rfin):
        def add_children():
            for n in range(3):
                @pl.when(kids[n])
                def _():
                    rem_copy(slots(n), slots(n), sup, rup(n), peers[n]).wait_recv()
                    acc[...] = (acc[...].astype(F32) + slots(n)[...].astype(F32)).astype(acc.dtype)

        def send_up(wait):
            for n in range(3):
                @pl.when(parents[n])
                def _():
                    c = rem_copy(acc, slots(slot_at_parent[n]), sup, rup(slot_at_parent[n]), peers[n])
                    c.wait_send() if wait else c.start()

        root = jnp.logical_not(parents[0] | parents[1] | parents[2])

        def finish_root():
            @pl.when(root)
            def _():
                fin[...] = acc[...]

        def wait_final():
            @pl.when(jnp.logical_not(root))
            def _():
                rem_copy(acc, fin, sup, rfin, peers[0]).wait_recv()

        def send_down(wait):
            for n in range(3):
                @pl.when(kids[n])
                def _():
                    c = rem_copy(fin, fin, sdown(n), rfin, peers[n])
                    c.wait_send() if wait else c.start()

        return root, add_children, send_up, finish_root, wait_final, send_down

    def chunk(kind, i):
        b = i // per
        at = pl.multiple_of(lax.rem(i, per) * STEP_ROWS + CLASS_AT[kind], 16)
        r = pl.ds(at, CLASS_ROWS[kind])
        kids, parents = roles(kind, root_of(kind, i))
        return tree(
            kids, parents, G.at[b, r], lambda n: RV.at[n, b, r], FIN.at[b, r],
            s_up.at[kind, i], lambda n: s_down.at[kind, n, i], lambda n: r_up.at[kind, n, i], r_fin.at[kind, i],
        )

    def up(i):
        @pl.when(lax.rem(i, per) == 0)
        def _():
            load(i // per).wait()

        for kind in range(3):
            root, add_children, send_up, finish_root, wait_final, send_down = chunk(kind, i)
            add_children()
            send_up(False)
            finish_root()

            @pl.when(root)
            def _():
                send_down(False)

    def down(i):
        for kind in range(3):
            root, add_children, send_up, finish_root, wait_final, send_down = chunk(kind, i)
            wait_final()

            @pl.when(jnp.logical_not(root))
            def _():
                send_down(False)

        @pl.when(lax.rem(i, per) == per - 1)
        def _():
            store(i // per).start()

    SR[3] = small_in[...]
    kids, parents = roles(0, line // 2)
    little = tree(
        kids, parents, SR.at[3], lambda n: SR.at[n], SR.at[4], t_up, lambda n: t_down.at[n], lambda n: q_up.at[n], q_fin
    )
    little[1]()
    little[2](False)
    little[3]()

    @pl.when(little[0])
    def _():
        little[5](False)

    def step(i, c):
        @pl.when(i < steps)
        def _():
            up(i)

        @pl.when(i >= LAG)
        def _():
            down(i - LAG)

        return c

    lax.fori_loop(0, steps + LAG, step, 0)
    little[4]()

    @pl.when(jnp.logical_not(little[0]))
    def _():
        little[5](False)

    small_out[...] = SR[4]

    def drain(i, c):
        for kind in range(3):
            t = chunk(kind, i)
            t[2](True)
            t[5](True)
        return c

    lax.fori_loop(0, steps, drain, 0)
    little[2](True)
    little[5](True)
    for b in range(blocks):
        store(b).wait()


def sum_over_dp(grads, small):
    blocks, D, _ = grads.shape
    steps = blocks * D // STEP_ROWS
    line = lax.axis_size("dp") // 2
    dma = pltpu.SemaphoreType.DMA
    any_spec = pl.BlockSpec(memory_space=pl.ANY)
    vmem_spec = pl.BlockSpec(memory_space=pltpu.VMEM)
    return pl.pallas_call(
        partial(sum_kernel, line),
        name="sum_over_dp",
        out_shape=(
            jax.ShapeDtypeStruct(grads.shape, BF),
            jax.ShapeDtypeStruct(small.shape, F32),
        ),
        in_specs=[any_spec, vmem_spec],
        out_specs=(any_spec, vmem_spec),
        scratch_shapes=[
            pltpu.VMEM((blocks, D, D), BF),
            pltpu.VMEM((3, blocks, D, D), BF),
            pltpu.VMEM((blocks, D, D), BF),
            pltpu.VMEM((5,) + small.shape, F32),
            dma((blocks,)), dma((blocks,)),
            dma((3, steps)), dma((3, 3, steps)), dma((3, 3, steps)), dma((3, steps)),
            dma, dma((3,)), dma((3,)), dma,
        ],
        compiler_params=pltpu.CompilerParams(
            collective_id=1, has_side_effects=True, vmem_limit_bytes=60 * MIB
        ),
        cost_estimate=pl.CostEstimate(flops=10**7, bytes_accessed=30 * 10**6, transcendentals=0),
    )(grads, small)


def on_device(tokens, lengths, w_main, w_down_half, out_bias, ln_gain, ln_bias, cotangent):
    D = tokens.shape[-1]
    s = lax.axis_index("section")
    p = lax.rem(s, 2)
    vec = jnp.concatenate([out_bias, ln_gain, ln_bias, jnp.zeros((5, D), F32)], axis=0)
    kept_out, kept_grad, grads, small = run_layers(tokens, cotangent, lengths, w_main[0], w_down_half[0], vec)
    mine = lax.dynamic_index_in_dim(small, p, 0, keepdims=False)
    theirs = lax.dynamic_index_in_dim(small, 1 - p, 0, keepdims=False)
    pairs = [(i, i + 1 - 2 * (i % 2)) for i in range(lax.axis_size("section"))]
    small = mine + lax.ppermute(theirs, "section", pairs)
    total, small = sum_over_dp(grads, small)
    grad_main = jnp.swapaxes(total[:4], 0, 1).reshape(D, 4 * D).astype(F32)
    grad_half = total[4:].reshape(2 * D, D).astype(F32)
    return (
        kept_out[None],
        kept_grad[None],
        grad_main[None],
        grad_half[None],
        small[0:1],
        small[1:2],
        small[2:3],
    )


def solution(mesh):
    in_specs = (
        P("dp", None, None),
        P("dp"),
        P("section", None, None),
        P("section", None, None),
        P("section", None),
        P("section", None),
        P("section", None),
        P("dp", None, None),
    )
    out_specs = (
        P("section", "dp", None, None),
        P("section", "dp", None, None),
        P("section", None, None),
        P("section", None, None),
        P("section", None),
        P("section", None),
        P("section", None),
    )
    return jax.shard_map(
        on_device, mesh=mesh, in_specs=in_specs, out_specs=out_specs, check_vma=False
    )
```

```python
from functools import partial

import jax
import jax.numpy as jnp
from jax import lax
from jax.experimental import pallas as pl
from jax.experimental.pallas import tpu as pltpu
from jax.sharding import PartitionSpec as P

HEAD = 64
NORM_EPS = 1e-06
MASK_FILL = -1000000000.0
MESH = pl.DeviceIdType.MESH
BF = jnp.bfloat16
F32 = jnp.float32
MIB = 1024 * 1024
NN = (((1,), (0,)), ((), ()))
NT = (((1,), (1,)), ((), ()))
TN = (((0,), (0,)), ((), ()))
LN_ROWS = 64
W_ORDER = (1, 2, 0, 3)


def mm(a, b, dims=NN):
    return lax.dot_general(a, b, dims, preferred_element_type=F32)


def gelu_pair(x):
    ax = jnp.abs(x)
    t = 1.0 / (1.0 + ax * (0.3275911 * 0.7071067811865476))
    e = jnp.exp(x * x * -0.5)
    poly = ((((0.5 * 1.061405429) * t + (0.5 * -1.453152027)) * t + (0.5 * 1.421413741)) * t + (0.5 * -0.284496736)) * t + (0.5 * 0.254829592)
    tail = poly * t * e
    cdf = jnp.where(x >= 0.0, 1.0 - tail, tail)
    return x * cdf, cdf + x * (e * 0.3989422804014327)


def layer_kernel(
    tok, cot, lens, wm, wd, vec,
    out_ref, ing_ref, g_ref, small_ref,
    W, W2, V, L, R, Q, KV, N, RS, LSE, H2, GIN, GMID, GOUT, RES, DCTX, DKV, DKVR, GR, GS, VR,
    sem_w, sem_tok, sem_cot, send_w, recv_w, send_kv, recv_kv, send_h, recv_h, sem_o, recv_o,
    send_dkv, recv_dkv, send_g, recv_g, sem_i, recv_i, send_gr, recv_gr, sem_go, send_v, recv_v,
):
    nq, seq_len, D = tok.shape
    half = seq_len // 2
    pairs = D // 128
    dp = lax.axis_index("dp")
    s = lax.axis_index("section")
    p = lax.rem(s, 2)
    layer = s // 2
    partner = (dp, s + 1 - 2 * p)
    across = (dp, lax.rem(s + 2, 4))
    first = layer == 0
    last = layer == 1
    own = pl.ds(pl.multiple_of(p * half, half), half)
    other = pl.ds(pl.multiple_of((1 - p) * half, half), half)

    def rows(q):
        return pl.ds(pl.multiple_of(q * half, half), half)

    def copy_w(b):
        return pltpu.make_async_copy(wm.at[:, pl.ds(b * D, D)], W.at[p, b], sem_w.at[b])

    def copy_w2(b):
        return pltpu.make_async_copy(wd.at[pl.ds(b * D, D), :], W2.at[2 * p + b], sem_w.at[4 + b])

    def copy_tok(q):
        return pltpu.make_async_copy(tok.at[q, own], L.at[0, rows(q)], sem_tok.at[q])

    def copy_cot(q):
        return pltpu.make_async_copy(cot.at[q, own], GIN.at[q], sem_cot.at[q])

    @pl.when(first)
    def _():
        for q in range(nq):
            copy_tok(q).start()

    for b in W_ORDER:
        copy_w(b).start()
    for b in range(2):
        copy_w2(b).start()

    @pl.when(last)
    def _():
        for q in range(nq):
            copy_cot(q).start()

    barrier = pltpu.get_barrier_semaphore()
    for peer in (partner, across):
        pl.semaphore_signal(barrier, inc=1, device_id=peer, device_id_type=MESH)
    pl.semaphore_wait(barrier, 2)

    def remote(src, dst, send, recv, dev):
        return pltpu.make_async_remote_copy(
            src_ref=src, dst_ref=dst, send_sem=send, recv_sem=recv, device_id=dev, device_id_type=MESH
        )

    def send_weights(b):
        return remote(wm.at[:, pl.ds(b * D, D)], W.at[p, b], send_w.at[b], recv_w.at[b], partner)

    def send_weights2(b):
        return remote(wd.at[pl.ds(b * D, D), :], W2.at[2 * p + b], send_w.at[4 + b], recv_w.at[4 + b], partner)

    def send_vec():
        return remote(vec, VR, send_v, recv_v, partner)

    send_vec().start()
    for b in W_ORDER:
        send_weights(b).start()
    for b in range(2):
        send_weights2(b).start()

    def need_w(sec, b):
        @pl.when(p == sec)
        def _():
            copy_w(b).wait()

        @pl.when(p != sec)
        def _():
            remote(wm.at[:, pl.ds(b * D, D)], W.at[1 - p, b], send_w.at[b], recv_w.at[b], partner).wait_recv()

    def need_w2():
        for b in range(2):
            copy_w2(b).wait()
            remote(
                wd.at[pl.ds(b * D, D), :], W2.at[2 * (1 - p) + b], send_w.at[4 + b], recv_w.at[4 + b], partner
            ).wait_recv()

    def send_keys(q):
        return remote(KV.at[q, own], KV.at[q, own], send_kv.at[q], recv_kv.at[q], partner)

    def take_keys(q):
        return remote(KV.at[q, other], KV.at[q, other], send_kv.at[q], recv_kv.at[q], partner)

    def hand_on(q):
        return remote(H2.at[q], L.at[0, rows(q)], send_h.at[q], recv_h.at[q], across)

    def hand_back(q):
        return remote(GOUT.at[q], GIN.at[q], send_g.at[q], recv_g.at[q], across)

    def put(src, dst_ref, q, sec, sems, recvs):
        keep = pltpu.make_async_copy(src, dst_ref.at[q, own], sems.at[sec, q])
        give = remote(src, dst_ref.at[q, own], sems.at[sec, q], recvs.at[q], partner)
        return keep, give

    def put_start(src, dst_ref, q, sec, sems, recvs):
        keep, give = put(src, dst_ref, q, sec, sems, recvs)

        @pl.when(p == sec)
        def _():
            keep.start()

        @pl.when(p != sec)
        def _():
            give.start()

    def put_wait(src, dst_ref, q, sec, sems, recvs):
        keep, give = put(src, dst_ref, q, sec, sems, recvs)

        @pl.when(p == sec)
        def _():
            keep.wait()
            remote(src, dst_ref.at[q, other], sems.at[sec, q], recvs.at[q], partner).wait_recv()

        @pl.when(p != sec)
        def _():
            give.wait_send()

    lane = lax.broadcasted_iota(jnp.int32, (1, 128), 1)
    low_lanes = (lane < HEAD).astype(F32)
    high_lanes = 1.0 - low_lanes

    def split_lanes(x):
        wide = x.astype(F32)
        return (wide * low_lanes).astype(BF), (wide * high_lanes).astype(BF)

    key_row = lax.broadcasted_iota(jnp.int32, (seq_len, half), 0)

    def norm_forward(sec, h_ref_at, dst, q):
        bias, gain, shift = V[sec, 0:1, :], V[sec, 1:2, :], V[sec, 2:3, :]

        def body(i, c):
            r = pl.ds(pl.multiple_of(i * LN_ROWS, LN_ROWS), LN_ROWS)
            rq = pl.ds(pl.multiple_of(q * half + i * LN_ROWS, LN_ROWS), LN_ROWS)
            residual = L[h_ref_at, rq, :].astype(F32) + (RES[r, :] + bias)
            center = jnp.mean(residual, axis=-1, keepdims=True)
            centred = residual - center
            spread = jnp.mean(centred * centred, axis=-1, keepdims=True)
            rstd = lax.rsqrt(spread + NORM_EPS)
            normed = centred * rstd
            N[sec, rq, :] = normed.astype(BF)
            RS[sec, rq, :] = jnp.broadcast_to(rstd, (LN_ROWS, 128))
            dst(r, rq, (normed * gain + shift).astype(BF))
            return c

        lax.fori_loop(0, half // LN_ROWS, body, 0)

    def norm_backward(sec, g_ref, at, q):
        gain = V[sec, 1:2, :]

        def body(i, c):
            r = pl.ds(pl.multiple_of(i * LN_ROWS, LN_ROWS), LN_ROWS)
            rq = pl.ds(pl.multiple_of(q * half + i * LN_ROWS, LN_ROWS), LN_ROWS)
            g = g_ref[q, r, :].astype(F32)
            normed = N[sec, rq, :].astype(F32)
            rstd = RS[sec, rq, 0:1]
            gg = g * gain
            first_mean = jnp.mean(gg, axis=-1, keepdims=True)
            second_mean = jnp.mean(gg * normed, axis=-1, keepdims=True)
            dres = rstd * (gg - first_mean - normed * second_mean)
            RES[r, :] = dres
            R[at, rq, :] = dres.astype(BF)
            b, a, t = c
            return (
                b + jnp.sum(dres, axis=0, keepdims=True),
                a + jnp.sum(g * normed, axis=0, keepdims=True),
                t + jnp.sum(g, axis=0, keepdims=True),
            )

        zero = jnp.zeros((1, D), F32)
        b, a, t = lax.fori_loop(0, half // LN_ROWS, body, (zero, zero, zero))
        small_ref[sec, 0:1, :] += b
        small_ref[sec, 1:2, :] += a
        small_ref[sec, 2:3, :] += t

    small_ref[...] = jnp.zeros_like(small_ref)

    def forward(q, carry):
        length = lens[q]

        @pl.when(first)
        def _():
            copy_tok(q).wait()

        @pl.when(last)
        def _():
            hand_on(q).wait_recv()

        @pl.when(q == 0)
        def _():
            need_w(0, 1)

        h = L[0, rows(q), :]
        KV[q, own, 0:D] = mm(h, W[0, 1]).astype(BF)

        @pl.when(q == 0)
        def _():
            need_w(0, 2)

        KV[q, own, D : 2 * D] = mm(h, W[0, 2]).astype(BF)
        send_keys(q).start()

        @pl.when(q == 0)
        def _():
            need_w(0, 0)

        Q[rows(q), :] = (mm(h, W[0, 0]) * HEAD ** (-0.5)).astype(BF)
        take_keys(q).wait_recv()
        valid = key_row < length

        def heads(hp, c):
            cols = pl.ds(pl.multiple_of(hp * 128, 128), 128)
            vcols = pl.ds(pl.multiple_of(D + hp * 128, 128), 128)
            kp = KV[q, :, cols]
            v_t = jnp.transpose(KV[q, :, vcols])
            done = []
            for i, qh in enumerate(split_lanes(Q[rows(q), cols])):
                st = jnp.where(valid, mm(kp, qh, NT), MASK_FILL)
                top = jnp.max(st, axis=0, keepdims=True)
                e = jnp.exp(st - top)
                total = jnp.sum(e, axis=0, keepdims=True)
                LSE[q, 2 * hp + i] = top + jnp.log(total)
                ct = mm(v_t[i * HEAD : (i + 1) * HEAD, :], e.astype(BF))
                done.append(ct * (1.0 / total))
            L[1, rows(q), cols] = jnp.transpose(jnp.concatenate(done, axis=0)).astype(BF)
            return c

        lax.fori_loop(0, pairs, heads, 0)

        @pl.when(q == 0)
        def _():
            need_w(0, 3)
            send_vec().wait_recv()
            mine = vec[...]
            theirs = VR[...]

            @pl.when(p == 0)
            def _():
                V[0] = mine
                V[1] = theirs

            @pl.when(p == 1)
            def _():
                V[0] = theirs
                V[1] = mine

        RES[...] = mm(L[1, rows(q), :], W[0, 3])

        def keep_mid(r, rq, x):
            L[2, rq, :] = x

        norm_forward(0, 0, keep_mid, q)
        put_start(L.at[2, rows(q)], out_ref, q, 0, sem_o, recv_o)

        def up(b, c):
            for j in range(4):
                @pl.when((q == 0) & (b == j))
                def _():
                    need_w(1, j)
            hidden, slope = gelu_pair(mm(L[2, rows(q), :], W[1, b]))
            L[3 + b, rows(q), :] = hidden.astype(BF)
            R[5 + b, rows(q), :] = slope.astype(BF)
            return c

        lax.fori_loop(0, 4, up, 0)

        @pl.when(q == 0)
        def _():
            need_w2()

        for n in range(D // 256):
            c = slice(n * 256, (n + 1) * 256)
            acc = mm(L[3, rows(q), :], W2[0, :, c])
            for b in range(1, 4):
                acc += mm(L[3 + b, rows(q), :], W2[b, :, c])
            RES[:, c] = acc

        def keep_out(r, rq, x):
            H2[q, r, :] = x

        norm_forward(1, 2, keep_out, q)

        @pl.when(first)
        def _():
            hand_on(q).start()

        put_start(H2.at[q], out_ref, q, 1, sem_o, recv_o)
        return carry

    lax.fori_loop(0, nq, forward, 0)

    def send_dkeys(q):
        return remote(DKV.at[1 - p], DKVR.at[q], send_dkv.at[q], recv_dkv.at[q], partner)

    def backward(q, carry):
        length = lens[q]

        @pl.when(last)
        def _():
            copy_cot(q).wait()

        @pl.when(first)
        def _():
            hand_back(q).wait_recv()

        norm_backward(1, GIN, 4, q)

        def down(b, c):
            dh = mm(R[4, rows(q), :], W2[b], NT)
            R[5 + b, rows(q), :] = (dh * R[5 + b, rows(q), :].astype(F32)).astype(BF)
            return c

        lax.fori_loop(0, 4, down, 0)

        for n in range(D // 256):
            c = slice(n * 256, (n + 1) * 256)
            acc = RES[:, c]
            for b in range(4):
                acc += mm(R[5 + b, rows(q), :], W[1, b, c, :], NT)
            GMID[q, :, c] = acc.astype(BF)
        put_start(GMID.at[q], ing_ref, q, 1, sem_i, recv_i)

        norm_backward(0, GMID, 3, q)
        DCTX[...] = mm(R[3, rows(q), :], W[0, 3], NT).astype(BF)

        @pl.when(q > 0)
        def _():
            send_dkeys(q - 1).wait_send()

        valid = key_row < length

        def heads(hp, c):
            cols = pl.ds(pl.multiple_of(hp * 128, 128), 128)
            vcols = pl.ds(pl.multiple_of(D + hp * 128, 128), 128)
            kp = KV[q, :, cols]
            vp = KV[q, :, vcols]
            qp = Q[rows(q), cols]
            dcp = DCTX[:, cols]
            k_t = jnp.transpose(kp)
            dqs, dks, dvs = [], [], []
            for i, (qh, dch) in enumerate(zip(split_lanes(qp), split_lanes(dcp))):
                st = jnp.where(valid, mm(kp, qh, NT), MASK_FILL)
                prob = jnp.exp(st - LSE[q, 2 * hp + i])
                dprob = mm(vp, dch, NT)
                mean = jnp.sum(prob * dprob, axis=0, keepdims=True)
                ds = (prob * (dprob - mean)).astype(BF)
                dvs.append(mm(prob.astype(BF), dcp))
                dks.append(mm(ds, qp))
                dqs.append(mm(k_t[i * HEAD : (i + 1) * HEAD, :], ds))
            dq = jnp.concatenate(dqs, axis=0) * HEAD ** (-0.5)
            R[0, rows(q), cols] = jnp.transpose(dq).astype(BF)
            low = lane < HEAD
            dk = jnp.where(low, dks[0], dks[1]).astype(BF)
            dv = jnp.where(low, dvs[0], dvs[1]).astype(BF)
            DKV[0, :, cols] = dk[:half]
            DKV[1, :, cols] = dk[half:]
            DKV[0, :, vcols] = dv[:half]
            DKV[1, :, vcols] = dv[half:]
            return c

        lax.fori_loop(0, pairs, heads, 0)
        send_dkeys(q).start()
        for n in range(D // 256):
            c = slice(n * 256, (n + 1) * 256)
            RES[:, c] = RES[:, c] + mm(R[0, rows(q), :], W[0, 0, c, :], NT)
        send_dkeys(q).wait_recv()
        R[1, rows(q), :] = (DKV[p, :, 0:D].astype(F32) + DKVR[q, :, 0:D].astype(F32)).astype(BF)
        R[2, rows(q), :] = (DKV[p, :, D : 2 * D].astype(F32) + DKVR[q, :, D : 2 * D].astype(F32)).astype(BF)
        for n in range(D // 256):
            c = slice(n * 256, (n + 1) * 256)
            acc = RES[:, c]
            for b in range(1, 3):
                acc += mm(R[b, rows(q), :], W[0, b, c, :], NT)
            GOUT[q, :, c] = acc.astype(BF)

        @pl.when(last)
        def _():
            hand_back(q).start()

        put_start(GOUT.at[q], ing_ref, q, 0, sem_i, recv_i)
        return carry

    lax.fori_loop(0, nq, backward, 0)

    left = ((0, 0, 0, 1, 3, 4), (2, 2, 2, 2, 5, 6))
    right = ((0, 1, 2, 3, 4, 4), (5, 6, 7, 8, 4, 4))

    def pick(table, sec, j):
        return table[0][j] + sec * (table[1][j] - table[0][j])

    def send_grad(j):
        return remote(GS.at[j % 2], GR.at[j], send_gr.at[j], recv_gr.at[j], partner)

    def store_grad(j):
        return pltpu.make_async_copy(GR.at[j], g_ref.at[j], sem_go.at[j])

    for j in range(6):
        li, ri = pick(left, 1 - p, j), pick(right, 1 - p, j)
        if j >= 2:
            send_grad(j - 2).wait_send()
        for n in range(D // 256):
            c = slice(n * 256, (n + 1) * 256)
            GS[j % 2, :, c] = mm(L[li], R[ri, :, c], TN).astype(BF)
        send_grad(j).start()
    for j in range(6):
        li, ri = pick(left, p, j), pick(right, p, j)
        send_grad(j).wait_recv()
        for n in range(D // 256):
            c = slice(n * 256, (n + 1) * 256)
            GR[j, :, c] = (mm(L[li], R[ri, :, c], TN) + GR[j, :, c].astype(F32)).astype(BF)
        store_grad(j).start()

    for j in range(4, 6):
        send_grad(j).wait_send()
    for j in range(6):
        store_grad(j).wait()
    send_vec().wait_send()
    for b in range(4):
        send_weights(b).wait_send()
    for b in range(2):
        send_weights2(b).wait_send()
    send_dkeys(nq - 1).wait_send()
    for q in range(nq):
        send_keys(q).wait_send()

        @pl.when(first)
        def _():
            hand_on(q).wait_send()

        @pl.when(last)
        def _():
            hand_back(q).wait_send()

        put_wait(L.at[2, rows(q)], out_ref, q, 0, sem_o, recv_o)
        put_wait(H2.at[q], out_ref, q, 1, sem_o, recv_o)
        put_wait(GMID.at[q], ing_ref, q, 1, sem_i, recv_i)
        put_wait(GOUT.at[q], ing_ref, q, 0, sem_i, recv_i)


def run_layers(tokens, cotangent, lengths, weights, w_down, vec):
    nq, seq_len, D = tokens.shape
    half = seq_len // 2
    tall = nq * half
    dma = pltpu.SemaphoreType.DMA
    any_spec = pl.BlockSpec(memory_space=pl.ANY)
    vmem_spec = pl.BlockSpec(memory_space=pltpu.VMEM)
    return pl.pallas_call(
        layer_kernel,
        name="layers",
        out_shape=(
            jax.ShapeDtypeStruct((nq, seq_len, D), BF),
            jax.ShapeDtypeStruct((nq, seq_len, D), BF),
            jax.ShapeDtypeStruct((6, D, D), BF),
            jax.ShapeDtypeStruct((2, 8, D), F32),
        ),
        in_specs=[any_spec, any_spec, pl.BlockSpec(memory_space=pltpu.SMEM), any_spec, any_spec, vmem_spec],
        out_specs=(any_spec, any_spec, any_spec, vmem_spec),
        scratch_shapes=[
            pltpu.VMEM((2, 4, D, D), BF),
            pltpu.VMEM((4, D, D), BF),
            pltpu.VMEM((2, 8, D), F32),
            pltpu.VMEM((7, tall, D), BF),
            pltpu.VMEM((9, tall, D), BF),
            pltpu.VMEM((tall, D), BF),
            pltpu.VMEM((nq, seq_len, 2 * D), BF),
            pltpu.VMEM((2, tall, D), BF),
            pltpu.VMEM((2, tall, 128), F32),
            pltpu.VMEM((nq, D // HEAD, 1, half), F32),
            pltpu.VMEM((nq, half, D), BF),
            pltpu.VMEM((nq, half, D), BF),
            pltpu.VMEM((nq, half, D), BF),
            pltpu.VMEM((nq, half, D), BF),
            pltpu.VMEM((half, D), F32),
            pltpu.VMEM((half, D), BF),
            pltpu.VMEM((2, half, 2 * D), BF),
            pltpu.VMEM((nq, half, 2 * D), BF),
            pltpu.VMEM((6, D, D), BF),
            pltpu.VMEM((2, D, D), BF),
            pltpu.VMEM((8, D), F32),
            dma((6,)), dma((nq,)), dma((nq,)), dma((6,)), dma((6,)),
            dma((nq,)), dma((nq,)), dma((nq,)), dma((nq,)), dma((2, nq)), dma((nq,)),
            dma((nq,)), dma((nq,)), dma((nq,)), dma((nq,)), dma((2, nq)), dma((nq,)),
            dma((6,)), dma((6,)), dma((6,)), dma, dma,
        ],
        compiler_params=pltpu.CompilerParams(
            collective_id=0, has_side_effects=True, vmem_limit_bytes=63 * MIB
        ),
        cost_estimate=pl.CostEstimate(flops=60 * 10**9, bytes_accessed=40 * 10**6, transcendentals=10**7),
    )(tokens, cotangent, lengths, weights, w_down, vec)


CLASS_ROWS = 48
CLASSES = 4
STEP_ROWS = CLASSES * CLASS_ROWS


def sum_kernel(
    line, g_ref, small_in, main_ref, half_ref, small_out, G, RV, FIN, SR,
    sem_in, sem_out, s_up, s_down, r_up, r_fin, t_up, t_down, q_up, q_fin,
):
    blocks, D, _ = g_ref.shape
    per = D // STEP_ROWS
    steps = blocks * per
    dp = lax.axis_index("dp")
    s = lax.axis_index("section")
    y = lax.rem(dp, 2)
    z = dp // 2
    has_dn = z > 0
    has_up = z < line - 1
    side = (dp + 1 - 2 * y, s)
    below = (lax.rem(dp + 2 * line - 2, 2 * line), s)
    above = (lax.rem(dp + 2, 2 * line), s)
    peers = (side, below, above)

    def load(b):
        return pltpu.make_async_copy(g_ref.at[b], G.at[b], sem_in.at[b])

    def store_main(b):
        return pltpu.make_async_copy(
            FIN.at[b], main_ref.at[:, pl.ds(pl.multiple_of(b * D, D), D)], sem_out.at[b]
        )

    def store_half(b):
        return pltpu.make_async_copy(
            FIN.at[b], half_ref.at[pl.ds(pl.multiple_of((b - 4) * D, D), D)], sem_out.at[b]
        )

    for b in range(blocks):
        load(b).start()

    barrier = pltpu.get_barrier_semaphore()
    pl.semaphore_signal(barrier, inc=1, device_id=side, device_id_type=MESH)

    @pl.when(has_dn)
    def _():
        pl.semaphore_signal(barrier, inc=1, device_id=below, device_id_type=MESH)

    @pl.when(has_up)
    def _():
        pl.semaphore_signal(barrier, inc=1, device_id=above, device_id_type=MESH)

    pl.semaphore_wait(barrier, 1 + has_dn.astype(jnp.int32) + has_up.astype(jnp.int32))

    low_mid, high_mid = line // 2 - 1, line // 2

    def roles(kind):
        root_y = kind % 2
        k = (low_mid, high_mid)[root_y]
        away = jnp.abs(z - k) + (y != root_y).astype(jnp.int32)
        deep = max(k, line - 1 - k) + 1
        if kind < 2:
            rail = y == root_y
            return (
                (rail, rail & (z <= k) & has_dn, rail & (z >= k) & has_up),
                (jnp.logical_not(rail), rail & (z > k), rail & (z < k)),
                away, deep,
            )
        at = z == k
        return (
            (at & (y == root_y), (z <= k) & has_dn, (z >= k) & has_up),
            (at & (y != root_y), z > k, z < k),
            away, deep,
        )

    def rem_copy(src, dst, send, recv, dev):
        return pltpu.make_async_remote_copy(
            src_ref=src, dst_ref=dst, send_sem=send, recv_sem=recv, device_id=dev, device_id_type=MESH
        )

    slot_at_parent = (0, 2, 1)

    def tree(kids, parents, acc, slots, fin, sup, sdown, rup, rfin):
        root = jnp.logical_not(parents[0] | parents[1] | parents[2])

        def send_up(wait):
            for n in range(3):
                @pl.when(parents[n])
                def _():
                    m = slot_at_parent[n]
                    c = rem_copy(acc, slots(m), sup, rup(m), peers[n])
                    c.wait_send() if wait else c.start()

        def send_down(wait):
            for n in range(3):
                @pl.when(kids[n])
                def _():
                    c = rem_copy(fin, fin, sdown(n), rfin, peers[n])
                    c.wait_send() if wait else c.start()

        def up():
            for n in range(3):
                @pl.when(kids[n])
                def _():
                    rem_copy(slots(n), slots(n), sup, rup(n), peers[n]).wait_recv()
                    acc[...] = (acc[...].astype(F32) + slots(n)[...].astype(F32)).astype(acc.dtype)
            send_up(False)

            @pl.when(root)
            def _():
                fin[...] = acc[...]
                send_down(False)

        def down():
            @pl.when(jnp.logical_not(root))
            def _():
                rem_copy(acc, fin, sup, rfin, peers[0]).wait_recv()
                send_down(False)

        def drain():
            send_up(True)
            send_down(True)

        return up, down, drain

    def chunk(kind, i):
        b = i // per
        r = pl.ds(pl.multiple_of(lax.rem(i, per) * STEP_ROWS + kind * CLASS_ROWS, 16), CLASS_ROWS)
        kids, parents, _, _ = roles(kind)
        return tree(
            kids, parents, G.at[b, r], lambda n: RV.at[n, b, r], FIN.at[b, r],
            s_up.at[kind, i], lambda n: s_down.at[kind, n, i], lambda n: r_up.at[kind, n, i], r_fin.at[kind, i],
        )

    SR[3] = small_in[...]
    kids, parents, _, _ = roles(0)
    little = tree(
        kids, parents, SR.at[3], lambda n: SR.at[n], SR.at[4], t_up, lambda n: t_down.at[n], lambda n: q_up.at[n], q_fin
    )
    little[0]()
    deepest = max(roles(kind)[3] for kind in range(CLASSES))

    def step(t, c):
        @pl.when((lax.rem(t, per) == 0) & (t < steps))
        def _():
            load(t // per).wait()

        for kind in range(CLASSES):
            _, _, away, deep = roles(kind)
            i = t - (deep - away)

            @pl.when((i >= 0) & (i < steps))
            def _():
                chunk(kind, i)[0]()

        for kind in range(CLASSES):
            _, _, away, deep = roles(kind)
            i = t - deep - away

            @pl.when((i >= 0) & (i < steps))
            def _():
                chunk(kind, i)[1]()

        i = t - 2 * deepest

        @pl.when((i >= 0) & (lax.rem(i, per) == per - 1))
        def _():
            b = i // per

            @pl.when(b < 4)
            def _():
                store_main(b).start()

            @pl.when(b >= 4)
            def _():
                store_half(b).start()

        return c

    lax.fori_loop(0, steps + 2 * deepest, step, 0)
    little[1]()
    small_out[...] = SR[4]

    def drain(i, c):
        for kind in range(CLASSES):
            chunk(kind, i)[2]()
        return c

    lax.fori_loop(0, steps, drain, 0)
    little[2]()
    for b in range(blocks):
        (store_main(b) if b < 4 else store_half(b)).wait()


def sum_over_dp(grads, small):
    blocks, D, _ = grads.shape
    steps = blocks * D // STEP_ROWS
    line = lax.axis_size("dp") // 2
    dma = pltpu.SemaphoreType.DMA
    any_spec = pl.BlockSpec(memory_space=pl.ANY)
    vmem_spec = pl.BlockSpec(memory_space=pltpu.VMEM)
    return pl.pallas_call(
        partial(sum_kernel, line),
        name="sum_over_dp",
        out_shape=(
            jax.ShapeDtypeStruct((D, 4 * D), BF),
            jax.ShapeDtypeStruct((2 * D, D), BF),
            jax.ShapeDtypeStruct(small.shape, F32),
        ),
        in_specs=[any_spec, vmem_spec],
        out_specs=(any_spec, any_spec, vmem_spec),
        scratch_shapes=[
            pltpu.VMEM((blocks, D, D), BF),
            pltpu.VMEM((3, blocks, D, D), BF),
            pltpu.VMEM((blocks, D, D), BF),
            pltpu.VMEM((5,) + small.shape, F32),
            dma((blocks,)), dma((blocks,)),
            dma((CLASSES, steps)), dma((CLASSES, 3, steps)), dma((CLASSES, 3, steps)), dma((CLASSES, steps)),
            dma, dma((3,)), dma((3,)), dma,
        ],
        compiler_params=pltpu.CompilerParams(
            collective_id=1, has_side_effects=True, vmem_limit_bytes=60 * MIB
        ),
        cost_estimate=pl.CostEstimate(flops=10**7, bytes_accessed=30 * 10**6, transcendentals=0),
    )(grads, small)


def on_device(tokens, lengths, w_main, w_down_half, out_bias, ln_gain, ln_bias, cotangent):
    D = tokens.shape[-1]
    s = lax.axis_index("section")
    p = lax.rem(s, 2)
    vec = jnp.concatenate([out_bias, ln_gain, ln_bias, jnp.zeros((5, D), F32)], axis=0)
    kept_out, kept_grad, grads, small = run_layers(tokens, cotangent, lengths, w_main[0], w_down_half[0], vec)
    mine = lax.dynamic_index_in_dim(small, p, 0, keepdims=False)
    theirs = lax.dynamic_index_in_dim(small, 1 - p, 0, keepdims=False)
    pairs = [(i, i + 1 - 2 * (i % 2)) for i in range(lax.axis_size("section"))]
    small = mine + lax.ppermute(theirs, "section", pairs)
    grad_main, grad_half, small = sum_over_dp(grads, small)
    grad_main, grad_half = grad_main.astype(F32), grad_half.astype(F32)
    return (
        kept_out[None],
        kept_grad[None],
        grad_main[None],
        grad_half[None],
        small[0:1],
        small[1:2],
        small[2:3],
    )


def solution(mesh):
    in_specs = (
        P("dp", None, None),
        P("dp"),
        P("section", None, None),
        P("section", None, None),
        P("section", None),
        P("section", None),
        P("section", None),
        P("dp", None, None),
    )
    out_specs = (
        P("section", "dp", None, None),
        P("section", "dp", None, None),
        P("section", None, None),
        P("section", None, None),
        P("section", None),
        P("section", None),
        P("section", None),
    )
    return jax.shard_map(
        on_device, mesh=mesh, in_specs=in_specs, out_specs=out_specs, check_vma=False
    )
```

```python
from functools import partial

import jax
import jax.numpy as jnp
from jax import lax
from jax.experimental import pallas as pl
from jax.experimental.pallas import tpu as pltpu
from jax.sharding import PartitionSpec as P

HEAD = 64
NORM_EPS = 1e-06
MASK_FILL = -1000000000.0
MESH = pl.DeviceIdType.MESH
BF = jnp.bfloat16
F32 = jnp.float32
MIB = 1024 * 1024
NN = (((1,), (0,)), ((), ()))
NT = (((1,), (1,)), ((), ()))
TN = (((0,), (0,)), ((), ()))
LN_ROWS = 128
W_ORDER = (1, 2, 0, 3)


def mm(a, b, dims=NN):
    return lax.dot_general(a, b, dims, preferred_element_type=F32)


def gelu_pair(x):
    cdf = 0.5 * (1.0 + lax.erf(x * 0.7071067811865476))
    return x * cdf, cdf + x * (jnp.exp(x * x * -0.5) * 0.3989422804014327)


def layer_kernel(
    tok, cot, lens, wm, wd, vec,
    out_ref, ing_ref, g_ref, small_ref,
    W, W2, V, L, R, KV, N, RS, LSE, GIN, GOUT, RES, DCTX, DKV, DKVR, GR, GS, VR,
    sem_w, sem_tok, sem_cot, send_w, recv_w, send_kv, recv_kv, send_h, recv_h, sem_o, recv_o,
    send_dkv, recv_dkv, send_g, recv_g, sem_i, recv_i, send_gr, recv_gr, sem_go, send_v, recv_v,
):
    nq, seq_len, D = tok.shape
    half = seq_len // 2
    pairs = D // 128
    dp = lax.axis_index("dp")
    s = lax.axis_index("section")
    p = lax.rem(s, 2)
    layer = s // 2
    partner = (dp, s + 1 - 2 * p)
    across = (dp, lax.rem(s + 2, 4))
    first = layer == 0
    last = layer == 1
    own = pl.ds(pl.multiple_of(p * half, half), half)
    other = pl.ds(pl.multiple_of((1 - p) * half, half), half)

    def rows(q):
        return pl.ds(pl.multiple_of(q * half, half), half)

    def copy_w(b):
        return pltpu.make_async_copy(wm.at[:, pl.ds(b * D, D)], W.at[p, b], sem_w.at[b])

    def copy_w2(b):
        return pltpu.make_async_copy(wd.at[pl.ds(b * D, D), :], W2.at[2 * p + b], sem_w.at[4 + b])

    def copy_tok(q):
        return pltpu.make_async_copy(tok.at[q, own], L.at[0, rows(q)], sem_tok.at[q])

    def copy_cot(q):
        return pltpu.make_async_copy(cot.at[q, own], GIN.at[q], sem_cot.at[q])

    @pl.when(first)
    def _():
        for q in range(nq):
            copy_tok(q).start()

    for b in W_ORDER:
        copy_w(b).start()
    for b in range(2):
        copy_w2(b).start()

    @pl.when(last)
    def _():
        for q in range(nq):
            copy_cot(q).start()

    barrier = pltpu.get_barrier_semaphore()
    for peer in (partner, across):
        pl.semaphore_signal(barrier, inc=1, device_id=peer, device_id_type=MESH)
    pl.semaphore_wait(barrier, 2)

    def remote(src, dst, send, recv, dev):
        return pltpu.make_async_remote_copy(
            src_ref=src, dst_ref=dst, send_sem=send, recv_sem=recv, device_id=dev, device_id_type=MESH
        )

    def send_weights(b):
        return remote(wm.at[:, pl.ds(b * D, D)], W.at[p, b], send_w.at[b], recv_w.at[b], partner)

    def send_weights2(b):
        return remote(wd.at[pl.ds(b * D, D), :], W2.at[2 * p + b], send_w.at[4 + b], recv_w.at[4 + b], partner)

    def send_vec():
        return remote(vec, VR, send_v, recv_v, partner)

    send_vec().start()
    for b in W_ORDER:
        send_weights(b).start()
    for b in range(2):
        send_weights2(b).start()

    def need_w(sec, b):
        @pl.when(p == sec)
        def _():
            copy_w(b).wait()

        @pl.when(p != sec)
        def _():
            remote(wm.at[:, pl.ds(b * D, D)], W.at[1 - p, b], send_w.at[b], recv_w.at[b], partner).wait_recv()

    def need_w2():
        for b in range(2):
            copy_w2(b).wait()
            remote(
                wd.at[pl.ds(b * D, D), :], W2.at[2 * (1 - p) + b], send_w.at[4 + b], recv_w.at[4 + b], partner
            ).wait_recv()

    def send_keys(q, i):
        return remote(KV.at[q, i, own], KV.at[q, i, own], send_kv.at[q, i], recv_kv.at[q, i], partner)

    def take_keys(q, i):
        return remote(KV.at[q, i, other], KV.at[q, i, other], send_kv.at[q, i], recv_kv.at[q, i], partner)

    def hand_on(q):
        return remote(GOUT.at[q], L.at[0, rows(q)], send_h.at[q], recv_h.at[q], across)

    def hand_back(q):
        return remote(GOUT.at[q], GIN.at[q], send_g.at[q], recv_g.at[q], across)

    def put(src, dst_ref, q, sec, sems, recvs):
        keep = pltpu.make_async_copy(src, dst_ref.at[q, own], sems.at[sec, q])
        give = remote(src, dst_ref.at[q, own], sems.at[sec, q], recvs.at[q], partner)
        return keep, give

    def put_start(src, dst_ref, q, sec, sems, recvs):
        keep, give = put(src, dst_ref, q, sec, sems, recvs)

        @pl.when(p == sec)
        def _():
            keep.start()

        @pl.when(p != sec)
        def _():
            give.start()

    def put_wait(src, dst_ref, q, sec, sems, recvs):
        keep, give = put(src, dst_ref, q, sec, sems, recvs)

        @pl.when(p == sec)
        def _():
            keep.wait()
            remote(src, dst_ref.at[q, other], sems.at[sec, q], recvs.at[q], partner).wait_recv()

        @pl.when(p != sec)
        def _():
            give.wait_send()

    lane = lax.broadcasted_iota(jnp.int32, (1, 128), 1)
    low_lanes = (lane < HEAD).astype(F32)
    high_lanes = 1.0 - low_lanes

    def stack_heads(x):
        wide = x.astype(F32)
        return jnp.concatenate([(wide * low_lanes).astype(BF), (wide * high_lanes).astype(BF)], axis=0)

    def join_heads(x):
        return jnp.where(lane < HEAD, x[:half], x[half:])

    key_at = lax.broadcasted_iota(jnp.int32, (1, seq_len), 1)

    def norm_forward(sec, h_ref_at, dst, q):
        bias, gain, shift = V[sec, 0:1, :], V[sec, 1:2, :], V[sec, 2:3, :]

        def body(i, c):
            r = pl.ds(pl.multiple_of(i * LN_ROWS, LN_ROWS), LN_ROWS)
            rq = pl.ds(pl.multiple_of(q * half + i * LN_ROWS, LN_ROWS), LN_ROWS)
            residual = L[h_ref_at, rq, :].astype(F32) + (RES[r, :] + bias)
            center = jnp.mean(residual, axis=-1, keepdims=True)
            centred = residual - center
            spread = jnp.mean(centred * centred, axis=-1, keepdims=True)
            rstd = lax.rsqrt(spread + NORM_EPS)
            normed = centred * rstd
            N[sec, rq, :] = normed.astype(BF)
            RS[sec, rq, :] = jnp.broadcast_to(rstd, (LN_ROWS, 128))
            dst(r, rq, (normed * gain + shift).astype(BF))
            return c

        lax.fori_loop(0, half // LN_ROWS, body, 0)

    def norm_backward(sec, g_ref, at, q):
        gain = V[sec, 1:2, :]

        def body(i, c):
            r = pl.ds(pl.multiple_of(i * LN_ROWS, LN_ROWS), LN_ROWS)
            rq = pl.ds(pl.multiple_of(q * half + i * LN_ROWS, LN_ROWS), LN_ROWS)
            g = g_ref[q, r, :].astype(F32)
            normed = N[sec, rq, :].astype(F32)
            rstd = RS[sec, rq, 0:1]
            gg = g * gain
            first_mean = jnp.mean(gg, axis=-1, keepdims=True)
            second_mean = jnp.mean(gg * normed, axis=-1, keepdims=True)
            dres = rstd * (gg - first_mean - normed * second_mean)
            RES[r, :] = dres
            R[at, rq, :] = dres.astype(BF)
            b, a, t = c
            return (
                b + jnp.sum(dres, axis=0, keepdims=True),
                a + jnp.sum(g * normed, axis=0, keepdims=True),
                t + jnp.sum(g, axis=0, keepdims=True),
            )

        zero = jnp.zeros((1, D), F32)
        b, a, t = lax.fori_loop(0, half // LN_ROWS, body, (zero, zero, zero))
        small_ref[sec, 0:1, :] += b
        small_ref[sec, 1:2, :] += a
        small_ref[sec, 2:3, :] += t

    small_ref[...] = jnp.zeros_like(small_ref)

    def forward(q, carry):
        length = lens[q]

        @pl.when(first)
        def _():
            copy_tok(q).wait()

        @pl.when(last)
        def _():
            hand_on(q).wait_recv()

        @pl.when(q == 0)
        def _():
            need_w(0, 1)

        h = L[0, rows(q), :]
        KV[q, 0, own, :] = mm(h, W[0, 1]).astype(BF)
        send_keys(q, 0).start()

        @pl.when(q == 0)
        def _():
            need_w(0, 2)

        KV[q, 1, own, :] = mm(h, W[0, 2]).astype(BF)
        send_keys(q, 1).start()

        @pl.when(q == 0)
        def _():
            need_w(0, 0)

        R[0, rows(q), :] = (mm(h, W[0, 0]) * HEAD ** (-0.5)).astype(BF)
        take_keys(q, 0).wait_recv()
        take_keys(q, 1).wait_recv()
        valid = key_at < length

        for hp in range(pairs):
            cols = slice(hp * 128, (hp + 1) * 128)
            st = mm(stack_heads(R[0, rows(q), cols]), KV[q, 0, :, cols], NT)
            st = jnp.where(valid, st, MASK_FILL)
            top = jnp.max(st, axis=1, keepdims=True)
            e = jnp.exp(st - top)
            total = jnp.sum(e, axis=1, keepdims=True)
            ct = mm(e.astype(BF), KV[q, 1, :, cols]) * (1.0 / total)
            L[1, rows(q), cols] = join_heads(ct).astype(BF)
            lse = top + jnp.log(total)
            LSE[q, :, 2 * hp : 2 * hp + 1] = lse[:half]
            LSE[q, :, 2 * hp + 1 : 2 * hp + 2] = lse[half:]

        @pl.when(q == 0)
        def _():
            need_w(0, 3)
            send_vec().wait_recv()
            mine = vec[...]
            theirs = VR[...]

            @pl.when(p == 0)
            def _():
                V[0] = mine
                V[1] = theirs

            @pl.when(p == 1)
            def _():
                V[0] = theirs
                V[1] = mine

        RES[...] = mm(L[1, rows(q), :], W[0, 3])

        def keep_mid(r, rq, x):
            L[2, rq, :] = x

        norm_forward(0, 0, keep_mid, q)
        put_start(L.at[2, rows(q)], out_ref, q, 0, sem_o, recv_o)

        @pl.when(q == 0)
        def _():
            for b in range(4):
                need_w(1, b)

        for b in range(4):
            hidden, slope = gelu_pair(mm(L[2, rows(q), :], W[1, b]))
            L[3 + b, rows(q), :] = hidden.astype(BF)
            R[5 + b, rows(q), :] = slope.astype(BF)

        @pl.when(q == 0)
        def _():
            need_w2()

        for n in range(D // 256):
            c = slice(n * 256, (n + 1) * 256)
            acc = mm(L[3, rows(q), :], W2[0, :, c])
            for b in range(1, 4):
                acc += mm(L[3 + b, rows(q), :], W2[b, :, c])
            RES[:, c] = acc

        def keep_out(r, rq, x):
            GOUT[q, r, :] = x

        norm_forward(1, 2, keep_out, q)

        @pl.when(first)
        def _():
            hand_on(q).start()

        put_start(GOUT.at[q], out_ref, q, 1, sem_o, recv_o)
        return carry

    lax.fori_loop(0, nq, forward, 0)

    def send_dkeys(q):
        slot = lax.rem(q, 2)
        return remote(DKV.at[1 - p], DKVR.at[slot], send_dkv, recv_dkv.at[slot], partner)

    def backward(q, carry):
        length = lens[q]

        @pl.when(last)
        def _():
            copy_cot(q).wait()

        @pl.when(first)
        def _():
            hand_back(q).wait_recv()

        norm_backward(1, GIN, 4, q)

        for b in range(4):
            dh = mm(R[4, rows(q), :], W2[b], NT)
            R[5 + b, rows(q), :] = (dh * R[5 + b, rows(q), :].astype(F32)).astype(BF)

        for n in range(D // 256):
            c = slice(n * 256, (n + 1) * 256)
            acc = RES[:, c]
            for b in range(4):
                acc += mm(R[5 + b, rows(q), :], W[1, b, c, :], NT)
            GIN[q, :, c] = acc.astype(BF)
        put_start(GIN.at[q], ing_ref, q, 1, sem_i, recv_i)

        norm_backward(0, GIN, 3, q)
        DCTX[...] = mm(R[3, rows(q), :], W[0, 3], NT).astype(BF)

        @pl.when(q > 0)
        def _():
            send_dkeys(q - 1).wait_send()

        valid = key_at < length

        for hp in range(pairs):
            cols = slice(hp * 128, (hp + 1) * 128)
            kp = KV[q, 0, :, cols]
            qs = stack_heads(R[0, rows(q), cols])
            dcs = stack_heads(DCTX[:, cols])
            st = jnp.where(valid, mm(qs, kp, NT), MASK_FILL)
            lse = jnp.concatenate(
                [LSE[q, :, 2 * hp : 2 * hp + 1], LSE[q, :, 2 * hp + 1 : 2 * hp + 2]], axis=0
            )
            prob = jnp.exp(st - lse)
            dprob = mm(dcs, KV[q, 1, :, cols], NT)
            mean = jnp.sum(prob * dprob, axis=1, keepdims=True)
            ds = (prob * (dprob - mean)).astype(BF)
            R[0, rows(q), cols] = (join_heads(mm(ds, kp)) * HEAD ** (-0.5)).astype(BF)
            dk = jnp.transpose(mm(jnp.transpose(qs), ds)).astype(BF)
            dv = jnp.transpose(mm(jnp.transpose(dcs), prob.astype(BF))).astype(BF)
            DKV[0, 0, :, cols] = dk[:half]
            DKV[1, 0, :, cols] = dk[half:]
            DKV[0, 1, :, cols] = dv[:half]
            DKV[1, 1, :, cols] = dv[half:]

        send_dkeys(q).start()
        for n in range(D // 256):
            c = slice(n * 256, (n + 1) * 256)
            RES[:, c] = RES[:, c] + mm(R[0, rows(q), :], W[0, 0, c, :], NT)
        send_dkeys(q).wait_recv()
        slot = lax.rem(q, 2)
        for i in range(2):
            R[1 + i, rows(q), :] = (DKV[p, i].astype(F32) + DKVR[slot, i].astype(F32)).astype(BF)

        @pl.when(first)
        def _():
            hand_on(q).wait_send()

        put_wait(GOUT.at[q], out_ref, q, 1, sem_o, recv_o)
        put_wait(GIN.at[q], ing_ref, q, 1, sem_i, recv_i)
        for n in range(D // 256):
            c = slice(n * 256, (n + 1) * 256)
            acc = RES[:, c]
            for b in range(1, 3):
                acc += mm(R[b, rows(q), :], W[0, b, c, :], NT)
            GOUT[q, :, c] = acc.astype(BF)

        @pl.when(last)
        def _():
            hand_back(q).start()

        put_start(GOUT.at[q], ing_ref, q, 0, sem_i, recv_i)
        return carry

    lax.fori_loop(0, nq, backward, 0)

    left = ((0, 0, 0, 1, 3, 4), (2, 2, 2, 2, 5, 6))
    right = ((0, 1, 2, 3, 4, 4), (5, 6, 7, 8, 4, 4))

    def pick(table, sec, j):
        return table[0][j] + sec * (table[1][j] - table[0][j])

    def send_grad(j):
        return remote(GS.at[j % 2], GR.at[j], send_gr.at[j], recv_gr.at[j], partner)

    def store_grad(j):
        return pltpu.make_async_copy(GR.at[j], g_ref.at[j], sem_go.at[j])

    for j in range(6):
        li, ri = pick(left, 1 - p, j), pick(right, 1 - p, j)
        if j >= 2:
            send_grad(j - 2).wait_send()
        for n in range(D // 256):
            c = slice(n * 256, (n + 1) * 256)
            GS[j % 2, :, c] = mm(L[li], R[ri, :, c], TN).astype(BF)
        send_grad(j).start()
    for j in range(6):
        li, ri = pick(left, p, j), pick(right, p, j)
        send_grad(j).wait_recv()
        for n in range(D // 256):
            c = slice(n * 256, (n + 1) * 256)
            GR[j, :, c] = (mm(L[li], R[ri, :, c], TN) + GR[j, :, c].astype(F32)).astype(BF)
        store_grad(j).start()

    for j in range(4, 6):
        send_grad(j).wait_send()
    for j in range(6):
        store_grad(j).wait()
    send_vec().wait_send()
    for b in range(4):
        send_weights(b).wait_send()
    for b in range(2):
        send_weights2(b).wait_send()
    send_dkeys(nq - 1).wait_send()
    for q in range(nq):
        for i in range(2):
            send_keys(q, i).wait_send()

        @pl.when(last)
        def _():
            hand_back(q).wait_send()

        put_wait(L.at[2, rows(q)], out_ref, q, 0, sem_o, recv_o)
        put_wait(GOUT.at[q], ing_ref, q, 0, sem_i, recv_i)


def run_layers(tokens, cotangent, lengths, weights, w_down, vec):
    nq, seq_len, D = tokens.shape
    half = seq_len // 2
    tall = nq * half
    dma = pltpu.SemaphoreType.DMA
    any_spec = pl.BlockSpec(memory_space=pl.ANY)
    vmem_spec = pl.BlockSpec(memory_space=pltpu.VMEM)
    return pl.pallas_call(
        layer_kernel,
        name="layers",
        out_shape=(
            jax.ShapeDtypeStruct((nq, seq_len, D), BF),
            jax.ShapeDtypeStruct((nq, seq_len, D), BF),
            jax.ShapeDtypeStruct((6, D, D), BF),
            jax.ShapeDtypeStruct((2, 8, D), F32),
        ),
        in_specs=[any_spec, any_spec, pl.BlockSpec(memory_space=pltpu.SMEM), any_spec, any_spec, vmem_spec],
        out_specs=(any_spec, any_spec, any_spec, vmem_spec),
        scratch_shapes=[
            pltpu.VMEM((2, 4, D, D), BF),
            pltpu.VMEM((4, D, D), BF),
            pltpu.VMEM((2, 8, D), F32),
            pltpu.VMEM((7, tall, D), BF),
            pltpu.VMEM((9, tall, D), BF),
            pltpu.VMEM((nq, 2, seq_len, D), BF),
            pltpu.VMEM((2, tall, D), BF),
            pltpu.VMEM((2, tall, 128), F32),
            pltpu.VMEM((nq, half, 128), F32),
            pltpu.VMEM((nq, half, D), BF),
            pltpu.VMEM((nq, half, D), BF),
            pltpu.VMEM((half, D), F32),
            pltpu.VMEM((half, D), BF),
            pltpu.VMEM((2, 2, half, D), BF),
            pltpu.VMEM((2, 2, half, D), BF),
            pltpu.VMEM((6, D, D), BF),
            pltpu.VMEM((2, D, D), BF),
            pltpu.VMEM((8, D), F32),
            dma((6,)), dma((nq,)), dma((nq,)), dma((6,)), dma((6,)),
            dma((nq, 2)), dma((nq, 2)), dma((nq,)), dma((nq,)), dma((2, nq)), dma((nq,)),
            dma, dma((2,)), dma((nq,)), dma((nq,)), dma((2, nq)), dma((nq,)),
            dma((6,)), dma((6,)), dma((6,)), dma, dma,
        ],
        compiler_params=pltpu.CompilerParams(
            collective_id=0, has_side_effects=True, vmem_limit_bytes=63 * MIB
        ),
        cost_estimate=pl.CostEstimate(flops=60 * 10**9, bytes_accessed=40 * 10**6, transcendentals=10**7),
    )(tokens, cotangent, lengths, weights, w_down, vec)


CLASS_ROWS = 48
CLASSES = 4
STEP_ROWS = CLASSES * CLASS_ROWS


def sum_kernel(
    line, g_ref, small_in, main_ref, half_ref, small_out, G, RV, FIN, SR,
    sem_in, sem_out, s_up, s_down, r_up, r_fin, t_up, t_down, q_up, q_fin,
):
    blocks, D, _ = g_ref.shape
    per = D // STEP_ROWS
    steps = blocks * per
    dp = lax.axis_index("dp")
    s = lax.axis_index("section")
    y = lax.rem(dp, 2)
    z = dp // 2
    has_dn = z > 0
    has_up = z < line - 1
    side = (dp + 1 - 2 * y, s)
    below = (lax.rem(dp + 2 * line - 2, 2 * line), s)
    above = (lax.rem(dp + 2, 2 * line), s)
    peers = (side, below, above)

    def load(b):
        return pltpu.make_async_copy(g_ref.at[b], G.at[b], sem_in.at[b])

    def store_main(b):
        return pltpu.make_async_copy(
            FIN.at[b], main_ref.at[:, pl.ds(pl.multiple_of(b * D, D), D)], sem_out.at[b]
        )

    def store_half(b):
        return pltpu.make_async_copy(
            FIN.at[b], half_ref.at[pl.ds(pl.multiple_of((b - 4) * D, D), D)], sem_out.at[b]
        )

    for b in range(blocks):
        load(b).start()

    barrier = pltpu.get_barrier_semaphore()
    pl.semaphore_signal(barrier, inc=1, device_id=side, device_id_type=MESH)

    @pl.when(has_dn)
    def _():
        pl.semaphore_signal(barrier, inc=1, device_id=below, device_id_type=MESH)

    @pl.when(has_up)
    def _():
        pl.semaphore_signal(barrier, inc=1, device_id=above, device_id_type=MESH)

    pl.semaphore_wait(barrier, 1 + has_dn.astype(jnp.int32) + has_up.astype(jnp.int32))

    low_mid, high_mid = line // 2 - 1, line // 2

    def roles(kind):
        root_y = kind % 2
        k = (low_mid, high_mid)[root_y]
        away = jnp.abs(z - k) + (y != root_y).astype(jnp.int32)
        deep = max(k, line - 1 - k) + 1
        if kind < 2:
            rail = y == root_y
            return (
                (rail, rail & (z <= k) & has_dn, rail & (z >= k) & has_up),
                (jnp.logical_not(rail), rail & (z > k), rail & (z < k)),
                away, deep,
            )
        at = z == k
        return (
            (at & (y == root_y), (z <= k) & has_dn, (z >= k) & has_up),
            (at & (y != root_y), z > k, z < k),
            away, deep,
        )

    def rem_copy(src, dst, send, recv, dev):
        return pltpu.make_async_remote_copy(
            src_ref=src, dst_ref=dst, send_sem=send, recv_sem=recv, device_id=dev, device_id_type=MESH
        )

    slot_at_parent = (0, 2, 1)

    def tree(kids, parents, acc, slots, fin, sup, sdown, rup, rfin):
        root = jnp.logical_not(parents[0] | parents[1] | parents[2])

        def send_up(wait):
            for n in range(3):
                @pl.when(parents[n])
                def _():
                    m = slot_at_parent[n]
                    c = rem_copy(acc, slots(m), sup, rup(m), peers[n])
                    c.wait_send() if wait else c.start()

        def send_down(wait):
            for n in range(3):
                @pl.when(kids[n])
                def _():
                    c = rem_copy(fin, fin, sdown(n), rfin, peers[n])
                    c.wait_send() if wait else c.start()

        def up():
            for n in range(3):
                @pl.when(kids[n])
                def _():
                    rem_copy(slots(n), slots(n), sup, rup(n), peers[n]).wait_recv()
                    acc[...] = (acc[...].astype(F32) + slots(n)[...].astype(F32)).astype(acc.dtype)
            send_up(False)

            @pl.when(root)
            def _():
                fin[...] = acc[...]
                send_down(False)

        def down():
            @pl.when(jnp.logical_not(root))
            def _():
                rem_copy(acc, fin, sup, rfin, peers[0]).wait_recv()
                send_down(False)

        def drain():
            send_up(True)
            send_down(True)

        return up, down, drain

    def chunk(kind, i):
        b = i // per
        r = pl.ds(pl.multiple_of(lax.rem(i, per) * STEP_ROWS + kind * CLASS_ROWS, 16), CLASS_ROWS)
        kids, parents, _, _ = roles(kind)
        return tree(
            kids, parents, G.at[b, r], lambda n: RV.at[n, b, r], FIN.at[b, r],
            s_up.at[kind, i], lambda n: s_down.at[kind, n, i], lambda n: r_up.at[kind, n, i], r_fin.at[kind, i],
        )

    SR[3] = small_in[...]
    kids, parents, _, _ = roles(0)
    little = tree(
        kids, parents, SR.at[3], lambda n: SR.at[n], SR.at[4], t_up, lambda n: t_down.at[n], lambda n: q_up.at[n], q_fin
    )
    little[0]()
    deepest = max(roles(kind)[3] for kind in range(CLASSES))

    def step(t, c):
        @pl.when((lax.rem(t, per) == 0) & (t < steps))
        def _():
            load(t // per).wait()

        for kind in range(CLASSES):
            _, _, away, deep = roles(kind)
            i = t - (deep - away)

            @pl.when((i >= 0) & (i < steps))
            def _():
                chunk(kind, i)[0]()

        for kind in range(CLASSES):
            _, _, away, deep = roles(kind)
            i = t - deep - away

            @pl.when((i >= 0) & (i < steps))
            def _():
                chunk(kind, i)[1]()

        i = t - 2 * deepest

        @pl.when((i >= 0) & (lax.rem(i, per) == per - 1))
        def _():
            b = i // per

            @pl.when(b < 4)
            def _():
                store_main(b).start()

            @pl.when(b >= 4)
            def _():
                store_half(b).start()

        return c

    lax.fori_loop(0, steps + 2 * deepest, step, 0)
    little[1]()
    small_out[...] = SR[4]

    def drain(i, c):
        for kind in range(CLASSES):
            chunk(kind, i)[2]()
        return c

    lax.fori_loop(0, steps, drain, 0)
    little[2]()
    for b in range(blocks):
        (store_main(b) if b < 4 else store_half(b)).wait()


def sum_over_dp(grads, small):
    blocks, D, _ = grads.shape
    steps = blocks * D // STEP_ROWS
    line = lax.axis_size("dp") // 2
    dma = pltpu.SemaphoreType.DMA
    any_spec = pl.BlockSpec(memory_space=pl.ANY)
    vmem_spec = pl.BlockSpec(memory_space=pltpu.VMEM)
    return pl.pallas_call(
        partial(sum_kernel, line),
        name="sum_over_dp",
        out_shape=(
            jax.ShapeDtypeStruct((D, 4 * D), BF),
            jax.ShapeDtypeStruct((2 * D, D), BF),
            jax.ShapeDtypeStruct(small.shape, F32),
        ),
        in_specs=[any_spec, vmem_spec],
        out_specs=(any_spec, any_spec, vmem_spec),
        scratch_shapes=[
            pltpu.VMEM((blocks, D, D), BF),
            pltpu.VMEM((3, blocks, D, D), BF),
            pltpu.VMEM((blocks, D, D), BF),
            pltpu.VMEM((5,) + small.shape, F32),
            dma((blocks,)), dma((blocks,)),
            dma((CLASSES, steps)), dma((CLASSES, 3, steps)), dma((CLASSES, 3, steps)), dma((CLASSES, steps)),
            dma, dma((3,)), dma((3,)), dma,
        ],
        compiler_params=pltpu.CompilerParams(
            collective_id=1, has_side_effects=True, vmem_limit_bytes=60 * MIB
        ),
        cost_estimate=pl.CostEstimate(flops=10**7, bytes_accessed=30 * 10**6, transcendentals=0),
    )(grads, small)


def on_device(tokens, lengths, w_main, w_down_half, out_bias, ln_gain, ln_bias, cotangent):
    D = tokens.shape[-1]
    s = lax.axis_index("section")
    p = lax.rem(s, 2)
    vec = jnp.concatenate([out_bias, ln_gain, ln_bias, jnp.zeros((5, D), F32)], axis=0)
    kept_out, kept_grad, grads, small = run_layers(tokens, cotangent, lengths, w_main[0], w_down_half[0], vec)
    mine = lax.dynamic_index_in_dim(small, p, 0, keepdims=False)
    theirs = lax.dynamic_index_in_dim(small, 1 - p, 0, keepdims=False)
    pairs = [(i, i + 1 - 2 * (i % 2)) for i in range(lax.axis_size("section"))]
    small = mine + lax.ppermute(theirs, "section", pairs)
    grad_main, grad_half, small = sum_over_dp(grads, small)
    grad_main, grad_half = grad_main.astype(F32), grad_half.astype(F32)
    return (
        kept_out[None],
        kept_grad[None],
        grad_main[None],
        grad_half[None],
        small[0:1],
        small[1:2],
        small[2:3],
    )


def solution(mesh):
    in_specs = (
        P("dp", None, None),
        P("dp"),
        P("section", None, None),
        P("section", None, None),
        P("section", None),
        P("section", None),
        P("section", None),
        P("dp", None, None),
    )
    out_specs = (
        P("section", "dp", None, None),
        P("section", "dp", None, None),
        P("section", None, None),
        P("section", None, None),
        P("section", None),
        P("section", None),
        P("section", None),
    )
    return jax.shard_map(
        on_device, mesh=mesh, in_specs=in_specs, out_specs=out_specs, check_vma=False
    )
```

```python
from functools import partial

import jax
import jax.numpy as jnp
from jax import lax
from jax.experimental import pallas as pl
from jax.experimental.pallas import tpu as pltpu
from jax.sharding import PartitionSpec as P

HEAD = 64
NORM_EPS = 1e-06
MASK_FILL = -1000000000.0
MESH = pl.DeviceIdType.MESH
BF = jnp.bfloat16
F32 = jnp.float32
MIB = 1024 * 1024
NN = (((1,), (0,)), ((), ()))
NT = (((1,), (1,)), ((), ()))
TN = (((0,), (0,)), ((), ()))
LN_ROWS = 128
W_ORDER = (1, 2, 0, 3)
CLASSES = 4
CLASS_ROWS = 48
STEP_ROWS = CLASSES * CLASS_ROWS
UNITS = 7
HOP = 1
FINAL_AT = 3
FEED_PUMP = 3
PUMP = 1
FEED_AT = 0
DOWN_AT = 4


def mm(a, b, dims=NN):
    return lax.dot_general(a, b, dims, preferred_element_type=F32)


def gelu_pair(x):
    cdf = 0.5 * (1.0 + lax.erf(x * 0.7071067811865476))
    return x * cdf, cdf + x * (jnp.exp(x * x * -0.5) * 0.3989422804014327)


def layer_kernel(
    line, tok, cot, lens, wm, wd, vec,
    out_ref, ing_ref, main_ref, half_ref, small_out,
    BIG, AW, V, A, KV, N, LSE, GIN, GOUT, RES, DKV, DKVR, G, GP, VR, S, SP, SR,
    sem_w, sem_tok, sem_cot, send_w, recv_w, send_kv, recv_kv, send_h, recv_h, sem_o, recv_o,
    send_dkv, recv_dkv, send_g, recv_g, sem_i, recv_i, send_gr, recv_gr, sem_go, recv_go, send_v, recv_v,
    send_s, recv_s, s_up, s_down, r_up, r_fin, t_up, t_down, q_up, q_fin, free_sem, final_sem,
):
    nq, seq_len, D = tok.shape
    half = seq_len // 2
    pairs = D // 128
    spare = D // HEAD
    dp = lax.axis_index("dp")
    s = lax.axis_index("section")
    p = lax.rem(s, 2)
    layer = s // 2
    partner = (dp, s + 1 - 2 * p)
    across = (dp, lax.rem(s + 2, 4))
    first = layer == 0
    last = layer == 1
    wide = D // 2
    own_wide = pl.ds(pl.multiple_of(p * wide, 128), wide)
    other_wide = pl.ds(pl.multiple_of((1 - p) * wide, 128), wide)
    own = pl.ds(pl.multiple_of(p * half, half), half)
    other = pl.ds(pl.multiple_of((1 - p) * half, half), half)

    def down_rows(core, b):
        return pl.ds(pl.multiple_of((DOWN_AT + 2 * core + b) * D, 128), D)

    def main_place(sec, b):
        return AW.at[b] if sec == 0 else BIG.at[pl.ds((FEED_AT + b) * D, D)]

    def rows(q):
        return pl.ds(pl.multiple_of(q * half, half), half)

    def copy_w(sec, b):
        return pltpu.make_async_copy(wm.at[:, pl.ds(b * D, D)], main_place(sec, b), sem_w.at[b])

    def on_core(sec, act):
        pl.when(p == sec)(act)

    def copy_w2(b):
        return pltpu.make_async_copy(wd.at[pl.ds(b * D, D), :], BIG.at[down_rows(p, b)], sem_w.at[4 + b])

    def copy_tok(q):
        return pltpu.make_async_copy(tok.at[q, own], A.at[0, rows(q)], sem_tok.at[q])

    def copy_cot(q):
        return pltpu.make_async_copy(cot.at[q, own], GIN.at[q], sem_cot.at[q])

    @pl.when(first)
    def _():
        for q in range(nq):
            copy_tok(q).start()

    for b in W_ORDER:
        on_core(0, lambda: copy_w(0, b).start())
        on_core(1, lambda: copy_w(1, b).start())
    for b in range(2):
        copy_w2(b).start()

    @pl.when(last)
    def _():
        for q in range(nq):
            copy_cot(q).start()

    y = lax.rem(dp, 2)
    z = dp // 2
    has_dn = z > 0
    has_up = z < line - 1
    side = (dp + 1 - 2 * y, s)
    below = (lax.rem(dp + 2 * line - 2, 2 * line), s)
    above = (lax.rem(dp + 2, 2 * line), s)
    peers = (side, below, above)
    peer_count = 1 + has_dn.astype(jnp.int32) + has_up.astype(jnp.int32)

    def greet(sem):
        pl.semaphore_signal(sem, inc=1, device_id=side, device_id_type=MESH)

        @pl.when(has_dn)
        def _():
            pl.semaphore_signal(sem, inc=1, device_id=below, device_id_type=MESH)

        @pl.when(has_up)
        def _():
            pl.semaphore_signal(sem, inc=1, device_id=above, device_id_type=MESH)

    barrier = pltpu.get_barrier_semaphore()
    for peer in (partner, across):
        pl.semaphore_signal(barrier, inc=1, device_id=peer, device_id_type=MESH)
    greet(barrier)
    pl.semaphore_wait(barrier, 2 + peer_count)

    def remote(src, dst, send, recv, dev):
        return pltpu.make_async_remote_copy(
            src_ref=src, dst_ref=dst, send_sem=send, recv_sem=recv, device_id=dev, device_id_type=MESH
        )

    def send_weights(sec, b):
        return remote(wm.at[:, pl.ds(b * D, D)], main_place(sec, b), send_w.at[b], recv_w.at[b], partner)

    def send_weights2(b):
        return remote(wd.at[pl.ds(b * D, D), :], BIG.at[down_rows(p, b)], send_w.at[4 + b], recv_w.at[4 + b], partner)

    def send_vec():
        return remote(vec, VR, send_v, recv_v, partner)

    send_vec().start()
    for b in W_ORDER:
        on_core(0, lambda: send_weights(0, b).start())
        on_core(1, lambda: send_weights(1, b).start())
    for b in range(2):
        send_weights2(b).start()

    def need_w(sec, b):
        on_core(sec, lambda: copy_w(sec, b).wait())
        on_core(1 - sec, lambda: send_weights(sec, b).wait_recv())

    def need_w2():
        for b in range(2):
            copy_w2(b).wait()
            remote(
                wd.at[pl.ds(b * D, D), :], BIG.at[down_rows(1 - p, b)], send_w.at[4 + b], recv_w.at[4 + b], partner
            ).wait_recv()

    def send_keys(q, i):
        return remote(KV.at[q, i, own], KV.at[q, i, own], send_kv.at[q, i], recv_kv.at[q, i], partner)

    def take_keys(q, i):
        return remote(KV.at[q, i, other], KV.at[q, i, other], send_kv.at[q, i], recv_kv.at[q, i], partner)

    def hand_on(q):
        return remote(GOUT.at[q], A.at[0, rows(q)], send_h.at[q], recv_h.at[q], across)

    def hand_back(q):
        return remote(GOUT.at[q], GIN.at[q], send_g.at[q], recv_g.at[q], across)

    def put(src, dst_ref, q, sec, sems, recvs):
        keep = pltpu.make_async_copy(src, dst_ref.at[q, own], sems.at[sec, q])
        give = remote(src, dst_ref.at[q, own], sems.at[sec, q], recvs.at[q], partner)
        return keep, give

    def put_start(src, dst_ref, q, sec, sems, recvs):
        keep, give = put(src, dst_ref, q, sec, sems, recvs)

        @pl.when(p == sec)
        def _():
            keep.start()

        @pl.when(p != sec)
        def _():
            give.start()

    def put_wait(src, dst_ref, q, sec, sems, recvs):
        keep, give = put(src, dst_ref, q, sec, sems, recvs)

        @pl.when(p == sec)
        def _():
            keep.wait()
            remote(src, dst_ref.at[q, other], sems.at[sec, q], recvs.at[q], partner).wait_recv()

        @pl.when(p != sec)
        def _():
            give.wait_send()

    lane = lax.broadcasted_iota(jnp.int32, (1, 128), 1)
    low_lanes = (lane < HEAD).astype(F32)
    high_lanes = 1.0 - low_lanes

    def stack_heads(x):
        wide = x.astype(F32)
        return jnp.concatenate([(wide * low_lanes).astype(BF), (wide * high_lanes).astype(BF)], axis=0)

    def join_heads(x):
        return jnp.where(lane < HEAD, x[:half], x[half:])

    key_at = lax.broadcasted_iota(jnp.int32, (1, seq_len), 1)

    def norm_forward(sec, h_ref_at, dst, q):
        bias, gain, shift = V[sec, 0:1, :], V[sec, 1:2, :], V[sec, 2:3, :]

        def body(i, c):
            r = pl.ds(pl.multiple_of(i * LN_ROWS, LN_ROWS), LN_ROWS)
            rq = pl.ds(pl.multiple_of(q * half + i * LN_ROWS, LN_ROWS), LN_ROWS)
            residual = A[h_ref_at, rq, :].astype(F32) + (RES[r, :] + bias)
            center = jnp.mean(residual, axis=-1, keepdims=True)
            centred = residual - center
            spread = jnp.mean(centred * centred, axis=-1, keepdims=True)
            rstd = lax.rsqrt(spread + NORM_EPS)
            normed = centred * rstd
            N[sec, rq, :] = normed.astype(BF)
            LSE[q, r, spare + sec : spare + sec + 1] = rstd
            dst(r, rq, (normed * gain + shift).astype(BF))
            return c

        lax.fori_loop(0, half // LN_ROWS, body, 0)

    def norm_backward(sec, g_ref, at, q):
        gain = V[sec, 1:2, :]

        def body(i, c):
            r = pl.ds(pl.multiple_of(i * LN_ROWS, LN_ROWS), LN_ROWS)
            rq = pl.ds(pl.multiple_of(q * half + i * LN_ROWS, LN_ROWS), LN_ROWS)
            g = g_ref[q, r, :].astype(F32)
            normed = N[sec, rq, :].astype(F32)
            rstd = LSE[q, r, spare + sec : spare + sec + 1]
            gg = g * gain
            first_mean = jnp.mean(gg, axis=-1, keepdims=True)
            second_mean = jnp.mean(gg * normed, axis=-1, keepdims=True)
            dres = rstd * (gg - first_mean - normed * second_mean)
            RES[r, :] = dres
            A[at, rq, :] = dres.astype(BF)
            b, a, t = c
            return (
                b + jnp.sum(dres, axis=0, keepdims=True),
                a + jnp.sum(g * normed, axis=0, keepdims=True),
                t + jnp.sum(g, axis=0, keepdims=True),
            )

        zero = jnp.zeros((1, D), F32)
        b, a, t = lax.fori_loop(0, half // LN_ROWS, body, (zero, zero, zero))
        S[sec, 0:1, :] += b
        S[sec, 1:2, :] += a
        S[sec, 2:3, :] += t

    S[...] = jnp.zeros_like(S)

    def forward(q, carry):
        length = lens[q]

        @pl.when(first)
        def _():
            copy_tok(q).wait()

        @pl.when(last)
        def _():
            hand_on(q).wait_recv()

        @pl.when(q == 0)
        def _():
            need_w(0, 1)

        h = A[0, rows(q), :]
        KV[q, 0, own, :] = mm(h, AW[1]).astype(BF)
        send_keys(q, 0).start()

        @pl.when(q == 0)
        def _():
            need_w(0, 2)

        KV[q, 1, own, :] = mm(h, AW[2]).astype(BF)
        send_keys(q, 1).start()

        @pl.when(q == 0)
        def _():
            need_w(0, 0)

        A[12, rows(q), :] = (mm(h, AW[0]) * HEAD ** (-0.5)).astype(BF)
        take_keys(q, 0).wait_recv()
        take_keys(q, 1).wait_recv()
        valid = key_at < length

        for hp in range(pairs):
            cols = slice(hp * 128, (hp + 1) * 128)
            st = mm(stack_heads(A[12, rows(q), cols]), KV[q, 0, :, cols], NT)
            st = jnp.where(valid, st, MASK_FILL)
            top = jnp.max(st, axis=1, keepdims=True)
            e = jnp.exp(st - top)
            total = jnp.sum(e, axis=1, keepdims=True)
            ct = mm(e.astype(BF), KV[q, 1, :, cols]) * (1.0 / total)
            A[1, rows(q), cols] = join_heads(ct).astype(BF)
            lse = top + jnp.log(total)
            LSE[q, :, 2 * hp : 2 * hp + 1] = lse[:half]
            LSE[q, :, 2 * hp + 1 : 2 * hp + 2] = lse[half:]

        @pl.when(q == 0)
        def _():
            need_w(0, 3)
            send_vec().wait_recv()
            mine = vec[...]
            theirs = VR[...]

            @pl.when(p == 0)
            def _():
                V[0] = mine
                V[1] = theirs

            @pl.when(p == 1)
            def _():
                V[0] = theirs
                V[1] = mine

        RES[...] = mm(A[1, rows(q), :], AW[3])

        def keep_mid(r, rq, x):
            A[2, rq, :] = x

        norm_forward(0, 0, keep_mid, q)
        put_start(A.at[2, rows(q)], out_ref, q, 0, sem_o, recv_o)

        @pl.when(q == 0)
        def _():
            for b in range(4):
                need_w(1, b)

        for b in range(4):
            hidden, slope = gelu_pair(mm(A[2, rows(q), :], BIG[pl.ds((FEED_AT + b) * D, D), :]))
            A[3 + b, rows(q), :] = hidden.astype(BF)
            A[7 + b, rows(q), :] = slope.astype(BF)

        @pl.when(q == 0)
        def _():
            need_w2()

        for n in range(D // 256):
            c = slice(n * 256, (n + 1) * 256)
            acc = mm(A[3, rows(q), :], BIG[pl.ds((DOWN_AT + 0) * D, D), c])
            for b in range(1, 4):
                acc += mm(A[3 + b, rows(q), :], BIG[pl.ds((DOWN_AT + b) * D, D), c])
            RES[:, c] = acc

        def keep_out(r, rq, x):
            GOUT[q, r, :] = x

        norm_forward(1, 2, keep_out, q)

        @pl.when(first)
        def _():
            hand_on(q).start()

        put_start(GOUT.at[q], out_ref, q, 1, sem_o, recv_o)
        return carry

    lax.fori_loop(0, nq, forward, 0)

    per = wide // STEP_ROWS
    steps = 12 * per
    deep = line // 2 + 1
    low_mid = line // 2 - 1

    def roles(kind):
        root_y = lax.rem(kind, 2)
        k = low_mid + root_y
        at = z == k
        ours = y == root_y
        rung = kind >= 2
        along = rung | ours
        beside = at | (kind < 2)
        kids = (ours & beside, along & (z <= k) & has_dn, along & (z >= k) & has_up)
        to_side = jnp.logical_not(ours) & beside
        move = jnp.where(to_side, 1 - 2 * y, jnp.where(z > k, -2, 2))
        slot = jnp.where(to_side, 0, jnp.where(z > k, 2, 1))
        z_up = z + jnp.where(to_side, 0, jnp.where(z > k, -1, 1))
        away = jnp.abs(z - k) + 1 - ours.astype(jnp.int32)
        return k, kids, at & ours, (lax.rem(dp + move + 2 * line, 2 * line), s), slot, z_up, away

    def heap(kind, k, n, zz, i):
        spare = jnp.where((kind == 2) | (zz == low_mid), 6, 3)
        unit = jnp.where(kind < 2, n, jnp.where(zz == k, 3 + n, spare))
        flat = i * UNITS + unit
        return BIG.at[pl.ds(pl.multiple_of(flat * CLASS_ROWS, 16), CLASS_ROWS)]

    def part(kind, i):
        return G.at[i // per, pl.ds(pl.multiple_of(lax.rem(i, per) * STEP_ROWS + kind * CLASS_ROWS, 16), CLASS_ROWS)]

    def final_at(o, row, count):
        return A.at[FINAL_AT + o // 2, pl.ds(pl.multiple_of(lax.rem(o, 2) * wide + row, 16), count)]

    def final(kind, i):
        return final_at(i // per, lax.rem(i, per) * STEP_ROWS + kind * CLASS_ROWS, CLASS_ROWS)

    def send_down(kind, i, kids):
        for n in range(3):
            @pl.when(kids[n])
            def _():
                remote(final(kind, i), final(kind, i), s_down.at[kind, n], r_fin.at[kind, i], peers[n]).start()

    def up_chunk(kind, i):
        k, kids, root, parent, slot, z_up, _ = roles(kind)
        acc = part(kind, i)
        for n in range(3):
            @pl.when(kids[n])
            def _():
                got = heap(kind, k, n, z, i)
                remote(acc, got, s_up.at[kind], r_up.at[kind, n, i], peers[n]).wait_recv()
                acc[...] = (acc[...].astype(F32) + got[...].astype(F32)).astype(BF)

        @pl.when(root)
        def _():
            final(kind, i)[...] = acc[...]
            send_down(kind, i, kids)

        @pl.when(jnp.logical_not(root))
        def _():
            remote(acc, heap(kind, k, slot, z_up, i), s_up.at[kind], r_up.at[kind, slot, i], parent).start()

    def down_chunk(kind, i):
        _, kids, root, parent, _, _, _ = roles(kind)

        @pl.when(jnp.logical_not(root))
        def _():
            remote(final(kind, i), final(kind, i), s_up.at[kind], r_fin.at[kind, i], parent).wait_recv()
            send_down(kind, i, kids)

    def store(o, wait):
        owner = jnp.where((o < 4) | ((o >= 6) & (o < 8)), 1, 0)
        is_main = (o < 4) | (o >= 8)

        def place(core):
            cols = pl.ds(pl.multiple_of(lax.rem(o, 4) * D, D), D)
            main = main_ref.at[pl.ds(pl.multiple_of(core * wide, 128), wide), cols]
            down = half_ref.at[pl.ds(pl.multiple_of(lax.rem(o, 2) * D + core * wide, 128), wide)]
            return main, down

        for here, theirs, hit in zip(place(p), place(1 - p), (is_main, jnp.logical_not(is_main))):
            @pl.when(hit & (owner == p))
            def _():
                c = pltpu.make_async_copy(final_at(o, 0, wide), here, sem_go.at[o])
                if wait:
                    c.wait()
                    remote(final_at(o, 0, wide), theirs, sem_go.at[o], recv_go.at[o], partner).wait_recv()
                else:
                    c.start()

            @pl.when(hit & (owner != p))
            def _():
                c = remote(final_at(o, 0, wide), here, sem_go.at[o], recv_go.at[o], partner)
                c.wait_send() if wait else c.start()

    def sum_step(t):
        def ups(kind, c):
            i = t - HOP * (deep - roles(kind)[6])

            @pl.when((i >= 0) & (i < steps))
            def _():
                up_chunk(kind, i)

            return c

        def downs(kind, c):
            i = t - HOP * (deep + roles(kind)[6])

            @pl.when((i >= 0) & (i < steps))
            def _():
                down_chunk(kind, i)

            return c

        lax.fori_loop(0, CLASSES, ups, 0)
        lax.fori_loop(0, CLASSES, downs, 0)
        i = t - 2 * HOP * deep

        @pl.when((i >= 0) & (lax.rem(i, per) == per - 1))
        def _():
            store(i // per, False)

    def sum_steps(lo, hi):
        def one(t, c):
            sum_step(t)
            return c

        lax.fori_loop(lo, hi, one, 0)

    def pump(q, lo, hi):
        @pl.when((q == nq - 1) & first)
        def _():
            sum_steps(lo, hi)

    def stage(j):
        return DKV.at[pl.ds(pl.multiple_of(lax.rem(j, 2) * wide, 128), wide)]

    def send_grad(j):
        return remote(stage(j), GP.at[lax.rem(j, 2)], send_gr.at[lax.rem(j, 2)], recv_gr.at[lax.rem(j, 2)], partner)

    def take_grad(j):
        send_grad(j).wait_recv()
        G[j] = (G[j].astype(F32) + GP[lax.rem(j, 2)].astype(F32)).astype(BF)

    def weight_grads(lo, hi, after):
        def one(j, c):
            left = jnp.where(j < 4, 2, jnp.where(j < 8, j - 1, jnp.where(j < 11, 0, 1)))
            right = jnp.where(j < 4, 7 + j, jnp.where(j < 8, 11, j + 4))

            @pl.when(j >= lo + 2)
            def _():
                send_grad(j - 2).wait_send()

            stage(j)[...] = mm(A[left, :, other_wide], A[right], TN).astype(BF)

            @pl.when(j > lo)
            def _():
                take_grad(j - 1)

            send_grad(j).start()
            G[j] = mm(A[left, :, own_wide], A[right], TN).astype(BF)

            @pl.when(j > lo)
            def _():
                after(j - 1)

            return c

        lax.fori_loop(lo, hi, one, 0)
        take_grad(hi - 1)
        after(hi - 1)
        for j in (hi - 2, hi - 1):
            send_grad(j).wait_send()

    def feed_grads():
        greet(free_sem)

        def after(j):
            @pl.when(j == 0)
            def _():
                pl.semaphore_wait(free_sem, peer_count)

            sum_steps(FEED_PUMP * j // 8, FEED_PUMP * (j + 1) // 8)

        weight_grads(0, 8, after)
        greet(final_sem)
        pl.semaphore_wait(final_sem, peer_count)

    def send_small():
        return remote(S.at[1 - p], SP, send_s, recv_s, partner)

    def send_dkeys(q):
        slot = lax.rem(q, 2)
        theirs = pl.ds(pl.multiple_of((1 - p) * 2 * half, 128), 2 * half)
        return remote(DKV.at[theirs], DKVR.at[slot], send_dkv, recv_dkv.at[slot], partner)

    def backward(q, carry):
        length = lens[q]

        @pl.when(last)
        def _():
            copy_cot(q).wait()

        @pl.when(first)
        def _():
            hand_back(q).wait_recv()

        norm_backward(1, GIN, 11, q)

        for b in range(4):
            dh = mm(A[11, rows(q), :], BIG[pl.ds((DOWN_AT + b) * D, D), :], NT)
            A[7 + b, rows(q), :] = (dh * A[7 + b, rows(q), :].astype(F32)).astype(BF)

        for n in range(D // 256):
            c = slice(n * 256, (n + 1) * 256)
            acc = RES[:, c]
            for b in range(4):
                acc += mm(A[7 + b, rows(q), :], BIG[pl.ds((FEED_AT + b) * D + c.start, c.stop - c.start), :], NT)
            GIN[q, :, c] = acc.astype(BF)
        put_start(GIN.at[q], ing_ref, q, 1, sem_i, recv_i)

        @pl.when(q > 0)
        def _():
            send_dkeys(q - 1).wait_send()

        @pl.when((q == nq - 1) & first)
        def _():
            feed_grads()

        norm_backward(0, GIN, 15, q)

        @pl.when(q == nq - 1)
        def _():
            send_small().start()
        A[13, rows(q), :] = mm(A[15, rows(q), :], AW[3], NT).astype(BF)

        valid = key_at < length
        pump(q, FEED_PUMP + 0 * PUMP, FEED_PUMP + 1 * PUMP)

        for hp in range(pairs):
            if hp == pairs // 2:
                pump(q, FEED_PUMP + 1 * PUMP, FEED_PUMP + 2 * PUMP)
            cols = slice(hp * 128, (hp + 1) * 128)
            kp = KV[q, 0, :, cols]
            qs = stack_heads(A[12, rows(q), cols])
            dcs = stack_heads(A[13, rows(q), cols])
            st = jnp.where(valid, mm(qs, kp, NT), MASK_FILL)
            lse = jnp.concatenate(
                [LSE[q, :, 2 * hp : 2 * hp + 1], LSE[q, :, 2 * hp + 1 : 2 * hp + 2]], axis=0
            )
            prob = jnp.exp(st - lse)
            dprob = mm(dcs, KV[q, 1, :, cols], NT)
            mean = jnp.sum(prob * dprob, axis=1, keepdims=True)
            ds = (prob * (dprob - mean)).astype(BF)
            A[12, rows(q), cols] = (join_heads(mm(ds, kp)) * HEAD ** (-0.5)).astype(BF)
            dk = jnp.transpose(mm(jnp.transpose(qs), ds)).astype(BF)
            dv = jnp.transpose(mm(jnp.transpose(dcs), prob.astype(BF))).astype(BF)
            DKV[0:half, cols] = dk[:half]
            DKV[half : 2 * half, cols] = dv[:half]
            DKV[2 * half : 3 * half, cols] = dk[half:]
            DKV[3 * half : 4 * half, cols] = dv[half:]

        send_dkeys(q).start()
        pump(q, FEED_PUMP + 2 * PUMP, FEED_PUMP + 3 * PUMP)
        for n in range(D // 256):
            c = slice(n * 256, (n + 1) * 256)
            RES[:, c] = RES[:, c] + mm(A[12, rows(q), :], AW[0, c, :], NT)
        pump(q, FEED_PUMP + 3 * PUMP, FEED_PUMP + 4 * PUMP)
        send_dkeys(q).wait_recv()
        slot = lax.rem(q, 2)
        for i in range(2):
            mine = DKV[pl.ds(pl.multiple_of((2 * p + i) * half, half), half), :]
            A[13 + i, rows(q), :] = (mine.astype(F32) + DKVR[slot, i * half : (i + 1) * half].astype(F32)).astype(BF)

        @pl.when(first)
        def _():
            hand_on(q).wait_send()

        put_wait(GOUT.at[q], out_ref, q, 1, sem_o, recv_o)
        put_wait(GIN.at[q], ing_ref, q, 1, sem_i, recv_i)
        for n in range(D // 256):
            c = slice(n * 256, (n + 1) * 256)
            acc = RES[:, c]
            for b in range(1, 3):
                acc += mm(A[12 + b, rows(q), :], AW[b, c, :], NT)
            GOUT[q, :, c] = acc.astype(BF)

        @pl.when(last)
        def _():
            hand_back(q).start()

        put_start(GOUT.at[q], ing_ref, q, 0, sem_i, recv_i)
        pump(q, FEED_PUMP + 4 * PUMP, FEED_PUMP + 5 * PUMP)
        return carry

    lax.fori_loop(0, nq, backward, 0)

    send_dkeys(nq - 1).wait_send()

    @pl.when(last)
    def _():
        feed_grads()

    before = FEED_PUMP + jnp.where(first, 5 * PUMP, 0)
    weight_grads(8, 12, lambda j: sum_steps(before + (j - 8) * PUMP, before + (j - 7) * PUMP))

    send_small().wait_recv()
    SR[3] = S[p] + SP[...]
    _, kids, root, parent, slot, _, away = roles(jnp.int32(0))

    def small_down():
        for n in range(3):
            @pl.when(kids[n])
            def _():
                remote(SR.at[4], SR.at[4], t_down.at[n], q_fin, peers[n]).start()

    def small_up():
        for n in range(3):
            @pl.when(kids[n])
            def _():
                remote(SR.at[3], SR.at[n], t_up, q_up.at[n], peers[n]).wait_recv()
                SR[3] = SR[3] + SR[n]

        @pl.when(root)
        def _():
            SR[4] = SR[3]
            small_down()

        @pl.when(jnp.logical_not(root))
        def _():
            remote(SR.at[3], SR.at[slot], t_up, q_up.at[slot], parent).start()

    small_at = steps - HOP * deep

    def tail(t, c):
        sum_step(t)

        @pl.when(t == small_at + HOP * (deep - away))
        def _():
            small_up()

        @pl.when((t == small_at + HOP * (deep + away)) & jnp.logical_not(root))
        def _():
            remote(SR.at[3], SR.at[4], t_up, q_fin, parent).wait_recv()
            small_down()

        return c

    lax.fori_loop(before + 4 * PUMP, steps + 2 * HOP * deep, tail, 0)
    small_out[...] = SR[4]

    whole = G.at[pl.ds(0, 3)]
    for kind in range(CLASSES):
        _, kids_of, root_of, parent_of, _, _, _ = roles(jnp.int32(kind))

        @pl.when(jnp.logical_not(root_of))
        def _():
            remote(whole, whole, s_up.at[kind], r_fin.at[kind, 0], parent_of).wait_send()

        for n in range(3):
            @pl.when(kids_of[n])
            def _():
                remote(whole, whole, s_down.at[kind, n], r_fin.at[kind, 0], peers[n]).wait_send()

    @pl.when(jnp.logical_not(root))
    def _():
        remote(SR.at[3], SR.at[slot], t_up, q_up.at[slot], parent).wait_send()

    for n in range(3):
        @pl.when(kids[n])
        def _():
            remote(SR.at[4], SR.at[4], t_down.at[n], q_fin, peers[n]).wait_send()

    send_small().wait_send()

    for o in range(12):
        store(jnp.int32(o), True)
    send_vec().wait_send()
    for b in range(4):
        on_core(0, lambda: send_weights(0, b).wait_send())
        on_core(1, lambda: send_weights(1, b).wait_send())
    for b in range(2):
        send_weights2(b).wait_send()
    for q in range(nq):
        for i in range(2):
            send_keys(q, i).wait_send()

        @pl.when(last)
        def _():
            hand_back(q).wait_send()

        put_wait(A.at[2, rows(q)], out_ref, q, 0, sem_o, recv_o)
        put_wait(GOUT.at[q], ing_ref, q, 0, sem_i, recv_i)


def run_layers(tokens, cotangent, lengths, weights, w_down, vec):
    nq, seq_len, D = tokens.shape
    half = seq_len // 2
    tall = nq * half
    dma = pltpu.SemaphoreType.DMA
    any_spec = pl.BlockSpec(memory_space=pl.ANY)
    vmem_spec = pl.BlockSpec(memory_space=pltpu.VMEM)
    line = lax.axis_size("dp") // 2
    steps = 6 * D // STEP_ROWS
    return pl.pallas_call(
        partial(layer_kernel, line),
        name="layers",
        out_shape=(
            jax.ShapeDtypeStruct((nq, seq_len, D), BF),
            jax.ShapeDtypeStruct((nq, seq_len, D), BF),
            jax.ShapeDtypeStruct((D, 4 * D), BF),
            jax.ShapeDtypeStruct((2 * D, D), BF),
            jax.ShapeDtypeStruct((8, D), F32),
        ),
        in_specs=[any_spec, any_spec, pl.BlockSpec(memory_space=pltpu.SMEM), any_spec, any_spec, vmem_spec],
        out_specs=(any_spec, any_spec, any_spec, any_spec, vmem_spec),
        scratch_shapes=[
            pltpu.VMEM((max(8 * D, steps * UNITS * CLASS_ROWS), D), BF),
            pltpu.VMEM((4, D, D), BF),
            pltpu.VMEM((2, 8, D), F32),
            pltpu.VMEM((16, tall, D), BF),
            pltpu.VMEM((nq, 2, seq_len, D), BF),
            pltpu.VMEM((2, tall, D), BF),
            pltpu.VMEM((nq, half, 128), F32),
            pltpu.VMEM((nq, half, D), BF),
            pltpu.VMEM((nq, half, D), BF),
            pltpu.VMEM((half, D), F32),
            pltpu.VMEM((4 * half, D), BF),
            pltpu.VMEM((2, 2 * half, D), BF),
            pltpu.VMEM((12, D // 2, D), BF),
            pltpu.VMEM((2, D // 2, D), BF),
            pltpu.VMEM((8, D), F32),
            pltpu.VMEM((2, 8, D), F32),
            pltpu.VMEM((8, D), F32),
            pltpu.VMEM((5, 8, D), F32),
            dma((6,)), dma((nq,)), dma((nq,)), dma((6,)), dma((6,)),
            dma((nq, 2)), dma((nq, 2)), dma((nq,)), dma((nq,)), dma((2, nq)), dma((nq,)),
            dma, dma((2,)), dma((nq,)), dma((nq,)), dma((2, nq)), dma((nq,)),
            dma((2,)), dma((2,)), dma((12,)), dma((12,)), dma, dma,
            dma, dma, dma((CLASSES,)), dma((CLASSES, 3)), dma((CLASSES, 3, steps)), dma((CLASSES, steps)),
            dma, dma((3,)), dma((3,)), dma, pltpu.SemaphoreType.REGULAR, pltpu.SemaphoreType.REGULAR,
        ],
        compiler_params=pltpu.CompilerParams(
            collective_id=0, has_side_effects=True, vmem_limit_bytes=64 * MIB
        ),
        cost_estimate=pl.CostEstimate(flops=60 * 10**9, bytes_accessed=40 * 10**6, transcendentals=10**7),
    )(tokens, cotangent, lengths, weights, w_down, vec)


def on_device(tokens, lengths, w_main, w_down_half, out_bias, ln_gain, ln_bias, cotangent):
    D = tokens.shape[-1]
    vec = jnp.concatenate([out_bias, ln_gain, ln_bias, jnp.zeros((5, D), F32)], axis=0)
    kept_out, kept_grad, grad_main, grad_half, small = run_layers(
        tokens, cotangent, lengths, w_main[0], w_down_half[0], vec
    )
    grad_main, grad_half = grad_main.astype(F32), grad_half.astype(F32)
    return (
        kept_out[None],
        kept_grad[None],
        grad_main[None],
        grad_half[None],
        small[0:1],
        small[1:2],
        small[2:3],
    )


def solution(mesh):
    in_specs = (
        P("dp", None, None),
        P("dp"),
        P("section", None, None),
        P("section", None, None),
        P("section", None),
        P("section", None),
        P("section", None),
        P("dp", None, None),
    )
    out_specs = (
        P("section", "dp", None, None),
        P("section", "dp", None, None),
        P("section", None, None),
        P("section", None, None),
        P("section", None),
        P("section", None),
        P("section", None),
    )
    return jax.shard_map(
        on_device, mesh=mesh, in_specs=in_specs, out_specs=out_specs, check_vma=False
    )
```

```python
from functools import partial

import jax
import jax.numpy as jnp
from jax import lax
from jax.experimental import pallas as pl
from jax.experimental.pallas import tpu as pltpu
from jax.sharding import PartitionSpec as P

HEAD = 64
NORM_EPS = 1e-06
MASK_FILL = -1000000000.0
MESH = pl.DeviceIdType.MESH
BF = jnp.bfloat16
F32 = jnp.float32
MIB = 1024 * 1024
NN = (((1,), (0,)), ((), ()))
NT = (((1,), (1,)), ((), ()))
TN = (((0,), (0,)), ((), ()))
LN_ROWS = 128
W_ORDER = (1, 2, 0, 3)
FIRST = (slice(0, 256), slice(256, 768))
LAST = (slice(0, 512), slice(512, 768))
CLASSES = 4
CLASS_ROWS = 48
STEP_ROWS = CLASSES * CLASS_ROWS
UNITS = 7
HOP = 1
FINAL_AT = 3
FEED_PUMP = 3
PUMP = 1
FEED_AT = 0
DOWN_AT = 4


def mm(a, b, dims=NN):
    return lax.dot_general(a, b, dims, preferred_element_type=F32)


def gelu_pair(x):
    cdf = 0.5 * (1.0 + lax.erf(x * 0.7071067811865476))
    return x * cdf, cdf + x * (jnp.exp(x * x * -0.5) * 0.3989422804014327)


def layer_kernel(
    line, tok, cot, lens, wm, wd, bias_in, gain_in, shift_in,
    out_ref, ing_ref, main_ref, half_ref, small_out,
    BIG, AW, V, A, KV, N, LSE, GIN, GOUT, RES, DKV, DKVR, G, GP, S, SP, SR,
    sem_w, sem_tok, sem_cot, send_w, recv_w, send_kv, recv_kv, send_h, recv_h, sem_o, recv_o,
    send_dkv, recv_dkv, send_g, recv_g, sem_i, recv_i, send_gr, recv_gr, sem_go, recv_go, send_v, recv_v,
    send_s, recv_s, s_up, s_down, r_up, r_fin, t_up, t_down, q_up, q_fin, free_sem, final_sem,
):
    nq, seq_len, D = tok.shape
    half = seq_len // 2
    pairs = D // 128
    spare = D // HEAD
    dp = lax.axis_index("dp")
    s = lax.axis_index("section")
    p = lax.rem(s, 2)
    layer = s // 2
    partner = (dp, s + 1 - 2 * p)
    across = (dp, lax.rem(s + 2, 4))
    first = layer == 0
    last = layer == 1
    wide = D // 2
    own_wide = pl.ds(pl.multiple_of(p * wide, 128), wide)
    other_wide = pl.ds(pl.multiple_of((1 - p) * wide, 128), wide)
    own = pl.ds(pl.multiple_of(p * half, half), half)
    other = pl.ds(pl.multiple_of((1 - p) * half, half), half)

    def down_rows(core, b):
        return pl.ds(pl.multiple_of((DOWN_AT + 2 * core + b) * D, 128), D)

    def main_place(sec, b):
        return AW.at[b] if sec == 0 else BIG.at[pl.ds((FEED_AT + b) * D, D)]

    def rows(q):
        return pl.ds(pl.multiple_of(q * half, half), half)

    def copy_w(sec, b):
        return pltpu.make_async_copy(wm.at[:, pl.ds(b * D, D)], main_place(sec, b), sem_w.at[b])

    def on_core(sec, act):
        pl.when(p == sec)(act)

    def copy_w2(b):
        return pltpu.make_async_copy(wd.at[pl.ds(b * D, D), :], BIG.at[down_rows(p, b)], sem_w.at[4 + b])

    def copy_tok(q):
        return pltpu.make_async_copy(tok.at[q, own], A.at[0, rows(q)], sem_tok.at[q])

    def copy_cot(q):
        return pltpu.make_async_copy(cot.at[q, own], GIN.at[q], sem_cot.at[q])

    @pl.when(first)
    def _():
        for q in range(nq):
            copy_tok(q).start()

    for b in W_ORDER:
        on_core(0, lambda: copy_w(0, b).start())
        on_core(1, lambda: copy_w(1, b).start())
    for b in range(2):
        copy_w2(b).start()

    @pl.when(last)
    def _():
        for q in range(nq):
            copy_cot(q).start()

    y = lax.rem(dp, 2)
    z = dp // 2
    has_dn = z > 0
    has_up = z < line - 1
    side = (dp + 1 - 2 * y, s)
    below = (lax.rem(dp + 2 * line - 2, 2 * line), s)
    above = (lax.rem(dp + 2, 2 * line), s)
    peers = (side, below, above)
    peer_count = 1 + has_dn.astype(jnp.int32) + has_up.astype(jnp.int32)

    def greet(sem):
        pl.semaphore_signal(sem, inc=1, device_id=side, device_id_type=MESH)

        @pl.when(has_dn)
        def _():
            pl.semaphore_signal(sem, inc=1, device_id=below, device_id_type=MESH)

        @pl.when(has_up)
        def _():
            pl.semaphore_signal(sem, inc=1, device_id=above, device_id_type=MESH)

    barrier = pltpu.get_barrier_semaphore()
    for peer in (partner, across):
        pl.semaphore_signal(barrier, inc=1, device_id=peer, device_id_type=MESH)
    greet(barrier)
    pl.semaphore_wait(barrier, 2 + peer_count)

    def remote(src, dst, send, recv, dev):
        return pltpu.make_async_remote_copy(
            src_ref=src, dst_ref=dst, send_sem=send, recv_sem=recv, device_id=dev, device_id_type=MESH
        )

    def send_weights(sec, b):
        return remote(wm.at[:, pl.ds(b * D, D)], main_place(sec, b), send_w.at[b], recv_w.at[b], partner)

    def send_weights2(b):
        return remote(wd.at[pl.ds(b * D, D), :], BIG.at[down_rows(p, b)], send_w.at[4 + b], recv_w.at[4 + b], partner)

    def send_vec():
        return remote(V.at[p], V.at[p], send_v, recv_v, partner)

    V[p] = jnp.concatenate([bias_in[...], gain_in[...], shift_in[...], jnp.zeros((5, D), F32)], axis=0)
    send_vec().start()
    for b in range(4):
        on_core(1, lambda: send_weights(1, b).start())
    for b in W_ORDER[:2]:
        on_core(0, lambda: send_weights(0, b).start())

    def send_later():
        for b in W_ORDER[:2]:
            on_core(0, lambda: send_weights(0, b).wait_send())
        for b in W_ORDER[2:]:
            on_core(0, lambda: send_weights(0, b).start())
        for b in range(2):
            send_weights2(b).start()

    def need_w(sec, b):
        on_core(sec, lambda: copy_w(sec, b).wait())
        on_core(1 - sec, lambda: send_weights(sec, b).wait_recv())

    def need_w2():
        for b in range(2):
            copy_w2(b).wait()
            remote(
                wd.at[pl.ds(b * D, D), :], BIG.at[down_rows(1 - p, b)], send_w.at[4 + b], recv_w.at[4 + b], partner
            ).wait_recv()

    def send_keys(q, i, group):
        here = KV.at[q, i, own, FIRST[group]]
        return remote(here, here, send_kv.at[q, i, group], recv_kv.at[q, i, group], partner)

    def take_keys(q, i, group):
        here = KV.at[q, i, other, FIRST[group]]
        return remote(here, here, send_kv.at[q, i, group], recv_kv.at[q, i, group], partner)

    def hand_on(q):
        return remote(GOUT.at[q], A.at[0, rows(q)], send_h.at[q], recv_h.at[q], across)

    def hand_back(q):
        return remote(GOUT.at[q], GIN.at[q], send_g.at[q], recv_g.at[q], across)

    def put(src, dst_ref, q, sec, sems, recvs):
        keep = pltpu.make_async_copy(src, dst_ref.at[q, own], sems.at[sec, q])
        give = remote(src, dst_ref.at[q, own], sems.at[sec, q], recvs.at[q], partner)
        return keep, give

    def put_start(src, dst_ref, q, sec, sems, recvs):
        keep, give = put(src, dst_ref, q, sec, sems, recvs)

        @pl.when(p == sec)
        def _():
            keep.start()

        @pl.when(p != sec)
        def _():
            give.start()

    def put_wait(src, dst_ref, q, sec, sems, recvs):
        keep, give = put(src, dst_ref, q, sec, sems, recvs)

        @pl.when(p == sec)
        def _():
            keep.wait()
            remote(src, dst_ref.at[q, other], sems.at[sec, q], recvs.at[q], partner).wait_recv()

        @pl.when(p != sec)
        def _():
            give.wait_send()

    lane = lax.broadcasted_iota(jnp.int32, (1, 128), 1)
    low_lanes = (lane < HEAD).astype(F32)
    high_lanes = 1.0 - low_lanes

    def stack_heads(x):
        wide = x.astype(F32)
        return jnp.concatenate([(wide * low_lanes).astype(BF), (wide * high_lanes).astype(BF)], axis=0)

    def join_heads(x):
        return jnp.where(lane < HEAD, x[:half], x[half:])

    key_at = lax.broadcasted_iota(jnp.int32, (1, seq_len), 1)

    def norm_forward(sec, h_ref_at, dst, q):
        bias, gain, shift = V[sec, 0:1, :], V[sec, 1:2, :], V[sec, 2:3, :]

        def body(i, c):
            r = pl.ds(pl.multiple_of(i * LN_ROWS, LN_ROWS), LN_ROWS)
            rq = pl.ds(pl.multiple_of(q * half + i * LN_ROWS, LN_ROWS), LN_ROWS)
            residual = A[h_ref_at, rq, :].astype(F32) + (RES[r, :] + bias)
            center = jnp.mean(residual, axis=-1, keepdims=True)
            centred = residual - center
            spread = jnp.mean(centred * centred, axis=-1, keepdims=True)
            rstd = lax.rsqrt(spread + NORM_EPS)
            normed = centred * rstd
            N[sec, rq, :] = normed.astype(BF)
            LSE[q, r, spare + sec : spare + sec + 1] = rstd
            dst(r, rq, (normed * gain + shift).astype(BF))
            return c

        lax.fori_loop(0, half // LN_ROWS, body, 0)

    def norm_backward(sec, g_ref, at, q):
        gain = V[sec, 1:2, :]

        def body(i, c):
            r = pl.ds(pl.multiple_of(i * LN_ROWS, LN_ROWS), LN_ROWS)
            rq = pl.ds(pl.multiple_of(q * half + i * LN_ROWS, LN_ROWS), LN_ROWS)
            g = g_ref[q, r, :].astype(F32)
            normed = N[sec, rq, :].astype(F32)
            rstd = LSE[q, r, spare + sec : spare + sec + 1]
            gg = g * gain
            first_mean = jnp.mean(gg, axis=-1, keepdims=True)
            second_mean = jnp.mean(gg * normed, axis=-1, keepdims=True)
            dres = rstd * (gg - first_mean - normed * second_mean)
            RES[r, :] = dres
            A[at, rq, :] = dres.astype(BF)
            b, a, t = c
            return (
                b + jnp.sum(dres, axis=0, keepdims=True),
                a + jnp.sum(g * normed, axis=0, keepdims=True),
                t + jnp.sum(g, axis=0, keepdims=True),
            )

        zero = jnp.zeros((1, D), F32)
        b, a, t = lax.fori_loop(0, half // LN_ROWS, body, (zero, zero, zero))
        S[sec, 0:1, :] += b
        S[sec, 1:2, :] += a
        S[sec, 2:3, :] += t

    S[...] = jnp.zeros_like(S)

    def forward(q, carry):
        length = lens[q]

        @pl.when(first)
        def _():
            copy_tok(q).wait()

        @pl.when(last)
        def _():
            hand_on(q).wait_recv()

        @pl.when(q == 0)
        def _():
            need_w(0, 1)
            need_w(0, 2)

        h = A[0, rows(q), :]
        for group, cols in enumerate(FIRST):
            for i in range(2):
                KV[q, i, own, cols] = mm(h, AW[1 + i, :, cols]).astype(BF)
                send_keys(q, i, group).start()

        @pl.when(q == 0)
        def _():
            send_later()
            need_w(0, 0)

        A[12, rows(q), :] = (mm(h, AW[0]) * HEAD ** (-0.5)).astype(BF)
        valid = key_at < length

        for hp in range(pairs):
            cols = slice(hp * 128, (hp + 1) * 128)
            for group in range(2):
                if FIRST[group].start == cols.start:
                    for i in range(2):
                        take_keys(q, i, group).wait_recv()
            st = mm(stack_heads(A[12, rows(q), cols]), KV[q, 0, :, cols], NT)
            st = jnp.where(valid, st, MASK_FILL)
            top = jnp.max(st, axis=1, keepdims=True)
            e = jnp.exp(st - top)
            total = jnp.sum(e, axis=1, keepdims=True)
            ct = mm(e.astype(BF), KV[q, 1, :, cols]) * (1.0 / total)
            A[1, rows(q), cols] = join_heads(ct).astype(BF)
            lse = top + jnp.log(total)
            LSE[q, :, 2 * hp : 2 * hp + 1] = lse[:half]
            LSE[q, :, 2 * hp + 1 : 2 * hp + 2] = lse[half:]

        @pl.when(q == 0)
        def _():
            need_w(0, 3)
            remote(V.at[1 - p], V.at[1 - p], send_v, recv_v, partner).wait_recv()

        RES[...] = mm(A[1, rows(q), :], AW[3])

        def keep_mid(r, rq, x):
            A[2, rq, :] = x

        norm_forward(0, 0, keep_mid, q)
        put_start(A.at[2, rows(q)], out_ref, q, 0, sem_o, recv_o)

        @pl.when(q == 0)
        def _():
            for b in range(4):
                need_w(1, b)

        for b in range(4):
            hidden, slope = gelu_pair(mm(A[2, rows(q), :], BIG[pl.ds((FEED_AT + b) * D, D), :]))
            A[3 + b, rows(q), :] = hidden.astype(BF)
            A[7 + b, rows(q), :] = slope.astype(BF)

        @pl.when(q == 0)
        def _():
            need_w2()

        for n in range(D // 256):
            c = slice(n * 256, (n + 1) * 256)
            acc = mm(A[3, rows(q), :], BIG[pl.ds((DOWN_AT + 0) * D, D), c])
            for b in range(1, 4):
                acc += mm(A[3 + b, rows(q), :], BIG[pl.ds((DOWN_AT + b) * D, D), c])
            RES[:, c] = acc

        def keep_out(r, rq, x):
            GOUT[q, r, :] = x

        norm_forward(1, 2, keep_out, q)

        @pl.when(first)
        def _():
            hand_on(q).start()

        put_start(GOUT.at[q], out_ref, q, 1, sem_o, recv_o)
        return carry

    lax.fori_loop(0, nq, forward, 0)

    per = wide // STEP_ROWS
    steps = 12 * per
    deep = line // 2 + 1
    low_mid = line // 2 - 1

    def roles(kind):
        root_y = lax.rem(kind, 2)
        k = low_mid + root_y
        at = z == k
        ours = y == root_y
        rung = kind >= 2
        along = rung | ours
        beside = at | (kind < 2)
        kids = (ours & beside, along & (z <= k) & has_dn, along & (z >= k) & has_up)
        to_side = jnp.logical_not(ours) & beside
        move = jnp.where(to_side, 1 - 2 * y, jnp.where(z > k, -2, 2))
        slot = jnp.where(to_side, 0, jnp.where(z > k, 2, 1))
        z_up = z + jnp.where(to_side, 0, jnp.where(z > k, -1, 1))
        away = jnp.abs(z - k) + 1 - ours.astype(jnp.int32)
        return k, kids, at & ours, (lax.rem(dp + move + 2 * line, 2 * line), s), slot, z_up, away

    def heap(kind, k, n, zz, i):
        spare = jnp.where((kind == 2) | (zz == low_mid), 6, 3)
        unit = jnp.where(kind < 2, n, jnp.where(zz == k, 3 + n, spare))
        flat = i * UNITS + unit
        return BIG.at[pl.ds(pl.multiple_of(flat * CLASS_ROWS, 16), CLASS_ROWS)]

    def part(kind, i):
        return G.at[i // per, pl.ds(pl.multiple_of(lax.rem(i, per) * STEP_ROWS + kind * CLASS_ROWS, 16), CLASS_ROWS)]

    def final_at(o, row, count):
        return A.at[FINAL_AT + o // 2, pl.ds(pl.multiple_of(lax.rem(o, 2) * wide + row, 16), count)]

    def final(kind, i):
        return final_at(i // per, lax.rem(i, per) * STEP_ROWS + kind * CLASS_ROWS, CLASS_ROWS)

    def send_down(kind, i, kids):
        for n in range(3):
            @pl.when(kids[n])
            def _():
                remote(final(kind, i), final(kind, i), s_down.at[kind, n], r_fin.at[kind, i], peers[n]).start()

    def up_chunk(kind, i):
        k, kids, root, parent, slot, z_up, _ = roles(kind)
        acc = part(kind, i)
        for n in range(3):
            @pl.when(kids[n])
            def _():
                got = heap(kind, k, n, z, i)
                remote(acc, got, s_up.at[kind], r_up.at[kind, n, i], peers[n]).wait_recv()
                acc[...] = (acc[...].astype(F32) + got[...].astype(F32)).astype(BF)

        @pl.when(root)
        def _():
            final(kind, i)[...] = acc[...]
            send_down(kind, i, kids)

        @pl.when(jnp.logical_not(root))
        def _():
            remote(acc, heap(kind, k, slot, z_up, i), s_up.at[kind], r_up.at[kind, slot, i], parent).start()

    def down_chunk(kind, i):
        _, kids, root, parent, _, _, _ = roles(kind)

        @pl.when(jnp.logical_not(root))
        def _():
            remote(final(kind, i), final(kind, i), s_up.at[kind], r_fin.at[kind, i], parent).wait_recv()
            send_down(kind, i, kids)

    def store(o, wait):
        owner = jnp.where((o < 4) | ((o >= 6) & (o < 8)), 1, 0)
        is_main = (o < 4) | (o >= 8)

        def place(core):
            cols = pl.ds(pl.multiple_of(lax.rem(o, 4) * D, D), D)
            main = main_ref.at[pl.ds(pl.multiple_of(core * wide, 128), wide), cols]
            down = half_ref.at[pl.ds(pl.multiple_of(lax.rem(o, 2) * D + core * wide, 128), wide)]
            return main, down

        for here, theirs, hit in zip(place(p), place(1 - p), (is_main, jnp.logical_not(is_main))):
            @pl.when(hit & (owner == p))
            def _():
                c = pltpu.make_async_copy(final_at(o, 0, wide), here, sem_go.at[o])
                if wait:
                    c.wait()
                    remote(final_at(o, 0, wide), theirs, sem_go.at[o], recv_go.at[o], partner).wait_recv()
                else:
                    c.start()

            @pl.when(hit & (owner != p))
            def _():
                c = remote(final_at(o, 0, wide), here, sem_go.at[o], recv_go.at[o], partner)
                c.wait_send() if wait else c.start()

    def sum_step(t):
        def ups(kind, c):
            i = t - HOP * (deep - roles(kind)[6])

            @pl.when((i >= 0) & (i < steps))
            def _():
                up_chunk(kind, i)

            return c

        def downs(kind, c):
            i = t - HOP * (deep + roles(kind)[6])

            @pl.when((i >= 0) & (i < steps))
            def _():
                down_chunk(kind, i)

            return c

        lax.fori_loop(0, CLASSES, ups, 0)
        lax.fori_loop(0, CLASSES, downs, 0)
        i = t - 2 * HOP * deep

        @pl.when((i >= 0) & (lax.rem(i, per) == per - 1))
        def _():
            store(i // per, False)

    def sum_steps(lo, hi):
        def one(t, c):
            sum_step(t)
            return c

        lax.fori_loop(lo, hi, one, 0)

    def pump(q, lo, hi):
        @pl.when((q == nq - 1) & first)
        def _():
            sum_steps(lo, hi)

    def stage(j):
        return DKV.at[pl.ds(pl.multiple_of(lax.rem(j, 2) * wide, 128), wide)]

    def send_grad(j):
        return remote(stage(j), GP.at[lax.rem(j, 2)], send_gr.at[lax.rem(j, 2)], recv_gr.at[lax.rem(j, 2)], partner)

    def take_grad(j):
        send_grad(j).wait_recv()
        G[j] = (G[j].astype(F32) + GP[lax.rem(j, 2)].astype(F32)).astype(BF)

    def weight_grads(lo, hi, after):
        def one(j, c):
            left = jnp.where(j < 4, 2, jnp.where(j < 8, j - 1, jnp.where(j < 11, 0, 1)))
            right = jnp.where(j < 4, 7 + j, jnp.where(j < 8, 11, j + 4))

            @pl.when(j >= lo + 2)
            def _():
                send_grad(j - 2).wait_send()

            stage(j)[...] = mm(A[left, :, other_wide], A[right], TN).astype(BF)

            @pl.when(j > lo)
            def _():
                take_grad(j - 1)

            send_grad(j).start()
            G[j] = mm(A[left, :, own_wide], A[right], TN).astype(BF)

            @pl.when(j > lo)
            def _():
                after(j - 1)

            return c

        lax.fori_loop(lo, hi, one, 0)
        take_grad(hi - 1)
        after(hi - 1)
        for j in (hi - 2, hi - 1):
            send_grad(j).wait_send()

    def feed_grads():
        greet(free_sem)

        def after(j):
            @pl.when(j == 0)
            def _():
                pl.semaphore_wait(free_sem, peer_count)

            sum_steps((FEED_PUMP * j + 7) // 8, (FEED_PUMP * (j + 1) + 7) // 8)

        weight_grads(0, 8, after)
        greet(final_sem)
        pl.semaphore_wait(final_sem, peer_count)

    def send_small():
        return remote(S.at[1 - p], SP, send_s, recv_s, partner)

    def send_dkeys(q, group):
        slot = lax.rem(q, 2)
        theirs = pl.ds(pl.multiple_of((1 - p) * 2 * half, 128), 2 * half)
        return remote(
            DKV.at[theirs, LAST[group]], DKVR.at[slot, :, LAST[group]],
            send_dkv.at[group], recv_dkv.at[slot, group], partner,
        )

    def backward(q, carry):
        length = lens[q]

        @pl.when(last)
        def _():
            copy_cot(q).wait()

        @pl.when(first)
        def _():
            hand_back(q).wait_recv()

        norm_backward(1, GIN, 11, q)

        for b in range(4):
            dh = mm(A[11, rows(q), :], BIG[pl.ds((DOWN_AT + b) * D, D), :], NT)
            A[7 + b, rows(q), :] = (dh * A[7 + b, rows(q), :].astype(F32)).astype(BF)

        for n in range(D // 256):
            c = slice(n * 256, (n + 1) * 256)
            acc = RES[:, c]
            for b in range(4):
                acc += mm(A[7 + b, rows(q), :], BIG[pl.ds((FEED_AT + b) * D + c.start, c.stop - c.start), :], NT)
            GIN[q, :, c] = acc.astype(BF)
        put_start(GIN.at[q], ing_ref, q, 1, sem_i, recv_i)

        @pl.when(q > 0)
        def _():
            for group in range(2):
                send_dkeys(q - 1, group).wait_send()

        @pl.when((q == nq - 1) & first)
        def _():
            feed_grads()

        norm_backward(0, GIN, 15, q)

        @pl.when(q == nq - 1)
        def _():
            send_small().start()
        A[13, rows(q), :] = mm(A[15, rows(q), :], AW[3], NT).astype(BF)

        valid = key_at < length
        pump(q, FEED_PUMP + 0 * PUMP, FEED_PUMP + 1 * PUMP)

        for hp in range(pairs):
            if LAST[1].start == hp * 128:
                send_dkeys(q, 0).start()
                pump(q, FEED_PUMP + 1 * PUMP, FEED_PUMP + 2 * PUMP)
            cols = slice(hp * 128, (hp + 1) * 128)
            kp = KV[q, 0, :, cols]
            qs = stack_heads(A[12, rows(q), cols])
            dcs = stack_heads(A[13, rows(q), cols])
            st = jnp.where(valid, mm(qs, kp, NT), MASK_FILL)
            lse = jnp.concatenate(
                [LSE[q, :, 2 * hp : 2 * hp + 1], LSE[q, :, 2 * hp + 1 : 2 * hp + 2]], axis=0
            )
            prob = jnp.exp(st - lse)
            dprob = mm(dcs, KV[q, 1, :, cols], NT)
            mean = jnp.sum(prob * dprob, axis=1, keepdims=True)
            ds = (prob * (dprob - mean)).astype(BF)
            A[12, rows(q), cols] = (join_heads(mm(ds, kp)) * HEAD ** (-0.5)).astype(BF)
            dk = jnp.transpose(mm(jnp.transpose(qs), ds)).astype(BF)
            dv = jnp.transpose(mm(jnp.transpose(dcs), prob.astype(BF))).astype(BF)
            DKV[0:half, cols] = dk[:half]
            DKV[half : 2 * half, cols] = dv[:half]
            DKV[2 * half : 3 * half, cols] = dk[half:]
            DKV[3 * half : 4 * half, cols] = dv[half:]

        send_dkeys(q, 1).start()
        pump(q, FEED_PUMP + 2 * PUMP, FEED_PUMP + 3 * PUMP)
        for n in range(D // 256):
            c = slice(n * 256, (n + 1) * 256)
            RES[:, c] = RES[:, c] + mm(A[12, rows(q), :], AW[0, c, :], NT)
        pump(q, FEED_PUMP + 3 * PUMP, FEED_PUMP + 4 * PUMP)
        for group in range(2):
            send_dkeys(q, group).wait_recv()
        slot = lax.rem(q, 2)
        for i in range(2):
            mine = DKV[pl.ds(pl.multiple_of((2 * p + i) * half, half), half), :]
            A[13 + i, rows(q), :] = (mine.astype(F32) + DKVR[slot, i * half : (i + 1) * half].astype(F32)).astype(BF)

        @pl.when(first)
        def _():
            hand_on(q).wait_send()

        put_wait(GOUT.at[q], out_ref, q, 1, sem_o, recv_o)
        put_wait(GIN.at[q], ing_ref, q, 1, sem_i, recv_i)
        for n in range(D // 256):
            c = slice(n * 256, (n + 1) * 256)
            acc = RES[:, c]
            for b in range(1, 3):
                acc += mm(A[12 + b, rows(q), :], AW[b, c, :], NT)
            GOUT[q, :, c] = acc.astype(BF)

        @pl.when(last)
        def _():
            hand_back(q).start()

        put_start(GOUT.at[q], ing_ref, q, 0, sem_i, recv_i)
        pump(q, FEED_PUMP + 4 * PUMP, FEED_PUMP + 5 * PUMP)
        return carry

    lax.fori_loop(0, nq, backward, 0)

    for group in range(2):
        send_dkeys(nq - 1, group).wait_send()

    @pl.when(last)
    def _():
        feed_grads()

    before = FEED_PUMP + jnp.where(first, 5 * PUMP, 0)
    weight_grads(8, 12, lambda j: sum_steps(before + (j - 8) * PUMP, before + (j - 7) * PUMP))

    send_small().wait_recv()
    SR[3] = S[p] + SP[...]
    _, kids, root, parent, slot, _, away = roles(jnp.int32(0))

    def small_down():
        for n in range(3):
            @pl.when(kids[n])
            def _():
                remote(SR.at[4], SR.at[4], t_down.at[n], q_fin, peers[n]).start()

    def small_up():
        for n in range(3):
            @pl.when(kids[n])
            def _():
                remote(SR.at[3], SR.at[n], t_up, q_up.at[n], peers[n]).wait_recv()
                SR[3] = SR[3] + SR[n]

        @pl.when(root)
        def _():
            SR[4] = SR[3]
            small_down()

        @pl.when(jnp.logical_not(root))
        def _():
            remote(SR.at[3], SR.at[slot], t_up, q_up.at[slot], parent).start()

    small_at = steps - HOP * deep

    def tail(t, c):
        sum_step(t)

        @pl.when(t == small_at + HOP * (deep - away))
        def _():
            small_up()

        @pl.when((t == small_at + HOP * (deep + away)) & jnp.logical_not(root))
        def _():
            remote(SR.at[3], SR.at[4], t_up, q_fin, parent).wait_recv()
            small_down()

        return c

    lax.fori_loop(before + 4 * PUMP, steps + 2 * HOP * deep, tail, 0)
    small_out[...] = SR[4]

    whole = G.at[pl.ds(0, 3)]
    for kind in range(CLASSES):
        _, kids_of, root_of, parent_of, _, _, _ = roles(jnp.int32(kind))

        @pl.when(jnp.logical_not(root_of))
        def _():
            remote(whole, whole, s_up.at[kind], r_fin.at[kind, 0], parent_of).wait_send()

        for n in range(3):
            @pl.when(kids_of[n])
            def _():
                remote(whole, whole, s_down.at[kind, n], r_fin.at[kind, 0], peers[n]).wait_send()

    @pl.when(jnp.logical_not(root))
    def _():
        remote(SR.at[3], SR.at[slot], t_up, q_up.at[slot], parent).wait_send()

    for n in range(3):
        @pl.when(kids[n])
        def _():
            remote(SR.at[4], SR.at[4], t_down.at[n], q_fin, peers[n]).wait_send()

    send_small().wait_send()

    for o in range(12):
        store(jnp.int32(o), True)
    send_vec().wait_send()
    for b in range(4):
        on_core(1, lambda: send_weights(1, b).wait_send())
    for b in W_ORDER[2:]:
        on_core(0, lambda: send_weights(0, b).wait_send())
    for b in range(2):
        send_weights2(b).wait_send()
    for q in range(nq):
        for i in range(2):
            for group in range(2):
                send_keys(q, i, group).wait_send()

        @pl.when(last)
        def _():
            hand_back(q).wait_send()

        put_wait(A.at[2, rows(q)], out_ref, q, 0, sem_o, recv_o)
        put_wait(GOUT.at[q], ing_ref, q, 0, sem_i, recv_i)


def run_layers(tokens, cotangent, lengths, weights, w_down, *rows):
    nq, seq_len, D = tokens.shape
    half = seq_len // 2
    tall = nq * half
    dma = pltpu.SemaphoreType.DMA
    any_spec = pl.BlockSpec(memory_space=pl.ANY)
    vmem_spec = pl.BlockSpec(memory_space=pltpu.VMEM)
    line = lax.axis_size("dp") // 2
    steps = 6 * D // STEP_ROWS
    return pl.pallas_call(
        partial(layer_kernel, line),
        name="layers",
        out_shape=(
            jax.ShapeDtypeStruct((nq, seq_len, D), BF),
            jax.ShapeDtypeStruct((nq, seq_len, D), BF),
            jax.ShapeDtypeStruct((D, 4 * D), BF),
            jax.ShapeDtypeStruct((2 * D, D), BF),
            jax.ShapeDtypeStruct((8, D), F32),
        ),
        in_specs=[any_spec, any_spec, pl.BlockSpec(memory_space=pltpu.SMEM), any_spec, any_spec] + [vmem_spec] * 3,
        out_specs=(any_spec, any_spec, any_spec, any_spec, vmem_spec),
        scratch_shapes=[
            pltpu.VMEM((max(8 * D, steps * UNITS * CLASS_ROWS), D), BF),
            pltpu.VMEM((4, D, D), BF),
            pltpu.VMEM((2, 8, D), F32),
            pltpu.VMEM((16, tall, D), BF),
            pltpu.VMEM((nq, 2, seq_len, D), BF),
            pltpu.VMEM((2, tall, D), BF),
            pltpu.VMEM((nq, half, 128), F32),
            pltpu.VMEM((nq, half, D), BF),
            pltpu.VMEM((nq, half, D), BF),
            pltpu.VMEM((half, D), F32),
            pltpu.VMEM((4 * half, D), BF),
            pltpu.VMEM((2, 2 * half, D), BF),
            pltpu.VMEM((12, D // 2, D), BF),
            pltpu.VMEM((2, D // 2, D), BF),
            pltpu.VMEM((2, 8, D), F32),
            pltpu.VMEM((8, D), F32),
            pltpu.VMEM((5, 8, D), F32),
            dma((6,)), dma((nq,)), dma((nq,)), dma((6,)), dma((6,)),
            dma((nq, 2, 2)), dma((nq, 2, 2)), dma((nq,)), dma((nq,)), dma((2, nq)), dma((nq,)),
            dma((2,)), dma((2, 2)), dma((nq,)), dma((nq,)), dma((2, nq)), dma((nq,)),
            dma((2,)), dma((2,)), dma((12,)), dma((12,)), dma, dma,
            dma, dma, dma((CLASSES,)), dma((CLASSES, 3)), dma((CLASSES, 3, steps)), dma((CLASSES, steps)),
            dma, dma((3,)), dma((3,)), dma, pltpu.SemaphoreType.REGULAR, pltpu.SemaphoreType.REGULAR,
        ],
        compiler_params=pltpu.CompilerParams(
            collective_id=0, has_side_effects=True, vmem_limit_bytes=64 * MIB
        ),
        cost_estimate=pl.CostEstimate(flops=60 * 10**9, bytes_accessed=40 * 10**6, transcendentals=10**7),
    )(tokens, cotangent, lengths, weights, w_down, *rows)


def result_kernel(out_in, grad_in, main_in, half_in, small_in, out, grad, main, down, bias, gain, shift):
    out[...] = out_in[...]
    grad[...] = grad_in[...]
    main[...] = main_in[...].astype(F32)
    down[...] = half_in[...].astype(F32)
    bias[...] = small_in[0:1, :]
    gain[...] = small_in[1:2, :]
    shift[...] = small_in[2:3, :]


RESULT_STEPS = 8


def results(*arrays):
    types = (BF, BF, F32, F32)

    def rows_of(a):
        return pl.BlockSpec((a.shape[0] // RESULT_STEPS, a.shape[1]), lambda i: (i, 0))

    def whole(a, rows):
        return pl.BlockSpec((rows, a.shape[1]), lambda i: (0, 0))

    small = arrays[4]
    return pl.pallas_call(
        result_kernel,
        name="results",
        grid=(RESULT_STEPS,),
        out_shape=tuple(jax.ShapeDtypeStruct(a.shape, t) for a, t in zip(arrays[:4], types))
        + tuple(jax.ShapeDtypeStruct((1, small.shape[1]), F32) for _ in range(3)),
        in_specs=[rows_of(a) for a in arrays[:4]] + [whole(small, 8)],
        out_specs=tuple(rows_of(a) for a in arrays[:4]) + tuple(whole(small, 1) for _ in range(3)),
        compiler_params=pltpu.CompilerParams(vmem_limit_bytes=63 * MIB),
    )(*arrays)


def on_device(tokens, lengths, w_main, w_down_half, out_bias, ln_gain, ln_bias, cotangent):
    nq, seq_len, D = tokens.shape
    kept_out, kept_grad, grad_main, grad_half, small = run_layers(
        tokens, cotangent, lengths, w_main[0], w_down_half[0], out_bias, ln_gain, ln_bias
    )
    tall = nq * seq_len
    kept_out, kept_grad, grad_main, grad_half, bias, gain, shift = results(
        kept_out.reshape(tall, D), kept_grad.reshape(tall, D), grad_main, grad_half, small
    )
    return (
        kept_out.reshape(1, nq, seq_len, D),
        kept_grad.reshape(1, nq, seq_len, D),
        grad_main[None],
        grad_half[None],
        bias,
        gain,
        shift,
    )


def solution(mesh):
    in_specs = (
        P("dp", None, None),
        P("dp"),
        P("section", None, None),
        P("section", None, None),
        P("section", None),
        P("section", None),
        P("section", None),
        P("dp", None, None),
    )
    out_specs = (
        P("section", "dp", None, None),
        P("section", "dp", None, None),
        P("section", None, None),
        P("section", None, None),
        P("section", None),
        P("section", None),
        P("section", None),
    )
    return jax.shard_map(
        on_device, mesh=mesh, in_specs=in_specs, out_specs=out_specs, check_vma=False
    )
```

```python
from functools import partial

import jax
import jax.numpy as jnp
from jax import lax
from jax.experimental import pallas as pl
from jax.experimental.pallas import tpu as pltpu
from jax.sharding import PartitionSpec as P

HEAD = 64
NORM_EPS = 1e-06
MASK_FILL = -1000000000.0
MESH = pl.DeviceIdType.MESH
BF = jnp.bfloat16
F32 = jnp.float32
MIB = 1024 * 1024
NN = (((1,), (0,)), ((), ()))
NT = (((1,), (1,)), ((), ()))
TN = (((0,), (0,)), ((), ()))
LN_ROWS = 128
W_ORDER = (1, 2, 0, 3)
FIRST = (slice(0, 256), slice(256, 768))
LAST = (slice(0, 512), slice(512, 768))
CLASSES = 4
CLASS_ROWS = 48
STEP_ROWS = CLASSES * CLASS_ROWS
UNITS = 7
GUEST = 10
HOP = 1
FINAL_AT = 3
FEED_PUMP = 3
PUMP = 1
FEED_AT = 0
DOWN_AT = 4


def mm(a, b, dims=NN):
    return lax.dot_general(a, b, dims, preferred_element_type=F32)


def gelu_pair(x):
    cdf = 0.5 * (1.0 + lax.erf(x * 0.7071067811865476))
    return x * cdf, cdf + x * (jnp.exp(x * x * -0.5) * 0.3989422804014327)


def layer_kernel(
    line, tok, cot, lens, wm, wd, bias_in, gain_in, shift_in,
    out_ref, ing_ref, main_ref, half_ref, small_out,
    BIG, AW, V, A, KV, N, LSE, GIN, GOUT, RES, DKV, DKVR, G, GP, S, SP, SR,
    sem_w, sem_tok, sem_cot, send_w, recv_w, send_kv, recv_kv, send_h, recv_h, sem_o, recv_o,
    send_dkv, recv_dkv, send_g, recv_g, sem_i, recv_i, send_gr, recv_gr, sem_go, recv_go, send_v, recv_v,
    send_s, recv_s, s_up, s_down, r_up, r_fin, t_up, t_down, q_up, q_fin, free_sem, final_sem, send_lend, recv_lend, send_back, recv_back,
):
    nq, seq_len, D = tok.shape
    half = seq_len // 2
    pairs = D // 128
    spare = D // HEAD
    dp = lax.axis_index("dp")
    s = lax.axis_index("section")
    p = lax.rem(s, 2)
    layer = s // 2
    partner = (dp, s + 1 - 2 * p)
    across = (dp, lax.rem(s + 2, 4))
    first = layer == 0
    last = layer == 1
    wide = D // 2
    own_wide = pl.ds(pl.multiple_of(p * wide, 128), wide)
    other_wide = pl.ds(pl.multiple_of((1 - p) * wide, 128), wide)
    own = pl.ds(pl.multiple_of(p * half, half), half)
    other = pl.ds(pl.multiple_of((1 - p) * half, half), half)

    def down_rows(core, b):
        return pl.ds(pl.multiple_of((DOWN_AT + 2 * core + b) * D, 128), D)

    def main_place(sec, b):
        return AW.at[b] if sec == 0 else BIG.at[pl.ds((FEED_AT + b) * D, D)]

    def rows(q):
        return pl.ds(pl.multiple_of(q * half, half), half)

    def copy_w(sec, b):
        return pltpu.make_async_copy(wm.at[:, pl.ds(b * D, D)], main_place(sec, b), sem_w.at[b])

    def on_core(sec, act):
        pl.when(p == sec)(act)

    def copy_w2(b):
        return pltpu.make_async_copy(wd.at[pl.ds(b * D, D), :], BIG.at[down_rows(p, b)], sem_w.at[4 + b])

    def copy_tok(q):
        return pltpu.make_async_copy(tok.at[q, own], A.at[0, rows(q)], sem_tok.at[q])

    def copy_cot(q):
        return pltpu.make_async_copy(cot.at[q, own], GIN.at[q], sem_cot.at[q])

    @pl.when(first)
    def _():
        for q in range(nq):
            copy_tok(q).start()

    for b in W_ORDER:
        on_core(0, lambda: copy_w(0, b).start())
        on_core(1, lambda: copy_w(1, b).start())
    for b in range(2):
        copy_w2(b).start()

    @pl.when(last)
    def _():
        for q in range(nq):
            copy_cot(q).start()

    y = lax.rem(dp, 2)
    z = dp // 2
    has_dn = z > 0
    has_up = z < line - 1
    side = (dp + 1 - 2 * y, s)
    below = (lax.rem(dp + 2 * line - 2, 2 * line), s)
    above = (lax.rem(dp + 2, 2 * line), s)
    peers = (side, below, above)
    peer_count = 1 + has_dn.astype(jnp.int32) + has_up.astype(jnp.int32)

    def greet(sem):
        pl.semaphore_signal(sem, inc=1, device_id=side, device_id_type=MESH)

        @pl.when(has_dn)
        def _():
            pl.semaphore_signal(sem, inc=1, device_id=below, device_id_type=MESH)

        @pl.when(has_up)
        def _():
            pl.semaphore_signal(sem, inc=1, device_id=above, device_id_type=MESH)

    barrier = pltpu.get_barrier_semaphore()
    for peer in (partner, across):
        pl.semaphore_signal(barrier, inc=1, device_id=peer, device_id_type=MESH)
    greet(barrier)
    pl.semaphore_wait(barrier, 2 + peer_count)

    def remote(src, dst, send, recv, dev):
        return pltpu.make_async_remote_copy(
            src_ref=src, dst_ref=dst, send_sem=send, recv_sem=recv, device_id=dev, device_id_type=MESH
        )

    def send_weights(sec, b):
        return remote(wm.at[:, pl.ds(b * D, D)], main_place(sec, b), send_w.at[b], recv_w.at[b], partner)

    def send_weights2(b):
        return remote(wd.at[pl.ds(b * D, D), :], BIG.at[down_rows(p, b)], send_w.at[4 + b], recv_w.at[4 + b], partner)

    def send_vec():
        return remote(V.at[p], V.at[p], send_v, recv_v, partner)

    V[p] = jnp.concatenate([bias_in[...], gain_in[...], shift_in[...], jnp.zeros((5, D), F32)], axis=0)
    send_vec().start()
    for b in range(4):
        on_core(1, lambda: send_weights(1, b).start())
    for b in W_ORDER[:2]:
        on_core(0, lambda: send_weights(0, b).start())

    def send_later():
        for b in W_ORDER[:2]:
            on_core(0, lambda: send_weights(0, b).wait_send())
        for b in W_ORDER[2:]:
            on_core(0, lambda: send_weights(0, b).start())
        for b in range(2):
            send_weights2(b).start()

    def need_w(sec, b):
        on_core(sec, lambda: copy_w(sec, b).wait())
        on_core(1 - sec, lambda: send_weights(sec, b).wait_recv())

    def need_w2():
        for b in range(2):
            copy_w2(b).wait()
            remote(
                wd.at[pl.ds(b * D, D), :], BIG.at[down_rows(1 - p, b)], send_w.at[4 + b], recv_w.at[4 + b], partner
            ).wait_recv()

    def send_keys(q, i, group):
        here = KV.at[q, i, own, FIRST[group]]
        return remote(here, here, send_kv.at[q, i, group], recv_kv.at[q, i, group], partner)

    def take_keys(q, i, group):
        here = KV.at[q, i, other, FIRST[group]]
        return remote(here, here, send_kv.at[q, i, group], recv_kv.at[q, i, group], partner)

    def hand_on(q):
        return remote(GOUT.at[q], A.at[0, rows(q)], send_h.at[q], recv_h.at[q], across)

    def hand_back(q):
        return remote(GOUT.at[q], GIN.at[q], send_g.at[q], recv_g.at[q], across)

    def put(src, dst_ref, q, sec, sems, recvs):
        keep = pltpu.make_async_copy(src, dst_ref.at[q, own], sems.at[sec, q])
        give = remote(src, dst_ref.at[q, own], sems.at[sec, q], recvs.at[q], partner)
        return keep, give

    def put_start(src, dst_ref, q, sec, sems, recvs):
        keep, give = put(src, dst_ref, q, sec, sems, recvs)

        @pl.when(p == sec)
        def _():
            keep.start()

        @pl.when(p != sec)
        def _():
            give.start()

    def put_wait(src, dst_ref, q, sec, sems, recvs):
        keep, give = put(src, dst_ref, q, sec, sems, recvs)

        @pl.when(p == sec)
        def _():
            keep.wait()
            remote(src, dst_ref.at[q, other], sems.at[sec, q], recvs.at[q], partner).wait_recv()

        @pl.when(p != sec)
        def _():
            give.wait_send()

    lane = lax.broadcasted_iota(jnp.int32, (1, 128), 1)
    low_lanes = (lane < HEAD).astype(F32)
    high_lanes = 1.0 - low_lanes

    def stack_heads(x):
        wide = x.astype(F32)
        return jnp.concatenate([(wide * low_lanes).astype(BF), (wide * high_lanes).astype(BF)], axis=0)

    def join_heads(x):
        return jnp.where(lane < HEAD, x[:half], x[half:])

    key_at = lax.broadcasted_iota(jnp.int32, (1, seq_len), 1)

    def norm_forward(sec, h_ref_at, dst, q):
        bias, gain, shift = V[sec, 0:1, :], V[sec, 1:2, :], V[sec, 2:3, :]

        def body(i, c):
            r = pl.ds(pl.multiple_of(i * LN_ROWS, LN_ROWS), LN_ROWS)
            rq = pl.ds(pl.multiple_of(q * half + i * LN_ROWS, LN_ROWS), LN_ROWS)
            residual = A[h_ref_at, rq, :].astype(F32) + (RES[r, :] + bias)
            center = jnp.mean(residual, axis=-1, keepdims=True)
            centred = residual - center
            spread = jnp.mean(centred * centred, axis=-1, keepdims=True)
            rstd = lax.rsqrt(spread + NORM_EPS)
            normed = centred * rstd
            N[sec, rq, :] = normed.astype(BF)
            LSE[q, r, spare + sec : spare + sec + 1] = rstd
            dst(r, rq, (normed * gain + shift).astype(BF))
            return c

        lax.fori_loop(0, half // LN_ROWS, body, 0)

    def norm_backward(sec, g_ref, at, q):
        gain = V[sec, 1:2, :]

        def body(i, c):
            r = pl.ds(pl.multiple_of(i * LN_ROWS, LN_ROWS), LN_ROWS)
            rq = pl.ds(pl.multiple_of(q * half + i * LN_ROWS, LN_ROWS), LN_ROWS)
            g = g_ref[q, r, :].astype(F32)
            normed = N[sec, rq, :].astype(F32)
            rstd = LSE[q, r, spare + sec : spare + sec + 1]
            gg = g * gain
            first_mean = jnp.mean(gg, axis=-1, keepdims=True)
            second_mean = jnp.mean(gg * normed, axis=-1, keepdims=True)
            dres = rstd * (gg - first_mean - normed * second_mean)
            RES[r, :] = dres
            A[at, rq, :] = dres.astype(BF)
            b, a, t = c
            return (
                b + jnp.sum(dres, axis=0, keepdims=True),
                a + jnp.sum(g * normed, axis=0, keepdims=True),
                t + jnp.sum(g, axis=0, keepdims=True),
            )

        zero = jnp.zeros((1, D), F32)
        b, a, t = lax.fori_loop(0, half // LN_ROWS, body, (zero, zero, zero))
        S[sec, 0:1, :] += b
        S[sec, 1:2, :] += a
        S[sec, 2:3, :] += t

    S[...] = jnp.zeros_like(S)

    def forward(q, carry):
        length = lens[q]

        @pl.when(first)
        def _():
            copy_tok(q).wait()

        @pl.when(last)
        def _():
            hand_on(q).wait_recv()

        @pl.when(q == 0)
        def _():
            need_w(0, 1)
            need_w(0, 2)

        h = A[0, rows(q), :]
        for group, cols in enumerate(FIRST):
            for i in range(2):
                KV[q, i, own, cols] = mm(h, AW[1 + i, :, cols]).astype(BF)
                send_keys(q, i, group).start()

        @pl.when(q == 0)
        def _():
            send_later()
            need_w(0, 0)

        A[12, rows(q), :] = (mm(h, AW[0]) * HEAD ** (-0.5)).astype(BF)
        valid = key_at < length

        for hp in range(pairs):
            cols = slice(hp * 128, (hp + 1) * 128)
            for group in range(2):
                if FIRST[group].start == cols.start:
                    for i in range(2):
                        take_keys(q, i, group).wait_recv()
            st = mm(stack_heads(A[12, rows(q), cols]), KV[q, 0, :, cols], NT)
            st = jnp.where(valid, st, MASK_FILL)
            top = jnp.max(st, axis=1, keepdims=True)
            e = jnp.exp(st - top)
            total = jnp.sum(e, axis=1, keepdims=True)
            ct = mm(e.astype(BF), KV[q, 1, :, cols]) * (1.0 / total)
            A[1, rows(q), cols] = join_heads(ct).astype(BF)
            lse = top + jnp.log(total)
            LSE[q, :, 2 * hp : 2 * hp + 1] = lse[:half]
            LSE[q, :, 2 * hp + 1 : 2 * hp + 2] = lse[half:]

        @pl.when(q == 0)
        def _():
            need_w(0, 3)
            remote(V.at[1 - p], V.at[1 - p], send_v, recv_v, partner).wait_recv()

        RES[...] = mm(A[1, rows(q), :], AW[3])

        def keep_mid(r, rq, x):
            A[2, rq, :] = x

        norm_forward(0, 0, keep_mid, q)
        put_start(A.at[2, rows(q)], out_ref, q, 0, sem_o, recv_o)

        @pl.when(q == 0)
        def _():
            for b in range(4):
                need_w(1, b)

        for b in range(4):
            hidden, slope = gelu_pair(mm(A[2, rows(q), :], BIG[pl.ds((FEED_AT + b) * D, D), :]))
            A[3 + b, rows(q), :] = hidden.astype(BF)
            A[7 + b, rows(q), :] = slope.astype(BF)

        @pl.when(q == 0)
        def _():
            need_w2()

        for n in range(D // 256):
            c = slice(n * 256, (n + 1) * 256)
            acc = mm(A[3, rows(q), :], BIG[pl.ds((DOWN_AT + 0) * D, D), c])
            for b in range(1, 4):
                acc += mm(A[3 + b, rows(q), :], BIG[pl.ds((DOWN_AT + b) * D, D), c])
            RES[:, c] = acc

        def keep_out(r, rq, x):
            GOUT[q, r, :] = x

        norm_forward(1, 2, keep_out, q)

        @pl.when(first)
        def _():
            hand_on(q).start()

        put_start(GOUT.at[q], out_ref, q, 1, sem_o, recv_o)
        return carry

    lax.fori_loop(0, nq, forward, 0)

    per = wide // STEP_ROWS
    done = jnp.where(first, 11, 13)
    steps = done * per
    deep = line // 2 + 1
    low_mid = line // 2 - 1

    def roles(kind):
        root_y = lax.rem(kind, 2)
        k = low_mid + root_y
        at = z == k
        ours = y == root_y
        rung = kind >= 2
        along = rung | ours
        beside = at | (kind < 2)
        kids = (ours & beside, along & (z <= k) & has_dn, along & (z >= k) & has_up)
        to_side = jnp.logical_not(ours) & beside
        move = jnp.where(to_side, 1 - 2 * y, jnp.where(z > k, -2, 2))
        slot = jnp.where(to_side, 0, jnp.where(z > k, 2, 1))
        z_up = z + jnp.where(to_side, 0, jnp.where(z > k, -1, 1))
        away = jnp.abs(z - k) + 1 - ours.astype(jnp.int32)
        return k, kids, at & ours, (lax.rem(dp + move + 2 * line, 2 * line), s), slot, z_up, away

    def heap(kind, k, n, zz, i):
        spare = jnp.where((kind == 2) | (zz == low_mid), 6, 3)
        unit = jnp.where(kind < 2, n, jnp.where(zz == k, 3 + n, spare))
        flat = i * UNITS + unit
        return BIG.at[pl.ds(pl.multiple_of(flat * CLASS_ROWS, 16), CLASS_ROWS)]

    def part(kind, i):
        return G.at[i // per, pl.ds(pl.multiple_of(lax.rem(i, per) * STEP_ROWS + kind * CLASS_ROWS, 16), CLASS_ROWS)]

    def final_at(o, row, count):
        return A.at[FINAL_AT + o // 2, pl.ds(pl.multiple_of(lax.rem(o, 2) * wide + row, 16), count)]

    def final(kind, i):
        return final_at(i // per, lax.rem(i, per) * STEP_ROWS + kind * CLASS_ROWS, CLASS_ROWS)

    def send_down(kind, i, kids):
        for n in range(3):
            @pl.when(kids[n])
            def _():
                remote(final(kind, i), final(kind, i), s_down.at[kind, n], r_fin.at[kind, i], peers[n]).start()

    def up_chunk(kind, i):
        k, kids, root, parent, slot, z_up, _ = roles(kind)
        acc = part(kind, i)
        for n in range(3):
            @pl.when(kids[n])
            def _():
                got = heap(kind, k, n, z, i)
                remote(acc, got, s_up.at[kind], r_up.at[kind, n, i], peers[n]).wait_recv()
                acc[...] = (acc[...].astype(F32) + got[...].astype(F32)).astype(BF)

        @pl.when(root)
        def _():
            final(kind, i)[...] = acc[...]
            send_down(kind, i, kids)

        @pl.when(jnp.logical_not(root))
        def _():
            remote(acc, heap(kind, k, slot, z_up, i), s_up.at[kind], r_up.at[kind, slot, i], parent).start()

    def down_chunk(kind, i):
        _, kids, root, parent, _, _, _ = roles(kind)

        @pl.when(jnp.logical_not(root))
        def _():
            remote(final(kind, i), final(kind, i), s_up.at[kind], r_fin.at[kind, i], parent).wait_recv()
            send_down(kind, i, kids)

    def place_of(o):
        return o + jnp.where(last & (o >= GUEST), 1, 0)

    def lend():
        return remote(G.at[11], G.at[GUEST], send_lend, recv_lend, across)

    def give_back():
        return remote(final_at(GUEST, 0, wide), final_at(11, 0, wide), send_back, recv_back, across)

    def store(o, wait):
        lies = final_at(place_of(o), 0, wide)
        owner = jnp.where((o < 4) | ((o >= 6) & (o < 8)), 1, 0)
        is_main = (o < 4) | (o >= 8)

        def place(core):
            cols = pl.ds(pl.multiple_of(lax.rem(o, 4) * D, D), D)
            main = main_ref.at[pl.ds(pl.multiple_of(core * wide, 128), wide), cols]
            down = half_ref.at[pl.ds(pl.multiple_of(lax.rem(o, 2) * D + core * wide, 128), wide)]
            return main, down

        for here, theirs, hit in zip(place(p), place(1 - p), (is_main, jnp.logical_not(is_main))):
            @pl.when(hit & (owner == p))
            def _():
                c = pltpu.make_async_copy(lies, here, sem_go.at[o])
                if wait:
                    c.wait()
                    remote(lies, theirs, sem_go.at[o], recv_go.at[o], partner).wait_recv()
                else:
                    c.start()

            @pl.when(hit & (owner != p))
            def _():
                c = remote(lies, here, sem_go.at[o], recv_go.at[o], partner)
                c.wait_send() if wait else c.start()

    def sum_step(t):
        def ups(kind, c):
            i = t - HOP * (deep - roles(kind)[6])

            @pl.when((i >= 0) & (i < steps))
            def _():
                up_chunk(kind, i)

            return c

        def downs(kind, c):
            i = t - HOP * (deep + roles(kind)[6])

            @pl.when((i >= 0) & (i < steps))
            def _():
                down_chunk(kind, i)

            return c

        lax.fori_loop(0, CLASSES, ups, 0)
        lax.fori_loop(0, CLASSES, downs, 0)
        i = t - 2 * HOP * deep

        @pl.when((i >= 0) & (lax.rem(i, per) == per - 1))
        def _():
            o = i // per
            guest = last & (o == GUEST)

            @pl.when(guest)
            def _():
                give_back().start()

            @pl.when(jnp.logical_not(guest))
            def _():
                store(o - jnp.where(last & (o > GUEST), 1, 0), False)

    def sum_steps(lo, hi):
        def one(t, c):
            sum_step(t)
            return c

        lax.fori_loop(lo, hi, one, 0)

    def pump(q, lo, hi):
        @pl.when((q == nq - 1) & first)
        def _():
            sum_steps(lo, hi)

    def stage(j):
        return DKV.at[pl.ds(pl.multiple_of(lax.rem(j, 2) * wide, 128), wide)]

    def send_grad(j):
        return remote(stage(j), GP.at[lax.rem(j, 2)], send_gr.at[lax.rem(j, 2)], recv_gr.at[lax.rem(j, 2)], partner)

    def take_grad(j):
        send_grad(j).wait_recv()
        o = place_of(j)
        G[o] = (G[o].astype(F32) + GP[lax.rem(j, 2)].astype(F32)).astype(BF)

    def weight_grads(lo, hi, after):
        def one(j, c):
            left = jnp.where(j < 4, 2, jnp.where(j < 8, j - 1, jnp.where(j < 11, 0, 1)))
            right = jnp.where(j < 4, 7 + j, jnp.where(j < 8, 11, j + 4))

            @pl.when(j >= lo + 2)
            def _():
                send_grad(j - 2).wait_send()

            stage(j)[...] = mm(A[left, :, other_wide], A[right], TN).astype(BF)

            @pl.when(j > lo)
            def _():
                take_grad(j - 1)

            send_grad(j).start()
            G[place_of(j)] = mm(A[left, :, own_wide], A[right], TN).astype(BF)

            @pl.when(j > lo)
            def _():
                after(j - 1)

            return c

        lax.fori_loop(lo, hi, one, 0)
        take_grad(hi - 1)
        after(hi - 1)
        for j in (hi - 2, hi - 1):
            send_grad(j).wait_send()

    def feed_grads():
        greet(free_sem)

        def after(j):
            @pl.when(j == 0)
            def _():
                pl.semaphore_wait(free_sem, peer_count)

            sum_steps((FEED_PUMP * j + 7) // 8, (FEED_PUMP * (j + 1) + 7) // 8)

        weight_grads(0, 8, after)
        greet(final_sem)
        pl.semaphore_wait(final_sem, peer_count)

    def send_small():
        return remote(S.at[1 - p], SP, send_s, recv_s, partner)

    def send_dkeys(q, group):
        slot = lax.rem(q, 2)
        theirs = pl.ds(pl.multiple_of((1 - p) * 2 * half, 128), 2 * half)
        return remote(
            DKV.at[theirs, LAST[group]], DKVR.at[slot, :, LAST[group]],
            send_dkv.at[group], recv_dkv.at[slot, group], partner,
        )

    def backward(q, carry):
        length = lens[q]

        @pl.when(last)
        def _():
            copy_cot(q).wait()

        @pl.when(first)
        def _():
            hand_back(q).wait_recv()

        norm_backward(1, GIN, 11, q)

        for b in range(4):
            dh = mm(A[11, rows(q), :], BIG[pl.ds((DOWN_AT + b) * D, D), :], NT)
            A[7 + b, rows(q), :] = (dh * A[7 + b, rows(q), :].astype(F32)).astype(BF)

        for n in range(D // 256):
            c = slice(n * 256, (n + 1) * 256)
            acc = RES[:, c]
            for b in range(4):
                acc += mm(A[7 + b, rows(q), :], BIG[pl.ds((FEED_AT + b) * D + c.start, c.stop - c.start), :], NT)
            GIN[q, :, c] = acc.astype(BF)
        put_start(GIN.at[q], ing_ref, q, 1, sem_i, recv_i)

        @pl.when(q > 0)
        def _():
            for group in range(2):
                send_dkeys(q - 1, group).wait_send()

        @pl.when((q == nq - 1) & first)
        def _():
            feed_grads()

        norm_backward(0, GIN, 15, q)

        @pl.when(q == nq - 1)
        def _():
            send_small().start()
        A[13, rows(q), :] = mm(A[15, rows(q), :], AW[3], NT).astype(BF)

        valid = key_at < length
        pump(q, FEED_PUMP + 0 * PUMP, FEED_PUMP + 1 * PUMP)

        for hp in range(pairs):
            if LAST[1].start == hp * 128:
                send_dkeys(q, 0).start()
                pump(q, FEED_PUMP + 1 * PUMP, FEED_PUMP + 2 * PUMP)
            cols = slice(hp * 128, (hp + 1) * 128)
            kp = KV[q, 0, :, cols]
            qs = stack_heads(A[12, rows(q), cols])
            dcs = stack_heads(A[13, rows(q), cols])
            st = jnp.where(valid, mm(qs, kp, NT), MASK_FILL)
            lse = jnp.concatenate(
                [LSE[q, :, 2 * hp : 2 * hp + 1], LSE[q, :, 2 * hp + 1 : 2 * hp + 2]], axis=0
            )
            prob = jnp.exp(st - lse)
            dprob = mm(dcs, KV[q, 1, :, cols], NT)
            mean = jnp.sum(prob * dprob, axis=1, keepdims=True)
            ds = (prob * (dprob - mean)).astype(BF)
            A[12, rows(q), cols] = (join_heads(mm(ds, kp)) * HEAD ** (-0.5)).astype(BF)
            dk = jnp.transpose(mm(jnp.transpose(qs), ds)).astype(BF)
            dv = jnp.transpose(mm(jnp.transpose(dcs), prob.astype(BF))).astype(BF)
            DKV[0:half, cols] = dk[:half]
            DKV[half : 2 * half, cols] = dv[:half]
            DKV[2 * half : 3 * half, cols] = dk[half:]
            DKV[3 * half : 4 * half, cols] = dv[half:]

        send_dkeys(q, 1).start()
        pump(q, FEED_PUMP + 2 * PUMP, FEED_PUMP + 3 * PUMP)
        for n in range(D // 256):
            c = slice(n * 256, (n + 1) * 256)
            RES[:, c] = RES[:, c] + mm(A[12, rows(q), :], AW[0, c, :], NT)
        pump(q, FEED_PUMP + 3 * PUMP, FEED_PUMP + 4 * PUMP)
        for group in range(2):
            send_dkeys(q, group).wait_recv()
        slot = lax.rem(q, 2)
        for i in range(2):
            mine = DKV[pl.ds(pl.multiple_of((2 * p + i) * half, half), half), :]
            A[13 + i, rows(q), :] = (mine.astype(F32) + DKVR[slot, i * half : (i + 1) * half].astype(F32)).astype(BF)

        @pl.when(first)
        def _():
            hand_on(q).wait_send()

        put_wait(GOUT.at[q], out_ref, q, 1, sem_o, recv_o)
        put_wait(GIN.at[q], ing_ref, q, 1, sem_i, recv_i)
        for n in range(D // 256):
            c = slice(n * 256, (n + 1) * 256)
            acc = RES[:, c]
            for b in range(1, 3):
                acc += mm(A[12 + b, rows(q), :], AW[b, c, :], NT)
            GOUT[q, :, c] = acc.astype(BF)

        @pl.when(last)
        def _():
            hand_back(q).start()

        put_start(GOUT.at[q], ing_ref, q, 0, sem_i, recv_i)
        pump(q, FEED_PUMP + 4 * PUMP, FEED_PUMP + 5 * PUMP)
        return carry

    lax.fori_loop(0, nq, backward, 0)

    for group in range(2):
        send_dkeys(nq - 1, group).wait_send()

    @pl.when(last)
    def _():
        feed_grads()

    before = FEED_PUMP + jnp.where(first, 5 * PUMP, 0)
    weight_grads(8, 12, lambda j: sum_steps(before + (j - 8) * PUMP, before + (j - 7) * PUMP))

    @pl.when(first)
    def _():
        lend().start()

    send_small().wait_recv()
    SR[3] = S[p] + SP[...]
    _, kids, root, parent, slot, _, away = roles(jnp.int32(0))

    def small_down():
        for n in range(3):
            @pl.when(kids[n])
            def _():
                remote(SR.at[4], SR.at[4], t_down.at[n], q_fin, peers[n]).start()

    def small_up():
        for n in range(3):
            @pl.when(kids[n])
            def _():
                remote(SR.at[3], SR.at[n], t_up, q_up.at[n], peers[n]).wait_recv()
                SR[3] = SR[3] + SR[n]

        @pl.when(root)
        def _():
            SR[4] = SR[3]
            small_down()

        @pl.when(jnp.logical_not(root))
        def _():
            remote(SR.at[3], SR.at[slot], t_up, q_up.at[slot], parent).start()

    small_at = steps - HOP * deep

    def tail(t, c):
        @pl.when(last & (t == GUEST * per))
        def _():
            lend().wait_recv()

        sum_step(t)

        @pl.when(t == small_at + HOP * (deep - away))
        def _():
            small_up()

        @pl.when((t == small_at + HOP * (deep + away)) & jnp.logical_not(root))
        def _():
            remote(SR.at[3], SR.at[4], t_up, q_fin, parent).wait_recv()
            small_down()

        return c

    lax.fori_loop(before + 4 * PUMP, steps + 2 * HOP * deep, tail, 0)
    small_out[...] = SR[4]

    @pl.when(first)
    def _():
        give_back().wait_recv()
        store(jnp.int32(11), False)

    whole_first = G.at[pl.ds(0, 11), pl.ds(0, per * CLASS_ROWS)]
    whole_last = G.at[pl.ds(0, 13), pl.ds(0, per * CLASS_ROWS)]
    for kind in range(CLASSES):
        _, kids_of, root_of, parent_of, _, _, _ = roles(jnp.int32(kind))

        for here, whole in ((first, whole_first), (last, whole_last)):
            @pl.when(here & jnp.logical_not(root_of))
            def _():
                remote(whole, whole, s_up.at[kind], r_fin.at[kind, 0], parent_of).wait_send()

            for n in range(3):
                @pl.when(here & kids_of[n])
                def _():
                    remote(whole, whole, s_down.at[kind, n], r_fin.at[kind, 0], peers[n]).wait_send()

    @pl.when(jnp.logical_not(root))
    def _():
        remote(SR.at[3], SR.at[slot], t_up, q_up.at[slot], parent).wait_send()

    for n in range(3):
        @pl.when(kids[n])
        def _():
            remote(SR.at[4], SR.at[4], t_down.at[n], q_fin, peers[n]).wait_send()

    send_small().wait_send()

    @pl.when(first)
    def _():
        lend().wait_send()

    @pl.when(last)
    def _():
        give_back().wait_send()


    for o in range(12):
        store(jnp.int32(o), True)
    send_vec().wait_send()
    for b in range(4):
        on_core(1, lambda: send_weights(1, b).wait_send())
    for b in W_ORDER[2:]:
        on_core(0, lambda: send_weights(0, b).wait_send())
    for b in range(2):
        send_weights2(b).wait_send()
    for q in range(nq):
        for i in range(2):
            for group in range(2):
                send_keys(q, i, group).wait_send()

        @pl.when(last)
        def _():
            hand_back(q).wait_send()

        put_wait(A.at[2, rows(q)], out_ref, q, 0, sem_o, recv_o)
        put_wait(GOUT.at[q], ing_ref, q, 0, sem_i, recv_i)


def run_layers(tokens, cotangent, lengths, weights, w_down, *rows):
    nq, seq_len, D = tokens.shape
    half = seq_len // 2
    tall = nq * half
    dma = pltpu.SemaphoreType.DMA
    any_spec = pl.BlockSpec(memory_space=pl.ANY)
    vmem_spec = pl.BlockSpec(memory_space=pltpu.VMEM)
    line = lax.axis_size("dp") // 2
    steps = 13 * (D // 2) // STEP_ROWS
    return pl.pallas_call(
        partial(layer_kernel, line),
        name="layers",
        out_shape=(
            jax.ShapeDtypeStruct((nq, seq_len, D), BF),
            jax.ShapeDtypeStruct((nq, seq_len, D), BF),
            jax.ShapeDtypeStruct((D, 4 * D), BF),
            jax.ShapeDtypeStruct((2 * D, D), BF),
            jax.ShapeDtypeStruct((8, D), F32),
        ),
        in_specs=[any_spec, any_spec, pl.BlockSpec(memory_space=pltpu.SMEM), any_spec, any_spec] + [vmem_spec] * 3,
        out_specs=(any_spec, any_spec, any_spec, any_spec, vmem_spec),
        scratch_shapes=[
            pltpu.VMEM((max(8 * D, steps * UNITS * CLASS_ROWS), D), BF),
            pltpu.VMEM((4, D, D), BF),
            pltpu.VMEM((2, 8, D), F32),
            pltpu.VMEM((16, tall, D), BF),
            pltpu.VMEM((nq, 2, seq_len, D), BF),
            pltpu.VMEM((2, tall, D), BF),
            pltpu.VMEM((nq, half, 128), F32),
            pltpu.VMEM((nq, half, D), BF),
            pltpu.VMEM((nq, half, D), BF),
            pltpu.VMEM((half, D), F32),
            pltpu.VMEM((4 * half, D), BF),
            pltpu.VMEM((2, 2 * half, D), BF),
            pltpu.VMEM((13, D // 2, D), BF),
            pltpu.VMEM((2, D // 2, D), BF),
            pltpu.VMEM((2, 8, D), F32),
            pltpu.VMEM((8, D), F32),
            pltpu.VMEM((5, 8, D), F32),
            dma((6,)), dma((nq,)), dma((nq,)), dma((6,)), dma((6,)),
            dma((nq, 2, 2)), dma((nq, 2, 2)), dma((nq,)), dma((nq,)), dma((2, nq)), dma((nq,)),
            dma((2,)), dma((2, 2)), dma((nq,)), dma((nq,)), dma((2, nq)), dma((nq,)),
            dma((2,)), dma((2,)), dma((12,)), dma((12,)), dma, dma,
            dma, dma, dma((CLASSES,)), dma((CLASSES, 3)), dma((CLASSES, 3, steps)), dma((CLASSES, steps)),
            dma, dma((3,)), dma((3,)), dma, pltpu.SemaphoreType.REGULAR, pltpu.SemaphoreType.REGULAR,
            dma, dma, dma, dma,
        ],
        compiler_params=pltpu.CompilerParams(
            collective_id=0, has_side_effects=True, vmem_limit_bytes=64 * MIB
        ),
        cost_estimate=pl.CostEstimate(flops=60 * 10**9, bytes_accessed=40 * 10**6, transcendentals=10**7),
    )(tokens, cotangent, lengths, weights, w_down, *rows)


def result_kernel(out_in, grad_in, main_in, half_in, small_in, out, grad, main, down, bias, gain, shift):
    out[...] = out_in[...]
    grad[...] = grad_in[...]
    main[...] = main_in[...].astype(F32)
    down[...] = half_in[...].astype(F32)
    bias[...] = small_in[0:1, :]
    gain[...] = small_in[1:2, :]
    shift[...] = small_in[2:3, :]


RESULT_STEPS = 8


def results(*arrays):
    types = (BF, BF, F32, F32)

    def rows_of(a):
        return pl.BlockSpec((a.shape[0] // RESULT_STEPS, a.shape[1]), lambda i: (i, 0))

    def whole(a, rows):
        return pl.BlockSpec((rows, a.shape[1]), lambda i: (0, 0))

    small = arrays[4]
    return pl.pallas_call(
        result_kernel,
        name="results",
        grid=(RESULT_STEPS,),
        out_shape=tuple(jax.ShapeDtypeStruct(a.shape, t) for a, t in zip(arrays[:4], types))
        + tuple(jax.ShapeDtypeStruct((1, small.shape[1]), F32) for _ in range(3)),
        in_specs=[rows_of(a) for a in arrays[:4]] + [whole(small, 8)],
        out_specs=tuple(rows_of(a) for a in arrays[:4]) + tuple(whole(small, 1) for _ in range(3)),
        compiler_params=pltpu.CompilerParams(vmem_limit_bytes=63 * MIB),
    )(*arrays)


def on_device(tokens, lengths, w_main, w_down_half, out_bias, ln_gain, ln_bias, cotangent):
    nq, seq_len, D = tokens.shape
    kept_out, kept_grad, grad_main, grad_half, small = run_layers(
        tokens, cotangent, lengths, w_main[0], w_down_half[0], out_bias, ln_gain, ln_bias
    )
    tall = nq * seq_len
    kept_out, kept_grad, grad_main, grad_half, bias, gain, shift = results(
        kept_out.reshape(tall, D), kept_grad.reshape(tall, D), grad_main, grad_half, small
    )
    return (
        kept_out.reshape(1, nq, seq_len, D),
        kept_grad.reshape(1, nq, seq_len, D),
        grad_main[None],
        grad_half[None],
        bias,
        gain,
        shift,
    )


def solution(mesh):
    in_specs = (
        P("dp", None, None),
        P("dp"),
        P("section", None, None),
        P("section", None, None),
        P("section", None),
        P("section", None),
        P("section", None),
        P("dp", None, None),
    )
    out_specs = (
        P("section", "dp", None, None),
        P("section", "dp", None, None),
        P("section", None, None),
        P("section", None, None),
        P("section", None),
        P("section", None),
        P("section", None),
    )
    return jax.shard_map(
        on_device, mesh=mesh, in_specs=in_specs, out_specs=out_specs, check_vma=False
    )
```

```python
from functools import partial

import jax
import jax.numpy as jnp
from jax import lax
from jax.experimental import pallas as pl
from jax.experimental.pallas import tpu as pltpu
from jax.sharding import PartitionSpec as P

HEAD = 64
NORM_EPS = 1e-06
MASK_FILL = -1000000000.0
MESH = pl.DeviceIdType.MESH
BF = jnp.bfloat16
F32 = jnp.float32
MIB = 1024 * 1024
NN = (((1,), (0,)), ((), ()))
NT = (((1,), (1,)), ((), ()))
TN = (((0,), (0,)), ((), ()))
LN_ROWS = 256
W_ORDER = (1, 2, 0, 3)
FIRST = (slice(0, 256), slice(256, 768))
LAST = (slice(0, 512), slice(512, 768))
CLASSES = 4
CLASS_ROWS = 48
STEP_ROWS = CLASSES * CLASS_ROWS
UNITS = 7
GUEST = 10
HOP = 1
FINAL_AT = 3
FEED_PUMP = 3
PUMP = 1
FEED_AT = 0
DOWN_AT = 4


def mm(a, b, dims=NN):
    return lax.dot_general(a, b, dims, preferred_element_type=F32)


def gelu_pair(x):
    cdf = 0.5 * (1.0 + lax.erf(x * 0.7071067811865476))
    return x * cdf, cdf + x * (jnp.exp(x * x * -0.5) * 0.3989422804014327)


def layer_kernel(
    line, tok, cot, lens, wm, wd, bias_in, gain_in, shift_in,
    out_ref, ing_ref, main_ref, half_ref, small_out,
    BIG, AW, V, A, KV, N, LSE, GIN, GOUT, RES, DKV, DKVR, G, GP, S, SP, SR,
    sem_w, sem_tok, sem_cot, send_w, recv_w, send_kv, recv_kv, send_h, recv_h, sem_o, recv_o,
    send_dkv, recv_dkv, send_g, recv_g, sem_i, recv_i, send_gr, recv_gr, sem_go, recv_go, send_v, recv_v,
    send_s, recv_s, s_up, s_down, r_up, r_fin, t_up, t_down, q_up, q_fin, free_sem, final_sem, send_lend, recv_lend, send_back, recv_back,
):
    nq, seq_len, D = tok.shape
    half = seq_len // 2
    pairs = D // 128
    spare = D // HEAD
    dp = lax.axis_index("dp")
    s = lax.axis_index("section")
    p = lax.rem(s, 2)
    layer = s // 2
    partner = (dp, s + 1 - 2 * p)
    across = (dp, lax.rem(s + 2, 4))
    first = layer == 0
    last = layer == 1
    wide = D // 2
    own_wide = pl.ds(pl.multiple_of(p * wide, 128), wide)
    other_wide = pl.ds(pl.multiple_of((1 - p) * wide, 128), wide)
    own = pl.ds(pl.multiple_of(p * half, half), half)
    other = pl.ds(pl.multiple_of((1 - p) * half, half), half)

    def down_rows(core, b):
        return pl.ds(pl.multiple_of((DOWN_AT + 2 * core + b) * D, 128), D)

    def main_place(sec, b):
        return AW.at[b] if sec == 0 else BIG.at[pl.ds((FEED_AT + b) * D, D)]

    def rows(q):
        return pl.ds(pl.multiple_of(q * half, half), half)

    def copy_w(sec, b):
        return pltpu.make_async_copy(wm.at[:, pl.ds(b * D, D)], main_place(sec, b), sem_w.at[b])

    def on_core(sec, act):
        pl.when(p == sec)(act)

    def copy_w2(b):
        return pltpu.make_async_copy(wd.at[pl.ds(b * D, D), :], BIG.at[down_rows(p, b)], sem_w.at[4 + b])

    def copy_tok(q):
        return pltpu.make_async_copy(tok.at[q, own], A.at[0, rows(q)], sem_tok.at[q])

    def copy_cot(q):
        return pltpu.make_async_copy(cot.at[q, own], GIN.at[q], sem_cot.at[q])

    @pl.when(first)
    def _():
        for q in range(nq):
            copy_tok(q).start()

    for b in W_ORDER:
        on_core(0, lambda: copy_w(0, b).start())
        on_core(1, lambda: copy_w(1, b).start())
    for b in range(2):
        copy_w2(b).start()

    @pl.when(last)
    def _():
        for q in range(nq):
            copy_cot(q).start()

    y = lax.rem(dp, 2)
    z = dp // 2
    has_dn = z > 0
    has_up = z < line - 1
    side = (dp + 1 - 2 * y, s)
    below = (lax.rem(dp + 2 * line - 2, 2 * line), s)
    above = (lax.rem(dp + 2, 2 * line), s)
    peers = (side, below, above)
    peer_count = 1 + has_dn.astype(jnp.int32) + has_up.astype(jnp.int32)

    def greet(sem):
        pl.semaphore_signal(sem, inc=1, device_id=side, device_id_type=MESH)

        @pl.when(has_dn)
        def _():
            pl.semaphore_signal(sem, inc=1, device_id=below, device_id_type=MESH)

        @pl.when(has_up)
        def _():
            pl.semaphore_signal(sem, inc=1, device_id=above, device_id_type=MESH)

    barrier = pltpu.get_barrier_semaphore()
    for peer in (partner, across):
        pl.semaphore_signal(barrier, inc=1, device_id=peer, device_id_type=MESH)
    greet(barrier)
    pl.semaphore_wait(barrier, 2 + peer_count)

    def remote(src, dst, send, recv, dev):
        return pltpu.make_async_remote_copy(
            src_ref=src, dst_ref=dst, send_sem=send, recv_sem=recv, device_id=dev, device_id_type=MESH
        )

    def send_weights(sec, b):
        return remote(wm.at[:, pl.ds(b * D, D)], main_place(sec, b), send_w.at[b], recv_w.at[b], partner)

    def send_weights2(b):
        return remote(wd.at[pl.ds(b * D, D), :], BIG.at[down_rows(p, b)], send_w.at[4 + b], recv_w.at[4 + b], partner)

    def send_vec():
        return remote(V.at[p], V.at[p], send_v, recv_v, partner)

    V[p] = jnp.concatenate([bias_in[...], gain_in[...], shift_in[...], jnp.zeros((5, D), F32)], axis=0)
    send_vec().start()
    for b in range(4):
        on_core(1, lambda: send_weights(1, b).start())
    for b in W_ORDER[:2]:
        on_core(0, lambda: send_weights(0, b).start())

    def send_later():
        for b in W_ORDER[:2]:
            on_core(0, lambda: send_weights(0, b).wait_send())
        for b in W_ORDER[2:]:
            on_core(0, lambda: send_weights(0, b).start())
        for b in range(2):
            send_weights2(b).start()

    def need_w(sec, b):
        on_core(sec, lambda: copy_w(sec, b).wait())
        on_core(1 - sec, lambda: send_weights(sec, b).wait_recv())

    def need_w2():
        for b in range(2):
            copy_w2(b).wait()
            remote(
                wd.at[pl.ds(b * D, D), :], BIG.at[down_rows(1 - p, b)], send_w.at[4 + b], recv_w.at[4 + b], partner
            ).wait_recv()

    def send_keys(q, i, group):
        here = KV.at[q, i, own, FIRST[group]]
        return remote(here, here, send_kv.at[q, i, group], recv_kv.at[q, i, group], partner)

    def take_keys(q, i, group):
        here = KV.at[q, i, other, FIRST[group]]
        return remote(here, here, send_kv.at[q, i, group], recv_kv.at[q, i, group], partner)

    def hand_on(q):
        return remote(GOUT.at[q], A.at[0, rows(q)], send_h.at[q], recv_h.at[q], across)

    def hand_back(q):
        return remote(GOUT.at[q], GIN.at[q], send_g.at[q], recv_g.at[q], across)

    def put(src, dst_ref, q, sec, sems, recvs):
        keep = pltpu.make_async_copy(src, dst_ref.at[q, own], sems.at[sec, q])
        give = remote(src, dst_ref.at[q, own], sems.at[sec, q], recvs.at[q], partner)
        return keep, give

    def put_start(src, dst_ref, q, sec, sems, recvs):
        keep, give = put(src, dst_ref, q, sec, sems, recvs)

        @pl.when(p == sec)
        def _():
            keep.start()

        @pl.when(p != sec)
        def _():
            give.start()

    def put_wait(src, dst_ref, q, sec, sems, recvs):
        keep, give = put(src, dst_ref, q, sec, sems, recvs)

        @pl.when(p == sec)
        def _():
            keep.wait()
            remote(src, dst_ref.at[q, other], sems.at[sec, q], recvs.at[q], partner).wait_recv()

        @pl.when(p != sec)
        def _():
            give.wait_send()

    lane = lax.broadcasted_iota(jnp.int32, (1, 128), 1)
    low_lanes = (lane < HEAD).astype(F32)
    high_lanes = 1.0 - low_lanes

    def stack_heads(x):
        wide = x.astype(F32)
        return jnp.concatenate([(wide * low_lanes).astype(BF), (wide * high_lanes).astype(BF)], axis=0)

    def join_heads(x):
        return jnp.where(lane < HEAD, x[:half], x[half:])

    key_at = lax.broadcasted_iota(jnp.int32, (1, seq_len), 1)

    def norm_forward(sec, h_ref_at, dst, q):
        bias, gain, shift = V[sec, 0:1, :], V[sec, 1:2, :], V[sec, 2:3, :]

        def body(i, c):
            r = pl.ds(pl.multiple_of(i * LN_ROWS, LN_ROWS), LN_ROWS)
            rq = pl.ds(pl.multiple_of(q * half + i * LN_ROWS, LN_ROWS), LN_ROWS)
            residual = A[h_ref_at, rq, :].astype(F32) + (RES[r, :] + bias)
            center = jnp.mean(residual, axis=-1, keepdims=True)
            centred = residual - center
            spread = jnp.mean(centred * centred, axis=-1, keepdims=True)
            rstd = lax.rsqrt(spread + NORM_EPS)
            normed = centred * rstd
            N[sec, rq, :] = normed.astype(BF)
            LSE[q, r, spare + sec : spare + sec + 1] = rstd
            dst(r, rq, (normed * gain + shift).astype(BF))
            return c

        lax.fori_loop(0, half // LN_ROWS, body, 0)

    def norm_backward(sec, g_ref, at, q):
        gain = V[sec, 1:2, :]

        def body(i, c):
            r = pl.ds(pl.multiple_of(i * LN_ROWS, LN_ROWS), LN_ROWS)
            rq = pl.ds(pl.multiple_of(q * half + i * LN_ROWS, LN_ROWS), LN_ROWS)
            g = g_ref[q, r, :].astype(F32)
            normed = N[sec, rq, :].astype(F32)
            rstd = LSE[q, r, spare + sec : spare + sec + 1]
            gg = g * gain
            first_mean = jnp.mean(gg, axis=-1, keepdims=True)
            second_mean = jnp.mean(gg * normed, axis=-1, keepdims=True)
            dres = rstd * (gg - first_mean - normed * second_mean)
            RES[r, :] = dres
            A[at, rq, :] = dres.astype(BF)
            b, a, t = c
            return (
                b + jnp.sum(dres, axis=0, keepdims=True),
                a + jnp.sum(g * normed, axis=0, keepdims=True),
                t + jnp.sum(g, axis=0, keepdims=True),
            )

        zero = jnp.zeros((1, D), F32)
        b, a, t = lax.fori_loop(0, half // LN_ROWS, body, (zero, zero, zero))
        S[sec, 0:1, :] += b
        S[sec, 1:2, :] += a
        S[sec, 2:3, :] += t

    S[...] = jnp.zeros_like(S)

    def forward(q, carry):
        length = lens[q]

        @pl.when(first)
        def _():
            copy_tok(q).wait()

        @pl.when(last)
        def _():
            hand_on(q).wait_recv()

        @pl.when(q == 0)
        def _():
            need_w(0, 1)
            need_w(0, 2)

        h = A[0, rows(q), :]
        for group, cols in enumerate(FIRST):
            for i in range(2):
                KV[q, i, own, cols] = mm(h, AW[1 + i, :, cols]).astype(BF)
                send_keys(q, i, group).start()

        @pl.when(q == 0)
        def _():
            send_later()
            need_w(0, 0)

        A[12, rows(q), :] = (mm(h, AW[0]) * HEAD ** (-0.5)).astype(BF)
        valid = key_at < length

        for hp in range(pairs):
            cols = slice(hp * 128, (hp + 1) * 128)
            for group in range(2):
                if FIRST[group].start == cols.start:
                    for i in range(2):
                        take_keys(q, i, group).wait_recv()
            st = mm(stack_heads(A[12, rows(q), cols]), KV[q, 0, :, cols], NT)
            st = jnp.where(valid, st, MASK_FILL)
            top = jnp.max(st, axis=1, keepdims=True)
            e = jnp.exp(st - top)
            total = jnp.sum(e, axis=1, keepdims=True)
            ct = mm(e.astype(BF), KV[q, 1, :, cols]) * (1.0 / total)
            A[1, rows(q), cols] = join_heads(ct).astype(BF)
            lse = top + jnp.log(total)
            LSE[q, :, 2 * hp : 2 * hp + 1] = lse[:half]
            LSE[q, :, 2 * hp + 1 : 2 * hp + 2] = lse[half:]

        @pl.when(q == 0)
        def _():
            need_w(0, 3)
            remote(V.at[1 - p], V.at[1 - p], send_v, recv_v, partner).wait_recv()

        RES[...] = mm(A[1, rows(q), :], AW[3])

        def keep_mid(r, rq, x):
            A[2, rq, :] = x

        norm_forward(0, 0, keep_mid, q)
        put_start(A.at[2, rows(q)], out_ref, q, 0, sem_o, recv_o)

        @pl.when(q == 0)
        def _():
            for b in range(4):
                need_w(1, b)

        for b in range(4):
            hidden, slope = gelu_pair(mm(A[2, rows(q), :], BIG[pl.ds((FEED_AT + b) * D, D), :]))
            A[3 + b, rows(q), :] = hidden.astype(BF)
            A[7 + b, rows(q), :] = slope.astype(BF)

        @pl.when(q == 0)
        def _():
            need_w2()

        for n in range(D // 256):
            c = slice(n * 256, (n + 1) * 256)
            acc = mm(A[3, rows(q), :], BIG[pl.ds((DOWN_AT + 0) * D, D), c])
            for b in range(1, 4):
                acc += mm(A[3 + b, rows(q), :], BIG[pl.ds((DOWN_AT + b) * D, D), c])
            RES[:, c] = acc

        def keep_out(r, rq, x):
            GOUT[q, r, :] = x

        norm_forward(1, 2, keep_out, q)

        @pl.when(first)
        def _():
            hand_on(q).start()

        put_start(GOUT.at[q], out_ref, q, 1, sem_o, recv_o)
        return carry

    lax.fori_loop(0, nq, forward, 0)

    per = wide // STEP_ROWS
    done = jnp.where(first, 11, 13)
    steps = done * per
    deep = line // 2 + 1
    low_mid = line // 2 - 1

    def roles(kind):
        root_y = lax.rem(kind, 2)
        k = low_mid + root_y
        at = z == k
        ours = y == root_y
        rung = kind >= 2
        along = rung | ours
        beside = at | (kind < 2)
        kids = (ours & beside, along & (z <= k) & has_dn, along & (z >= k) & has_up)
        to_side = jnp.logical_not(ours) & beside
        move = jnp.where(to_side, 1 - 2 * y, jnp.where(z > k, -2, 2))
        slot = jnp.where(to_side, 0, jnp.where(z > k, 2, 1))
        z_up = z + jnp.where(to_side, 0, jnp.where(z > k, -1, 1))
        away = jnp.abs(z - k) + 1 - ours.astype(jnp.int32)
        return k, kids, at & ours, (lax.rem(dp + move + 2 * line, 2 * line), s), slot, z_up, away

    def heap(kind, k, n, zz, i):
        spare = jnp.where((kind == 2) | (zz == low_mid), 6, 3)
        unit = jnp.where(kind < 2, n, jnp.where(zz == k, 3 + n, spare))
        flat = i * UNITS + unit
        return BIG.at[pl.ds(pl.multiple_of(flat * CLASS_ROWS, 16), CLASS_ROWS)]

    def part(kind, i):
        return G.at[i // per, pl.ds(pl.multiple_of(lax.rem(i, per) * STEP_ROWS + kind * CLASS_ROWS, 16), CLASS_ROWS)]

    def final_at(o, row, count):
        return A.at[FINAL_AT + o // 2, pl.ds(pl.multiple_of(lax.rem(o, 2) * wide + row, 16), count)]

    def final(kind, i):
        return final_at(i // per, lax.rem(i, per) * STEP_ROWS + kind * CLASS_ROWS, CLASS_ROWS)

    def send_down(kind, i, kids):
        for n in range(3):
            @pl.when(kids[n])
            def _():
                remote(final(kind, i), final(kind, i), s_down.at[kind, n], r_fin.at[kind, i], peers[n]).start()

    def up_chunk(kind, i):
        k, kids, root, parent, slot, z_up, _ = roles(kind)
        acc = part(kind, i)
        for n in range(3):
            @pl.when(kids[n])
            def _():
                got = heap(kind, k, n, z, i)
                remote(acc, got, s_up.at[kind], r_up.at[kind, n, i], peers[n]).wait_recv()
                acc[...] = (acc[...].astype(F32) + got[...].astype(F32)).astype(BF)

        @pl.when(root)
        def _():
            final(kind, i)[...] = acc[...]
            send_down(kind, i, kids)

        @pl.when(jnp.logical_not(root))
        def _():
            remote(acc, heap(kind, k, slot, z_up, i), s_up.at[kind], r_up.at[kind, slot, i], parent).start()

    def down_chunk(kind, i):
        _, kids, root, parent, _, _, _ = roles(kind)

        @pl.when(jnp.logical_not(root))
        def _():
            remote(final(kind, i), final(kind, i), s_up.at[kind], r_fin.at[kind, i], parent).wait_recv()
            send_down(kind, i, kids)

    def place_of(o):
        return o + jnp.where(last & (o >= GUEST), 1, 0)

    def lend():
        return remote(G.at[11], G.at[GUEST], send_lend, recv_lend, across)

    def give_back():
        return remote(final_at(GUEST, 0, wide), final_at(11, 0, wide), send_back, recv_back, across)

    def store(o, wait):
        lies = final_at(place_of(o), 0, wide)
        owner = jnp.where((o < 4) | ((o >= 6) & (o < 8)), 1, 0)
        is_main = (o < 4) | (o >= 8)

        def place(core):
            cols = pl.ds(pl.multiple_of(lax.rem(o, 4) * D, D), D)
            main = main_ref.at[pl.ds(pl.multiple_of(core * wide, 128), wide), cols]
            down = half_ref.at[pl.ds(pl.multiple_of(lax.rem(o, 2) * D + core * wide, 128), wide)]
            return main, down

        for here, theirs, hit in zip(place(p), place(1 - p), (is_main, jnp.logical_not(is_main))):
            @pl.when(hit & (owner == p))
            def _():
                c = pltpu.make_async_copy(lies, here, sem_go.at[o])
                if wait:
                    c.wait()
                    remote(lies, theirs, sem_go.at[o], recv_go.at[o], partner).wait_recv()
                else:
                    c.start()

            @pl.when(hit & (owner != p))
            def _():
                c = remote(lies, here, sem_go.at[o], recv_go.at[o], partner)
                c.wait_send() if wait else c.start()

    def sum_step(t):
        def ups(kind, c):
            i = t - HOP * (deep - roles(kind)[6])

            @pl.when((i >= 0) & (i < steps))
            def _():
                up_chunk(kind, i)

            return c

        def downs(kind, c):
            i = t - HOP * (deep + roles(kind)[6])

            @pl.when((i >= 0) & (i < steps))
            def _():
                down_chunk(kind, i)

            return c

        lax.fori_loop(0, CLASSES, ups, 0)
        lax.fori_loop(0, CLASSES, downs, 0)
        i = t - 2 * HOP * deep

        @pl.when((i >= 0) & (lax.rem(i, per) == per - 1))
        def _():
            o = i // per
            guest = last & (o == GUEST)

            @pl.when(guest)
            def _():
                give_back().start()

            @pl.when(jnp.logical_not(guest))
            def _():
                store(o - jnp.where(last & (o > GUEST), 1, 0), False)

    def sum_steps(lo, hi):
        def one(t, c):
            sum_step(t)
            return c

        lax.fori_loop(lo, hi, one, 0)

    def pump(q, lo, hi):
        @pl.when((q == nq - 1) & first)
        def _():
            sum_steps(lo, hi)

    def stage(j):
        return DKV.at[pl.ds(pl.multiple_of(lax.rem(j, 2) * wide, 128), wide)]

    def send_grad(j):
        return remote(stage(j), GP.at[lax.rem(j, 2)], send_gr.at[lax.rem(j, 2)], recv_gr.at[lax.rem(j, 2)], partner)

    def take_grad(j):
        send_grad(j).wait_recv()
        o = place_of(j)
        G[o] = (G[o].astype(F32) + GP[lax.rem(j, 2)].astype(F32)).astype(BF)

    def weight_grads(lo, hi, after):
        def one(j, c):
            left = jnp.where(j < 4, 2, jnp.where(j < 8, j - 1, jnp.where(j < 11, 0, 1)))
            right = jnp.where(j < 4, 7 + j, jnp.where(j < 8, 11, j + 4))

            @pl.when(j >= lo + 2)
            def _():
                send_grad(j - 2).wait_send()

            stage(j)[...] = mm(A[left, :, other_wide], A[right], TN).astype(BF)

            @pl.when(j > lo)
            def _():
                take_grad(j - 1)

            send_grad(j).start()
            G[place_of(j)] = mm(A[left, :, own_wide], A[right], TN).astype(BF)

            @pl.when(j > lo)
            def _():
                after(j - 1)

            return c

        lax.fori_loop(lo, hi, one, 0)
        take_grad(hi - 1)
        after(hi - 1)
        for j in (hi - 2, hi - 1):
            send_grad(j).wait_send()

    def feed_grads():
        greet(free_sem)

        def after(j):
            @pl.when(j == 0)
            def _():
                pl.semaphore_wait(free_sem, peer_count)

            sum_steps((FEED_PUMP * j + 7) // 8, (FEED_PUMP * (j + 1) + 7) // 8)

        weight_grads(0, 8, after)
        greet(final_sem)
        pl.semaphore_wait(final_sem, peer_count)

    def send_small():
        return remote(S.at[1 - p], SP, send_s, recv_s, partner)

    def send_dkeys(q, group):
        slot = lax.rem(q, 2)
        theirs = pl.ds(pl.multiple_of((1 - p) * 2 * half, 128), 2 * half)
        return remote(
            DKV.at[theirs, LAST[group]], DKVR.at[slot, :, LAST[group]],
            send_dkv.at[group], recv_dkv.at[slot, group], partner,
        )

    def backward(q, carry):
        length = lens[q]

        @pl.when(last)
        def _():
            copy_cot(q).wait()

        @pl.when(first)
        def _():
            hand_back(q).wait_recv()

        norm_backward(1, GIN, 11, q)

        for b in range(4):
            dh = mm(A[11, rows(q), :], BIG[pl.ds((DOWN_AT + b) * D, D), :], NT)
            A[7 + b, rows(q), :] = (dh * A[7 + b, rows(q), :].astype(F32)).astype(BF)

        for n in range(D // 256):
            c = slice(n * 256, (n + 1) * 256)
            acc = RES[:, c]
            for b in range(4):
                acc += mm(A[7 + b, rows(q), :], BIG[pl.ds((FEED_AT + b) * D + c.start, c.stop - c.start), :], NT)
            GIN[q, :, c] = acc.astype(BF)
        put_start(GIN.at[q], ing_ref, q, 1, sem_i, recv_i)

        @pl.when(q > 0)
        def _():
            for group in range(2):
                send_dkeys(q - 1, group).wait_send()

        @pl.when((q == nq - 1) & first)
        def _():
            feed_grads()

        norm_backward(0, GIN, 15, q)

        @pl.when(q == nq - 1)
        def _():
            send_small().start()
        A[13, rows(q), :] = mm(A[15, rows(q), :], AW[3], NT).astype(BF)

        valid = key_at < length
        pump(q, FEED_PUMP + 0 * PUMP, FEED_PUMP + 1 * PUMP)

        for hp in range(pairs):
            if LAST[1].start == hp * 128:
                send_dkeys(q, 0).start()
                pump(q, FEED_PUMP + 1 * PUMP, FEED_PUMP + 2 * PUMP)
            cols = slice(hp * 128, (hp + 1) * 128)
            kp = KV[q, 0, :, cols]
            qs = stack_heads(A[12, rows(q), cols])
            dcs = stack_heads(A[13, rows(q), cols])
            st = jnp.where(valid, mm(qs, kp, NT), MASK_FILL)
            lse = jnp.concatenate(
                [LSE[q, :, 2 * hp : 2 * hp + 1], LSE[q, :, 2 * hp + 1 : 2 * hp + 2]], axis=0
            )
            prob = jnp.exp(st - lse)
            dprob = mm(dcs, KV[q, 1, :, cols], NT)
            mean = jnp.sum(prob * dprob, axis=1, keepdims=True)
            ds = (prob * (dprob - mean)).astype(BF)
            A[12, rows(q), cols] = (join_heads(mm(ds, kp)) * HEAD ** (-0.5)).astype(BF)
            dk = jnp.transpose(mm(jnp.transpose(qs), ds)).astype(BF)
            dv = jnp.transpose(mm(jnp.transpose(dcs), prob.astype(BF))).astype(BF)
            DKV[0:half, cols] = dk[:half]
            DKV[half : 2 * half, cols] = dv[:half]
            DKV[2 * half : 3 * half, cols] = dk[half:]
            DKV[3 * half : 4 * half, cols] = dv[half:]

        send_dkeys(q, 1).start()
        pump(q, FEED_PUMP + 2 * PUMP, FEED_PUMP + 3 * PUMP)
        for n in range(D // 256):
            c = slice(n * 256, (n + 1) * 256)
            RES[:, c] = RES[:, c] + mm(A[12, rows(q), :], AW[0, c, :], NT)
        pump(q, FEED_PUMP + 3 * PUMP, FEED_PUMP + 4 * PUMP)
        for group in range(2):
            send_dkeys(q, group).wait_recv()
        slot = lax.rem(q, 2)
        for i in range(2):
            mine = DKV[pl.ds(pl.multiple_of((2 * p + i) * half, half), half), :]
            A[13 + i, rows(q), :] = (mine.astype(F32) + DKVR[slot, i * half : (i + 1) * half].astype(F32)).astype(BF)

        @pl.when(first)
        def _():
            hand_on(q).wait_send()

        put_wait(GOUT.at[q], out_ref, q, 1, sem_o, recv_o)
        put_wait(GIN.at[q], ing_ref, q, 1, sem_i, recv_i)
        for n in range(D // 256):
            c = slice(n * 256, (n + 1) * 256)
            acc = RES[:, c]
            for b in range(1, 3):
                acc += mm(A[12 + b, rows(q), :], AW[b, c, :], NT)
            GOUT[q, :, c] = acc.astype(BF)

        @pl.when(last)
        def _():
            hand_back(q).start()

        put_start(GOUT.at[q], ing_ref, q, 0, sem_i, recv_i)
        pump(q, FEED_PUMP + 4 * PUMP, FEED_PUMP + 5 * PUMP)
        return carry

    lax.fori_loop(0, nq, backward, 0)

    for group in range(2):
        send_dkeys(nq - 1, group).wait_send()

    @pl.when(last)
    def _():
        feed_grads()

    before = FEED_PUMP + jnp.where(first, 5 * PUMP, 0)
    weight_grads(8, 12, lambda j: sum_steps(before + (j - 8) * PUMP, before + (j - 7) * PUMP))

    @pl.when(first)
    def _():
        lend().start()

    send_small().wait_recv()
    SR[3] = S[p] + SP[...]
    _, kids, root, parent, slot, _, away = roles(jnp.int32(0))

    def small_down():
        for n in range(3):
            @pl.when(kids[n])
            def _():
                remote(SR.at[4], SR.at[4], t_down.at[n], q_fin, peers[n]).start()

    def small_up():
        for n in range(3):
            @pl.when(kids[n])
            def _():
                remote(SR.at[3], SR.at[n], t_up, q_up.at[n], peers[n]).wait_recv()
                SR[3] = SR[3] + SR[n]

        @pl.when(root)
        def _():
            SR[4] = SR[3]
            small_down()

        @pl.when(jnp.logical_not(root))
        def _():
            remote(SR.at[3], SR.at[slot], t_up, q_up.at[slot], parent).start()

    small_at = steps - HOP * deep

    def tail(t, c):
        @pl.when(last & (t == GUEST * per))
        def _():
            lend().wait_recv()

        sum_step(t)

        @pl.when(t == small_at + HOP * (deep - away))
        def _():
            small_up()

        @pl.when((t == small_at + HOP * (deep + away)) & jnp.logical_not(root))
        def _():
            remote(SR.at[3], SR.at[4], t_up, q_fin, parent).wait_recv()
            small_down()

        return c

    lax.fori_loop(before + 4 * PUMP, steps + 2 * HOP * deep, tail, 0)
    small_out[...] = SR[4]

    @pl.when(first)
    def _():
        give_back().wait_recv()
        store(jnp.int32(11), False)

    whole_first = G.at[pl.ds(0, 11), pl.ds(0, per * CLASS_ROWS)]
    whole_last = G.at[pl.ds(0, 13), pl.ds(0, per * CLASS_ROWS)]
    for kind in range(CLASSES):
        _, kids_of, root_of, parent_of, _, _, _ = roles(jnp.int32(kind))

        for here, whole in ((first, whole_first), (last, whole_last)):
            @pl.when(here & jnp.logical_not(root_of))
            def _():
                remote(whole, whole, s_up.at[kind], r_fin.at[kind, 0], parent_of).wait_send()

            for n in range(3):
                @pl.when(here & kids_of[n])
                def _():
                    remote(whole, whole, s_down.at[kind, n], r_fin.at[kind, 0], peers[n]).wait_send()

    @pl.when(jnp.logical_not(root))
    def _():
        remote(SR.at[3], SR.at[slot], t_up, q_up.at[slot], parent).wait_send()

    for n in range(3):
        @pl.when(kids[n])
        def _():
            remote(SR.at[4], SR.at[4], t_down.at[n], q_fin, peers[n]).wait_send()

    send_small().wait_send()

    @pl.when(first)
    def _():
        lend().wait_send()

    @pl.when(last)
    def _():
        give_back().wait_send()


    for o in range(12):
        store(jnp.int32(o), True)
    send_vec().wait_send()
    for b in range(4):
        on_core(1, lambda: send_weights(1, b).wait_send())
    for b in W_ORDER[2:]:
        on_core(0, lambda: send_weights(0, b).wait_send())
    for b in range(2):
        send_weights2(b).wait_send()
    for q in range(nq):
        for i in range(2):
            for group in range(2):
                send_keys(q, i, group).wait_send()

        @pl.when(last)
        def _():
            hand_back(q).wait_send()

        put_wait(A.at[2, rows(q)], out_ref, q, 0, sem_o, recv_o)
        put_wait(GOUT.at[q], ing_ref, q, 0, sem_i, recv_i)


def run_layers(tokens, cotangent, lengths, weights, w_down, *rows):
    nq, seq_len, D = tokens.shape
    half = seq_len // 2
    tall = nq * half
    dma = pltpu.SemaphoreType.DMA
    any_spec = pl.BlockSpec(memory_space=pl.ANY)
    vmem_spec = pl.BlockSpec(memory_space=pltpu.VMEM)
    line = lax.axis_size("dp") // 2
    steps = 13 * (D // 2) // STEP_ROWS
    return pl.pallas_call(
        partial(layer_kernel, line),
        name="layers",
        out_shape=(
            jax.ShapeDtypeStruct((nq, seq_len, D), BF),
            jax.ShapeDtypeStruct((nq, seq_len, D), BF),
            jax.ShapeDtypeStruct((D, 4 * D), BF),
            jax.ShapeDtypeStruct((2 * D, D), BF),
            jax.ShapeDtypeStruct((8, D), F32),
        ),
        in_specs=[any_spec, any_spec, pl.BlockSpec(memory_space=pltpu.SMEM), any_spec, any_spec] + [vmem_spec] * 3,
        out_specs=(any_spec, any_spec, any_spec, any_spec, vmem_spec),
        scratch_shapes=[
            pltpu.VMEM((max(8 * D, steps * UNITS * CLASS_ROWS), D), BF),
            pltpu.VMEM((4, D, D), BF),
            pltpu.VMEM((2, 8, D), F32),
            pltpu.VMEM((16, tall, D), BF),
            pltpu.VMEM((nq, 2, seq_len, D), BF),
            pltpu.VMEM((2, tall, D), BF),
            pltpu.VMEM((nq, half, 128), F32),
            pltpu.VMEM((nq, half, D), BF),
            pltpu.VMEM((nq, half, D), BF),
            pltpu.VMEM((half, D), F32),
            pltpu.VMEM((4 * half, D), BF),
            pltpu.VMEM((2, 2 * half, D), BF),
            pltpu.VMEM((13, D // 2, D), BF),
            pltpu.VMEM((2, D // 2, D), BF),
            pltpu.VMEM((2, 8, D), F32),
            pltpu.VMEM((8, D), F32),
            pltpu.VMEM((5, 8, D), F32),
            dma((6,)), dma((nq,)), dma((nq,)), dma((6,)), dma((6,)),
            dma((nq, 2, 2)), dma((nq, 2, 2)), dma((nq,)), dma((nq,)), dma((2, nq)), dma((nq,)),
            dma((2,)), dma((2, 2)), dma((nq,)), dma((nq,)), dma((2, nq)), dma((nq,)),
            dma((2,)), dma((2,)), dma((12,)), dma((12,)), dma, dma,
            dma, dma, dma((CLASSES,)), dma((CLASSES, 3)), dma((CLASSES, 3, steps)), dma((CLASSES, steps)),
            dma, dma((3,)), dma((3,)), dma, pltpu.SemaphoreType.REGULAR, pltpu.SemaphoreType.REGULAR,
            dma, dma, dma, dma,
        ],
        compiler_params=pltpu.CompilerParams(
            collective_id=0, has_side_effects=True, vmem_limit_bytes=64 * MIB
        ),
        cost_estimate=pl.CostEstimate(flops=60 * 10**9, bytes_accessed=40 * 10**6, transcendentals=10**7),
    )(tokens, cotangent, lengths, weights, w_down, *rows)


def result_kernel(out_in, grad_in, main_in, half_in, small_in, out, grad, main, down, bias, gain, shift):
    out[...] = out_in[...]
    grad[...] = grad_in[...]
    main[...] = main_in[...].astype(F32)
    down[...] = half_in[...].astype(F32)
    bias[...] = small_in[0:1, :]
    gain[...] = small_in[1:2, :]
    shift[...] = small_in[2:3, :]


RESULT_STEPS = 8


def results(*arrays):
    types = (BF, BF, F32, F32)

    def rows_of(a):
        return pl.BlockSpec((a.shape[0] // RESULT_STEPS, a.shape[1]), lambda i: (i, 0))

    def whole(a, rows):
        return pl.BlockSpec((rows, a.shape[1]), lambda i: (0, 0))

    small = arrays[4]
    return pl.pallas_call(
        result_kernel,
        name="results",
        grid=(RESULT_STEPS,),
        out_shape=tuple(jax.ShapeDtypeStruct(a.shape, t) for a, t in zip(arrays[:4], types))
        + tuple(jax.ShapeDtypeStruct((1, small.shape[1]), F32) for _ in range(3)),
        in_specs=[rows_of(a) for a in arrays[:4]] + [whole(small, 8)],
        out_specs=tuple(rows_of(a) for a in arrays[:4]) + tuple(whole(small, 1) for _ in range(3)),
        compiler_params=pltpu.CompilerParams(vmem_limit_bytes=63 * MIB),
    )(*arrays)


def on_device(tokens, lengths, w_main, w_down_half, out_bias, ln_gain, ln_bias, cotangent):
    nq, seq_len, D = tokens.shape
    kept_out, kept_grad, grad_main, grad_half, small = run_layers(
        tokens, cotangent, lengths, w_main[0], w_down_half[0], out_bias, ln_gain, ln_bias
    )
    tall = nq * seq_len
    kept_out, kept_grad, grad_main, grad_half, bias, gain, shift = results(
        kept_out.reshape(tall, D), kept_grad.reshape(tall, D), grad_main, grad_half, small
    )
    return (
        kept_out.reshape(1, nq, seq_len, D),
        kept_grad.reshape(1, nq, seq_len, D),
        grad_main[None],
        grad_half[None],
        bias,
        gain,
        shift,
    )


def solution(mesh):
    in_specs = (
        P("dp", None, None),
        P("dp"),
        P("section", None, None),
        P("section", None, None),
        P("section", None),
        P("section", None),
        P("section", None),
        P("dp", None, None),
    )
    out_specs = (
        P("section", "dp", None, None),
        P("section", "dp", None, None),
        P("section", None, None),
        P("section", None, None),
        P("section", None),
        P("section", None),
        P("section", None),
    )
    return jax.shard_map(
        on_device, mesh=mesh, in_specs=in_specs, out_specs=out_specs, check_vma=False
    )
```
